32 devices in a mesh: seq: 8 (over z, x), rows: 4 (over y, core).
Axes of the slice: x: 2, y: 2, z: 4, core: 2. Of those that a mesh axis runs over, the one named last changes fastest.
Arguments:
- activations: float32 [8, 2048, 512], P('rows', 'seq'), may hold values from -6 to 6
- cotangent: float32 [8, 2048, 512], P('rows', 'seq')
- seq_starts: int32 [8, 3], P('rows'), may hold values from 0 to 2048, as said below
- attn_weight: float32 [4, 512, 512], P(None, 'rows')
- up_weight: float32 [512, 2048], P('rows'), may hold values from -0.25 to 0.25
- down_weight: float32 [2048, 512], P('rows'), may hold values from -0.125 to 0.125
- vectors: float32 [9, 512], replicated
- attn_m: float32 [4, 512, 512], P(None, 'rows'), may hold values from -0.0022552744 to 0.0022552744
- up_m: float32 [512, 2048], P('rows'), may hold values from -0.0022552744 to 0.0022552744
- down_m: float32 [2048, 512], P('rows'), may hold values from -0.0022552744 to 0.0022552744
- vec_m: float32 [9, 512], replicated, may hold values from -0.004510549 to 0.004510549
- attn_v: float32 [4, 512, 512], P(None, 'rows'), may hold values from 3.1789145e-07 to 1.2715658e-06
- up_v: float32 [512, 2048], P('rows'), may hold values from 3.1789145e-07 to 1.2715658e-06
- down_v: float32 [2048, 512], P('rows'), may hold values from 3.1789145e-07 to 1.2715658e-06
- vec_v: float32 [9, 512], replicated, may hold values from 1.2715658e-06 to 5.086263e-06
Outputs:
- out_act: float32 [8, 2048, 512], P('rows', 'seq')
- in_grad: float32 [8, 2048, 512], P('rows', 'seq')
- grad_norm: float32 [], replicated
- attn_grad: float32 [4, 512, 512], P(None, 'rows')
- up_grad: float32 [512, 2048], P('rows')
- down_grad: float32 [2048, 512], P('rows')
- vec_grad: float32 [9, 512], replicated
- attn_new: float32 [4, 512, 512], P(None, 'rows')
- up_new: float32 [512, 2048], P('rows')
- down_new: float32 [2048, 512], P('rows')
- vec_new: float32 [9, 512], replicated
- attn_m_new: float32 [4, 512, 512], P(None, 'rows')
- up_m_new: float32 [512, 2048], P('rows')
- down_m_new: float32 [2048, 512], P('rows')
- vec_m_new: float32 [9, 512], replicated
- attn_v_new: float32 [4, 512, 512], P(None, 'rows')
- up_v_new: float32 [512, 2048], P('rows')
- down_v_new: float32 [2048, 512], P('rows')
- vec_v_new: float32 [9, 512], replicated
The draws below stay inside these ranges and needn't reach their ends.
Inputs may be any that keep to these rules, and one draw needn't show every extreme that they name: `seq_starts`: in each row the entries rise from 0; an entry equal to 2048 marks an unused slot and all after it are unused. Of the 2 rows that share one index of rows, at least one holds a single sequence over the whole row.
All inputs are finite; a program needn't handle non-finite values.
Results may differ from the reference program's by a relative error of at most 0.0003.
Values sent between devices are 32-bit elements; how exact they have to be, the bound alone decides.
No kernel may reach another device: no remote copies, remote signals or barrier semaphores. Data moves between devices by JAX's collectives and lax.ppermute only.
A program may use at most 192 MiB of HBM per device.

```python
import math
import jax
import jax.numpy as jnp
from jax import lax

MODEL_WIDTH = 512
HEADS = 8
HEAD_DIM = 64
FF = 2048
ROWS_DEV = 2
SEG = 1024
STEP = 5
PACKED_ROWS = 8
ROW_POSITIONS = 2048
NSTART = 3
VROWS = 9


def draw_cotangent(key, part):
    key = jax.random.fold_in(key, 11)
    token_position = jnp.arange(ROW_POSITIONS, dtype=jnp.float32)[None, :, None] / ROW_POSITIONS
    drawn_variant = jax.random.normal(key, (PACKED_ROWS, ROW_POSITIONS, MODEL_WIDTH), jnp.float32)
    rising = 1.0 + 2.0 * token_position
    return drawn_variant * rising


def draw_seq_starts(key, part):
    key = jax.random.fold_in(key, 12)
    key_one, key_two = jax.random.split(key)
    offsets = jax.random.randint(key_one, (PACKED_ROWS, NSTART), 1, SEG // 2 + 1)
    slot_numbers = jnp.arange(NSTART, dtype=jnp.int32)
    packed = jnp.where(slot_numbers[None, :] == 0, 0, slot_numbers[None, :] * SEG - offsets)
    chosen = jax.random.randint(key_two, (PACKED_ROWS // ROWS_DEV,), 0, ROWS_DEV)
    whole_row = jnp.arange(PACKED_ROWS, dtype=jnp.int32) % ROWS_DEV == jnp.repeat(chosen, ROWS_DEV)
    single_device = jnp.where(slot_numbers == 0, 0, ROW_POSITIONS)
    return jnp.where(whole_row[:, None], single_device[None, :], packed).astype(jnp.int32)


def draw_attn_weight(key, part):
    key = jax.random.fold_in(key, 13)
    drawn_variant = jax.random.normal(key, (4, MODEL_WIDTH, MODEL_WIDTH), jnp.float32) * MODEL_WIDTH ** (-0.5)
    factor = jnp.array([1.0, 1.0, 1.0, 0.5 * SEG ** 0.5], jnp.float32)
    return drawn_variant * factor[:, None, None]


def draw_vectors(key, part):
    key = jax.random.fold_in(key, 14)
    key_one, key_two = jax.random.split(key)
    across = jnp.arange(MODEL_WIDTH, dtype=jnp.float32) / MODEL_WIDTH
    jitter = jax.random.uniform(key_one, (2, MODEL_WIDTH), jnp.float32, 0.8, 1.2)
    gain_rows = (0.5 + across)[None, :] * jitter
    shift_rows = jax.random.normal(key_two, (VROWS - 2, MODEL_WIDTH), jnp.float32) * 0.3
    return jnp.concatenate([gain_rows[:1], shift_rows[:1], gain_rows[1:], shift_rows[1:]], axis=0)


def levels(own_key, dims, cuts, smallest, largest):
    level = 1.0
    for dim, parts in cuts:
        steps = jax.random.uniform(jax.random.fold_in(jax.random.fold_in(own_key, 6), dim), (parts,), jnp.float32, smallest / len(cuts), largest / len(cuts))
        level = level * jnp.repeat(jnp.exp(steps), dims[dim] // parts).reshape((-1,) + (1,) * (len(dims) - 1 - dim))
    return level


def bell_draw(own_key, dims, deviation, most, shards=(), held_as=jnp.bfloat16):
    gain = levels(own_key, dims, shards, -0.22, 0.18) if shards else 1.0
    values = jax.random.normal(own_key, dims, jnp.float32) * deviation * gain
    return jnp.minimum(jnp.maximum(values, -most), most).astype(held_as)


def setup_inputs(seed: int = 0) -> dict:
    arg_keys = jax.random.split(jax.random.key(seed), 16)
    activations = bell_draw(arg_keys[0], (PACKED_ROWS, ROW_POSITIONS, MODEL_WIDTH), 1.0, 6.0, ((0, 4), (1, 8)), jnp.float32)
    cotangent = draw_cotangent(jax.random.fold_in(arg_keys[15], 71), 0)
    seq_starts = draw_seq_starts(jax.random.fold_in(arg_keys[15], 71), 0)
    attn_weight = draw_attn_weight(jax.random.fold_in(arg_keys[15], 71), 0)
    up_weight = bell_draw(arg_keys[4], (MODEL_WIDTH, FF), MODEL_WIDTH ** -0.5, 0.25, ((0, 4),), jnp.float32)
    down_weight = bell_draw(arg_keys[5], (FF, MODEL_WIDTH), FF ** -0.5, 0.125, ((0, 4),), jnp.float32)
    vectors = draw_vectors(jax.random.fold_in(arg_keys[15], 71), 0)
    attn_m = bell_draw(arg_keys[7], (4, MODEL_WIDTH, MODEL_WIDTH), ((4*MODEL_WIDTH*MODEL_WIDTH + 2*MODEL_WIDTH*FF) ** -0.5), 0.0022552744, ((1, 4),), jnp.float32)
    up_m = bell_draw(arg_keys[8], (MODEL_WIDTH, FF), ((4*MODEL_WIDTH*MODEL_WIDTH + 2*MODEL_WIDTH*FF) ** -0.5), 0.0022552744, ((0, 4),), jnp.float32)
    down_m = bell_draw(arg_keys[9], (FF, MODEL_WIDTH), ((4*MODEL_WIDTH*MODEL_WIDTH + 2*MODEL_WIDTH*FF) ** -0.5), 0.0022552744, ((0, 4),), jnp.float32)
    vec_m = bell_draw(arg_keys[10], (VROWS, MODEL_WIDTH), (2.0 * (4*MODEL_WIDTH*MODEL_WIDTH + 2*MODEL_WIDTH*FF) ** -0.5), 0.004510549, (), jnp.float32)
    attn_v = jnp.clip(jnp.exp(math.log(1.271565793103946e-06) - 1.3862944 * jax.random.uniform(arg_keys[11], (4, MODEL_WIDTH, MODEL_WIDTH), jnp.float32) ** levels(arg_keys[11], (4, MODEL_WIDTH, MODEL_WIDTH), ((1, 4),), -0.2, 0.2)), 3.178914482759865e-07, 1.271565793103946e-06)
    up_v = jnp.clip(jnp.exp(math.log(1.271565793103946e-06) - 1.3862944 * jax.random.uniform(arg_keys[12], (MODEL_WIDTH, FF), jnp.float32) ** levels(arg_keys[12], (MODEL_WIDTH, FF), ((0, 4),), -0.2, 0.2)), 3.178914482759865e-07, 1.271565793103946e-06)
    down_v = jnp.clip(jnp.exp(math.log(1.271565793103946e-06) - 1.3862944 * jax.random.uniform(arg_keys[13], (FF, MODEL_WIDTH), jnp.float32) ** levels(arg_keys[13], (FF, MODEL_WIDTH), ((0, 4),), -0.2, 0.2)), 3.178914482759865e-07, 1.271565793103946e-06)
    vec_v = jnp.clip(jnp.exp(jax.random.uniform(arg_keys[14], (VROWS, MODEL_WIDTH), jnp.float32, math.log(1.271565793103946e-06), math.log(5.086263172415784e-06))), 1.271565793103946e-06, 5.086263172415784e-06)
    return dict(activations=activations, cotangent=cotangent, seq_starts=seq_starts, attn_weight=attn_weight, up_weight=up_weight, down_weight=down_weight, vectors=vectors, attn_m=attn_m, up_m=up_m, down_m=down_m, vec_m=vec_m, attn_v=attn_v, up_v=up_v, down_v=down_v, vec_v=vec_v)


EPS_NORM = 1e-05
EPS_DEN = 1e-06
CLIP_AT = 1.0
BETA_ONE = 0.5
BETA_TWO = 0.5
RATE_MAT = 0.02
RATE_VEC = 0.1
DECAY_MAT = 0.1
EPS_ADAM = 1e-08
PRECISE = lax.Precision.HIGHEST

@jax.custom_vjp
def low(v):
    return lax.optimization_barrier(v.astype(jnp.bfloat16)).astype(jnp.float32)

@jax.custom_vjp
def low_back(v):
    return v

def low_keep(v):
    return (low(v), None)

def low_pass(kept, grad):
    return (grad,)

def back_keep(v):
    return (v, None)

def back_low(kept, grad):
    return (low(grad),)
low.defvjp(low_keep, low_pass)
low_back.defvjp(back_keep, back_low)

def feature(value):
    return jax.nn.elu(value) + 1.0

def layer_norm(inputs, scale_gain, offset):
    average = lax.optimization_barrier(jnp.mean(inputs, axis=-1, keepdims=True))
    centred = inputs - average
    spread = lax.optimization_barrier(jnp.mean(centred * centred, axis=-1, keepdims=True))
    return centred * lax.rsqrt(spread + EPS_NORM) * scale_gain + offset

def attend_block(carried, pieces):
    state, key_sum, last_doc = carried
    feat_q, feat_k, values_v, doc_ids = pieces
    span_len = doc_ids.shape[0]
    order = jnp.arange(span_len, dtype=jnp.int32)
    doc_mask = ((doc_ids[:, None] == doc_ids[None, :]) & (order[:, None] >= order[None, :])).astype(jnp.float32)
    scores = jnp.einsum('the,she->hts', feat_q, feat_k, precision=PRECISE) * doc_mask[None]
    numer = jnp.einsum('hts,she->the', scores, values_v, precision=PRECISE)
    denom = jnp.transpose(lax.optimization_barrier(jnp.sum(scores, axis=2)))
    use_state = (doc_ids == last_doc).astype(jnp.float32)
    numer = numer + use_state[:, None, None] * jnp.einsum('the,hef->thf', feat_q, state, precision=PRECISE)
    denom = denom + use_state[:, None] * jnp.einsum('the,he->th', feat_q, key_sum, precision=PRECISE)
    attended = numer / (denom[:, :, None] + EPS_DEN)
    end_doc = doc_ids[-1]
    kept_last = (doc_ids == end_doc).astype(jnp.float32)[:, None, None]
    continued = (end_doc == last_doc).astype(jnp.float32)
    state = continued * state + jnp.einsum('she,shf->hef', feat_k * kept_last, values_v, precision=PRECISE)
    key_sum = continued * key_sum + lax.optimization_barrier(jnp.sum(feat_k * kept_last, axis=0))
    return ((state, key_sum, end_doc), attended)

def row_forward(inputs, doc_ids, attention, up_matrix, down_matrix, vector_set):
    length = inputs.shape[0]
    normed = layer_norm(inputs, vector_set[0], vector_set[1])

    def head_split(matrix):
        return jnp.dot(normed, matrix, precision=PRECISE).reshape(length, HEADS, HEAD_DIM)
    feat_q = feature(head_split(attention[0]))
    feat_k = feature(head_split(attention[1]))
    values_v = head_split(attention[2])
    span_len = min(512, length)
    span_count = length // span_len

    def shaped(array):
        return array.reshape((span_count, span_len) + array.shape[1:])
    start = (jnp.zeros((HEADS, HEAD_DIM, HEAD_DIM), jnp.float32), jnp.zeros((HEADS, HEAD_DIM), jnp.float32), jnp.zeros((), jnp.int32))
    _, attended = lax.scan(jax.checkpoint(attend_block), start, (shaped(feat_q), shaped(feat_k), shaped(values_v), shaped(doc_ids)))
    attended = attended.reshape(length, HEADS * HEAD_DIM)
    resid = inputs + jnp.dot(attended, attention[3], precision=PRECISE)
    second = layer_norm(resid, vector_set[2], vector_set[3])
    upped = jnp.dot(second, up_matrix, precision=PRECISE) + vector_set[5:].reshape(FF)
    return resid + jnp.dot(jax.nn.gelu(upped, approximate=False), down_matrix, precision=PRECISE) + vector_set[4]

def adamw_step(weight, gradient, first_m, second_m, factor, rate, decay):
    clipped = gradient * factor
    new_m = BETA_ONE * first_m + (1.0 - BETA_ONE) * clipped
    new_v = BETA_TWO * second_m + (1.0 - BETA_TWO) * clipped * clipped
    moved = new_m / (1.0 - BETA_ONE ** STEP) / (jnp.sqrt(new_v / (1.0 - BETA_TWO ** STEP)) + EPS_ADAM)
    return (clipped, weight - rate * (moved + decay * weight), new_m, new_v)

def reference(activations, cotangent, seq_starts, attn_weight, up_weight, down_weight, vectors, attn_m, up_m, down_m, vec_m, attn_v, up_v, down_v, vec_v):
    token_positions = jnp.arange(ROW_POSITIONS, dtype=jnp.int32)
    doc_ids = lax.optimization_barrier(jnp.sum((seq_starts[:, None, :] <= token_positions[None, :, None]).astype(jnp.int32), axis=2)).astype(jnp.int32)

    def whole_layer(inputs, attention, up_matrix, down_matrix, vector_set):

        def row_fn(pair):
            return row_forward(pair[0], pair[1], attention, up_matrix, down_matrix, vector_set)
        return lax.map(jax.checkpoint(row_fn), (inputs, doc_ids))
    out_act, back_fn = jax.vjp(whole_layer, activations, attn_weight, up_weight, down_weight, vectors)
    in_grad, grad_attn, grad_up, grad_down, grad_vec = back_fn(cotangent)
    square = jnp.sum(grad_attn * grad_attn) + jnp.sum(grad_up * grad_up) + jnp.sum(grad_down * grad_down) + jnp.sum(grad_vec * grad_vec)
    grad_norm = jnp.sqrt(square)
    factor = jnp.minimum(1.0, CLIP_AT / (grad_norm + 1e-06))
    attn_g, attn_new, attn_m_new, attn_v_new = adamw_step(attn_weight, grad_attn, attn_m, attn_v, factor, RATE_MAT, DECAY_MAT)
    up_g, up_new, up_m_new, up_v_new = adamw_step(up_weight, grad_up, up_m, up_v, factor, RATE_MAT, DECAY_MAT)
    down_g, down_new, down_m_new, down_v_new = adamw_step(down_weight, grad_down, down_m, down_v, factor, RATE_MAT, DECAY_MAT)
    vec_g, vec_new, vec_m_new, vec_v_new = adamw_step(vectors, grad_vec, vec_m, vec_v, factor, RATE_VEC, 0.0)
    return (out_act, in_grad, grad_norm, attn_g, up_g, down_g, vec_g, attn_new, up_new, down_new, vec_new, attn_m_new, up_m_new, down_m_new, vec_m_new, attn_v_new, up_v_new, down_v_new, vec_v_new)
```

```python
import functools
import math

import jax
import jax.numpy as jnp
from jax import lax
from jax.experimental import pallas as pl
from jax.experimental.pallas import tpu as pltpu
from jax.sharding import PartitionSpec as P

HEADS = 8
HEAD_DIM = 64
PAIRS = HEADS // 2
LANES = 2 * HEAD_DIM
STEP = 5

EPS_NORM = 1e-05
EPS_DEN = 1e-06
CLIP_AT = 1.0
BETA_ONE = 0.5
BETA_TWO = 0.5
RATE_MAT = 0.02
RATE_VEC = 0.1
DECAY_MAT = 0.1
EPS_ADAM = 1e-08

F32 = jnp.float32
BF16 = jnp.bfloat16
VMEM = pl.BlockSpec(memory_space=pltpu.VMEM)
SMEM = pl.BlockSpec(memory_space=pltpu.SMEM)
LIMIT = 56 * 1024 * 1024


def split(a):
    high = a.astype(BF16)
    return high, (a - high.astype(F32)).astype(BF16)


def dot3(a, b, ca=1, cb=0):
    dims = (((ca,), (cb,)), ((), ()))

    def one(p, q):
        return lax.dot_general(p, q, dims, preferred_element_type=F32)

    return one(a[0], b[0]) + (one(a[0], b[1]) + one(a[1], b[0]))


def dot2(a, b):
    dims = (((1,), (0,)), ((), ()))
    return sum(lax.dot_general(p, b, dims, preferred_element_type=F32) for p in a)


def phi(u):
    return jnp.where(u > 0, u + 1.0, jnp.exp(jnp.minimum(u, 0.0)))


def normalise(x):
    centred = x - jnp.mean(x, axis=1, keepdims=True)
    scale = lax.rsqrt(jnp.mean(centred * centred, axis=1, keepdims=True) + EPS_NORM)
    return centred * scale, scale


def normalise_back(grad, unit, scale):
    inner = jnp.mean(grad * unit, axis=1, keepdims=True)
    return scale * (grad - jnp.mean(grad, axis=1, keepdims=True) - unit * inner)


def first_head(shape):
    return lax.broadcasted_iota(jnp.int32, shape, len(shape) - 1) % LANES < HEAD_DIM


def pick(value, head):
    return jnp.where(first_head(value.shape) == (head == 0), value, 0.0)


def block_ones():
    shape = (LANES, LANES)
    rows, lanes = (lax.broadcasted_iota(jnp.int32, shape, d) // HEAD_DIM for d in (0, 1))
    return jnp.where(rows == lanes, 1.0, 0.0).astype(BF16)


class Info:
    def __init__(self, ref, length, slots):
        self.ref, self.length, self.slots = ref, length, slots
        self.me, self.place, self.first = ref[0], ref[1], ref[2]

    def starts(self, r):
        return [self.ref[3 + r * self.slots + i] for i in range(self.slots)]

    def causal(self, r, flipped=False):
        shape = (self.length, self.length)
        t = self.first + lax.broadcasted_iota(jnp.int32, shape, 1 if flipped else 0)
        s = self.first + lax.broadcasted_iota(jnp.int32, shape, 0 if flipped else 1)
        ok = t >= s
        for a in self.starts(r):
            ok = ok & ((t < a) | (s >= a))
        return jnp.where(ok, 1.0, 0.0)

    def from_before(self, r, width):
        t = self.first + lax.broadcasted_iota(jnp.int32, (self.length, width), 0)
        ok = t >= 0
        for a in self.starts(r):
            ok = ok & ((a < self.first) | (t < a))
        return jnp.where(ok, 1.0, 0.0)

    def to_after(self, r, width):
        s = self.first + lax.broadcasted_iota(jnp.int32, (self.length, width), 0)
        last = self.first + self.length - 1
        ok = s >= 0
        for a in self.starts(r):
            ok = ok & ((s >= a) | (a > last))
        return jnp.where(ok, 1.0, 0.0)


def assemble(me, pieces, high, low):
    for j, piece in enumerate(pieces):
        rows = piece.shape[-2]
        at = pl.ds(pl.multiple_of((me ^ j) * rows, rows), rows)
        for lead in range(piece.shape[0]):
            h, l = split(piece[lead])
            high[lead, at, :] = h
            low[lead, at, :] = l


def state_blocks(ref, r, p):
    at = (r * PAIRS + p) * HEAD_DIM
    packed = ref[at : at + HEAD_DIM, :]
    sums = ref.shape[0] // (HEAD_DIM + 1) * HEAD_DIM + r * PAIRS + p
    return (
        jnp.concatenate([pick(packed, 0), pick(packed, 1)], axis=0),
        ref[sums : sums + 1, :],
    )


def store_state(ref, r, p, full, key_sum):
    at = (r * PAIRS + p) * HEAD_DIM
    top, bottom = full[:HEAD_DIM], full[HEAD_DIM:]
    ref[at : at + HEAD_DIM, :] = jnp.where(first_head(top.shape), top, bottom)
    sums = ref.shape[0] // (HEAD_DIM + 1) * HEAD_DIM + r * PAIRS + p
    ref[sums : sums + 1, :] = key_sum


def pair_slices(length, r, p):
    return slice(r * length, (r + 1) * length), slice(p * LANES, (p + 1) * LANES)


def keys_kernel(n, slots, rows, info, x, vec, *refs):
    pieces, (nh, nl, k, v, state, wh, wl) = refs[:n], refs[n:]
    length = x.shape[0] // rows
    info = Info(info, length, slots)
    assemble(info.me, pieces, wh, wl)
    unit, _ = normalise(x[...])
    normed = split(unit * vec[0:1, :] + vec[1:2, :])
    nh[...], nl[...] = normed
    k[...] = phi(dot3(normed, (wh[0], wl[0])))
    v[...] = dot3(normed, (wh[1], wl[1]))
    for r in range(rows):
        kept = info.to_after(r, LANES)
        for p in range(PAIRS):
            at = pair_slices(length, r, p)
            masked = k[at] * kept
            full = dot3(split(masked), split(v[at]), 0, 0)
            store_state(state, r, p, full, jnp.sum(masked, axis=0, keepdims=True))


def queries_kernel(n, slots, rows, info, nh, nl, k, v, *refs):
    pieces, (q, numer, denom, wh, wl) = refs[:n], refs[n:]
    length = k.shape[0] // rows
    info = Info(info, length, slots)
    assemble(info.me, pieces, wh, wl)
    q[...] = phi(dot3((nh[...], nl[...]), (wh[0], wl[0])))
    for r in range(rows):
        mask = info.causal(r)
        for p in range(PAIRS):
            at = pair_slices(length, r, p)
            q_pair, v_pair = q[at], v[at]
            keys = split(k[at])
            both = 0.0
            for head in range(2):
                scores = dot3(split(pick(q_pair, head)), keys, 1, 1) * mask
                ones = pick(jnp.ones_like(v_pair), head)
                wide = jnp.concatenate([pick(v_pair, head), ones], axis=1)
                both = both + dot3(split(scores), split(wide))
            numer[at] = both[:, :LANES]
            denom[at] = both[:, LANES:]


def attend_kernel(n, slots, rows, info, x, vec, q, numer, denom, state, *refs):
    pieces, (att, inv, resid, sh, sl, wh, wl) = refs[:n], refs[n:]
    length = x.shape[0] // rows
    info = Info(info, length, slots)
    assemble(info.me, pieces, wh, wl)
    ones = block_ones()
    for r in range(rows):
        use = info.from_before(r, LANES)
        for p in range(PAIRS):
            at = pair_slices(length, r, p)
            block, key_sum = state_blocks(state, r, p)
            q_pair = q[at] * use
            top = numer[at] + dot3(split(q_pair), split(block))
            under = denom[at] + dot2(split(q_pair * key_sum), ones) + EPS_DEN
            inverse = 1.0 / under
            inv[at] = inverse
            att[at] = top * inverse
    result = x[...] + dot3(split(att[...]), (wh[0], wl[0]))
    resid[...] = result
    unit, _ = normalise(result)
    sh[...], sl[...] = split(unit * vec[2:3, :] + vec[3:4, :])


def erf(u):
    return lax.erf(u)


def feed_kernel(vec, bias, sh, sl, dout, resid, uh, ul, dh_, dl_, out, gh, gl, eh, el, dresid, small, dbias, acc, back, oh, ol):
    step, last = pl.program_id(0), pl.num_programs(0) - 1

    @pl.when(step == 0)
    def _():
        oh[...], ol[...] = split(dout[...])

    up, down = (uh[...], ul[...]), (dh_[...], dl_[...])
    h = dot3((sh[...], sl[...]), up) + bias[...]
    cdf = 0.5 * (1.0 + erf(h * math.sqrt(0.5)))
    g = split(h * cdf)
    gh[...], gl[...] = g
    slope = cdf + h * (jnp.exp(-0.5 * h * h) * (1.0 / math.sqrt(2.0 * math.pi)))
    grad = dot3((oh[...], ol[...]), down, 1, 1) * slope
    dbias[...] = jnp.sum(grad, axis=0, keepdims=True)
    e = split(grad)
    eh[...], el[...] = e
    part = dot3(g, down)
    part_back = dot3(e, up, 1, 1)

    @pl.when(step == 0)
    def _():
        acc[...] = part
        back[...] = part_back

    @pl.when(step > 0)
    def _():
        acc[...] += part
        back[...] += part_back

    @pl.when(step == last)
    def _():
        out[...] = resid[...] + acc[...] + vec[4:5, :]
        unit, scale = normalise(resid[...])
        grad_second = back[...]
        small[...] = jnp.zeros_like(small)
        small[2:3, :] = jnp.sum(grad_second * unit, axis=0, keepdims=True)
        small[3:4, :] = jnp.sum(grad_second, axis=0, keepdims=True)
        small[4:5, :] = jnp.sum(dout[...], axis=0, keepdims=True)
        dresid[...] = dout[...] + normalise_back(grad_second * vec[2:3, :], unit, scale)


def attend_back_kernel(slots, rows, info, dresid, wh, wl, q, att, inv, dn, dd, state):
    length = q.shape[0] // rows
    info = Info(info, length, slots)
    grad = dot3(split(dresid[...]), (wh[0], wl[0]), 1, 1)
    dn[...] = grad * inv[...]
    ones = block_ones()
    for r in range(rows):
        use = info.from_before(r, LANES)
        for p in range(PAIRS):
            at = pair_slices(length, r, p)
            lanes = at[1]
            inner = dot2(split(grad[at[0], lanes] * att[at]), ones)
            under = -inner * inv[at]
            dd[at] = under
            q_pair = q[at] * use
            full = dot3(split(q_pair), split(dn[at]), 0, 0)
            store_state(state, r, p, full, jnp.sum(q_pair * under, axis=0, keepdims=True))


def down_grad_kernel(gh, gl, dout, theirs, mine, oh, ol):
    step, half = pl.program_id(0), pl.num_programs(0) // 2

    @pl.when(step == 0)
    def _():
        oh[...], ol[...] = split(dout[...])

    grad = dot3((gh[...], gl[...]), (oh[...], ol[...]), 0, 0)

    @pl.when(step < half)
    def _():
        theirs[0] = grad

    @pl.when(step >= half)
    def _():
        mine[0] = grad


def up_grad_kernel(n, info, sh, sl, eh, el, theirs, mine, full):
    me = info[0]
    full[...] = dot3((sh[...], sl[...]), (eh[...], el[...]), 0, 0)
    rows = full.shape[0] // n
    for j in range(n):
        at = pl.ds(pl.multiple_of((me ^ j) * rows, rows), rows)
        (theirs if j & 1 else mine)[j // 2, 0] = full[at, :]


def deal(me, n, full, theirs, mine, slot):
    rows = full.shape[0] // n
    for j in range(n):
        at = pl.ds(pl.multiple_of((me ^ j) * rows, rows), rows)
        (theirs if j & 1 else mine)[j // 2, slot] = full[at, :]


def local_back_kernel(n, slots, rows, info, nh, nl, q, k, v, dn, dd, state, att, dresid, wh, wl, dk, dv, dnormed, theirs, mine, dq, full):
    length = q.shape[0] // rows
    info = Info(info, length, slots)
    for r in range(rows):
        use = info.from_before(r, LANES)
        mask, flipped = info.causal(r), info.causal(r, True)
        for p in range(PAIRS):
            at = pair_slices(length, r, p)
            q_pair, k_pair, v_pair, dn_pair, dd_pair = q[at], k[at], v[at], dn[at], dd[at]
            block, key_sum = state_blocks(state, r, p)
            grad_q = use * (dot3(split(dn_pair), split(block), 1, 1) + dd_pair * key_sum)
            grad_k = grad_v = 0.0
            keys = split(k_pair)
            values = split(jnp.concatenate([v_pair, jnp.full_like(v_pair, 1.0 / HEAD_DIM)], axis=1))
            both = jnp.concatenate([dn_pair, dd_pair], axis=1)
            for head in range(2):
                tops = split(pick(both, head))
                queries = split(pick(q_pair, head))
                tops_n = (tops[0][:, :LANES], tops[1][:, :LANES])
                grad_scores = dot3(tops, values, 1, 1) * mask
                grad_q = grad_q + dot3(split(grad_scores), split(pick(k_pair, head)))
                grad_flipped = dot3(values, tops, 1, 1) * flipped
                grad_k = grad_k + dot3(split(grad_flipped), queries)
                scores_flipped = dot3(keys, queries, 1, 1) * flipped
                grad_v = grad_v + dot3(split(scores_flipped), tops_n)
            dq[at] = grad_q * jnp.minimum(q_pair, 1.0)
            dk[at] = grad_k
            dv[at] = grad_v
    normed = (nh[...], nl[...])
    grads = split(dq[...])
    dnormed[...] = dot3(grads, (wh[0], wl[0]), 1, 1)
    full[...] = dot3(normed, grads, 0, 0)
    deal(info.me, n, full, theirs, mine, 0)
    full[...] = dot3(split(att[...]), split(dresid[...]), 0, 0)
    deal(info.me, n, full, theirs, mine, 1)


def keys_back_kernel(n, slots, rows, info, x, vec, nh, nl, k, v, dk, dv, dnormed, dresid, state, wh, wl, small_in, dbias, dx, theirs, mine, small, gk, gv, full):
    length = k.shape[0] // rows
    info = Info(info, length, slots)
    for r in range(rows):
        kept = info.to_after(r, LANES)
        for p in range(PAIRS):
            at = pair_slices(length, r, p)
            block, key_sum = state_blocks(state, r, p)
            blocks = split(block)
            k_pair = k[at]
            grad_k = dk[at] + kept * (dot3(split(v[at]), blocks, 1, 1) + key_sum)
            gk[at] = grad_k * jnp.minimum(k_pair, 1.0)
            gv[at] = dv[at] + dot3(split(k_pair * kept), blocks)
    normed = (nh[...], nl[...])
    keys, values = split(gk[...]), split(gv[...])
    full[...] = dot3(normed, keys, 0, 0)
    deal(info.me, n, full, theirs, mine, 0)
    full[...] = dot3(normed, values, 0, 0)
    deal(info.me, n, full, theirs, mine, 1)
    grad = dnormed[...] + dot3(keys, (wh[0], wl[0]), 1, 1) + dot3(values, (wh[1], wl[1]), 1, 1)
    unit, scale = normalise(x[...])
    dx[...] = dresid[...] + normalise_back(grad * vec[0:1, :], unit, scale)
    small[...] = small_in[...]
    small[0:1, :] = jnp.sum(grad * unit, axis=0, keepdims=True)
    small[1:2, :] = jnp.sum(grad, axis=0, keepdims=True)
    width = small.shape[1]
    for i in range(dbias.shape[1] // width):
        small[5 + i : 6 + i, :] = dbias[0:1, i * width : (i + 1) * width]


def call(kernel, outs, args, scratch=(), specs=None, **kw):
    specs = specs or [VMEM] * len(args)
    return pl.pallas_call(
        kernel,
        out_shape=outs,
        in_specs=specs,
        out_specs=[VMEM] * len(outs),
        scratch_shapes=list(scratch),
        compiler_params=pltpu.CompilerParams(vmem_limit_bytes=LIMIT),
        **kw,
    )(*args)


def shaped(shape, dtype=F32):
    return jax.ShapeDtypeStruct(tuple(shape), dtype)


def swap(part, axis, bit):
    return lax.ppermute(part, axis, [(i, i ^ bit) for i in range(lax.axis_size(axis))])


def bits_of(axis):
    return [1 << i for i in range(lax.axis_size(axis).bit_length() - 1)]


def gather_rows(part):
    pieces = {0: part}
    for bit in reversed(bits_of("rows")):
        pieces.update({j ^ bit: swap(piece, "rows", bit) for j, piece in pieces.items()})
    return [pieces[j] for j in range(len(pieces))]


def entering(part, end_docs, prev_doc, reverse):
    place = lax.axis_index("seq")
    rows = end_docs.shape[0]
    total, prefix = part, jnp.zeros_like(part)
    sums = part.shape[0] // (HEAD_DIM + 1)
    row_of = jnp.arange(part.shape[0])
    row_of = jnp.where(row_of < sums * HEAD_DIM, row_of // (PAIRS * HEAD_DIM), (row_of - sums * HEAD_DIM) // PAIRS)

    def at(place):
        return lax.dynamic_index_in_dim(end_docs, place, 1, False)

    def scaled(flag, array):
        column = sum(jnp.where(row_of == r, flag[r], 0.0) for r in range(rows))
        return column[:, None] * array

    for bit in bits_of("seq"):
        other = swap(total, "seq", bit)
        mine_late = ((place & bit) != 0) != reverse
        low = place & ~(bit - 1)
        edge = (lambda group: group) if reverse else (lambda group, bit=bit: group + bit - 1)
        my_edge, other_edge = at(edge(low)), at(edge(low ^ bit))
        prefix = prefix + scaled(jnp.where(mine_late & (other_edge == prev_doc), 1.0, 0.0), other)
        same = jnp.where(my_edge == other_edge, 1.0, 0.0)
        total = scaled(jnp.where(mine_late, 1.0, same), total) + scaled(
            jnp.where(mine_late, same, 1.0), other
        )
    return prefix


def sum_scatter(theirs, mine, extra):
    seq_place = lax.axis_index("seq")
    held = mine + swap(theirs, "rows", 1)
    if extra is not None:
        extra = extra + swap(extra, "rows", 1)
    for bit in bits_of("rows")[1:]:
        held = held.reshape((-1, 2) + held.shape[1:])
        held = held[:, 0] + swap(held[:, 1], "rows", bit)
        if extra is not None:
            extra = extra + swap(extra, "rows", bit)
    held = held[0]
    for bit in bits_of("seq"):
        half = held.shape[0] // 2
        late = ((seq_place & bit) != 0).astype(jnp.int32)
        got = swap(lax.dynamic_slice_in_dim(held, (1 - late) * half, half, 0), "seq", bit)
        held = lax.dynamic_slice_in_dim(held, late * half, half, 0) + got
        if extra is not None:
            extra = extra + swap(extra, "seq", bit)
    for bit in reversed(bits_of("seq")):
        got = swap(held, "seq", bit)
        late = (seq_place & bit) != 0
        held = jnp.where(late, jnp.concatenate([got, held]), jnp.concatenate([held, got]))
    return held, extra


def adamw_step(weight, gradient, first_m, second_m, factor, rate, decay):
    clipped = gradient * factor
    new_m = BETA_ONE * first_m + (1.0 - BETA_ONE) * clipped
    new_v = BETA_TWO * second_m + (1.0 - BETA_TWO) * clipped * clipped
    moved = new_m / (1.0 - BETA_ONE**STEP) / (jnp.sqrt(new_v / (1.0 - BETA_TWO**STEP)) + EPS_ADAM)
    return (clipped, weight - rate * (moved + decay * weight), new_m, new_v)


def body(
    activations,
    cotangent,
    seq_starts,
    attn_weight,
    up_weight,
    down_weight,
    vectors,
    attn_m,
    up_m,
    down_m,
    vec_m,
    attn_v,
    up_v,
    down_v,
    vec_v,
):
    rows, length, width = activations.shape
    n = lax.axis_size("rows")
    hidden = up_weight.shape[1]
    tokens = rows * length
    slots = seq_starts.shape[1]
    block = width // n
    me, place = lax.axis_index("rows"), lax.axis_index("seq")
    first = place * length
    info = jnp.concatenate(
        [jnp.stack([me, place, first]).astype(jnp.int32), seq_starts.reshape(-1)]
    )

    edges = jnp.arange(lax.axis_size("seq"), dtype=jnp.int32) * length

    def docs_at(positions):
        return jnp.sum(
            (seq_starts[:, None, :] <= positions[None, :, None]).astype(jnp.int32), axis=2
        )

    end_docs, begin_docs = docs_at(edges + length - 1), docs_at(edges - 1)
    prev_doc = lax.dynamic_index_in_dim(begin_docs, place, 1, False)
    last_doc = lax.dynamic_index_in_dim(end_docs, place, 1, False)

    x = activations.reshape(tokens, width)
    dout = cotangent.reshape(tokens, width)
    state_shape = shaped((rows * PAIRS * (HEAD_DIM + 1), LANES))
    act, half = shaped((tokens, width)), shaped((tokens, width), BF16)

    def matrix(count):
        return [shaped((count, width, width), BF16)] * 2

    kv_pieces = gather_rows(attn_weight[1:3])
    q_pieces = gather_rows(attn_weight[0:1])
    o_pieces = gather_rows(attn_weight[3:4])
    up_pieces = gather_rows(up_weight[None])
    down_pieces = gather_rows(down_weight[None])

    nh, nl, k, v, state, kvh, kvl = call(
        functools.partial(keys_kernel, n, slots, rows),
        [half, half, act, act, state_shape] + matrix(2),
        [info, x, vectors] + kv_pieces,
        specs=[SMEM] + [VMEM] * (2 + n),
    )
    state_in = entering(state, end_docs, prev_doc, False)
    q, numer, denom, qh, ql = call(
        functools.partial(queries_kernel, n, slots, rows),
        [act, act, act] + matrix(1),
        [info, nh, nl, k, v] + q_pieces,
        specs=[SMEM] + [VMEM] * (4 + n),
    )
    att, inv, resid, sh, sl, oh, ol = call(
        functools.partial(attend_kernel, n, slots, rows),
        [act, act, act, half, half] + matrix(1),
        [info, x, vectors, q, numer, denom, state_in] + o_pieces,
        specs=[SMEM] + [VMEM] * (6 + n),
    )

    def assemble_kernel(info, *refs):
        assemble(info[0], refs[:n], refs[n], refs[n + 1])

    uph, upl = call(
        assemble_kernel,
        [shaped((1, width, hidden), BF16)] * 2,
        [info] + up_pieces,
        specs=[SMEM] + [VMEM] * n,
    )
    dnh, dnl = call(
        assemble_kernel,
        [shaped((1, hidden, width), BF16)] * 2,
        [info] + down_pieces,
        specs=[SMEM] + [VMEM] * n,
    )
    wide = min(512, hidden)
    steps = hidden // wide
    whole = lambda shape: pl.BlockSpec(shape, lambda j: (0,) * len(shape))
    across = pl.BlockSpec((tokens, wide), lambda j: (0, j))
    up_block = pl.BlockSpec((width, wide), lambda j: (0, j))
    down_block = pl.BlockSpec((wide, width), lambda j: (j, 0))
    flat = whole((tokens, width))
    row = pl.BlockSpec((1, wide), lambda j: (0, j))
    out, gh, gl, eh, el, dresid, small, dbias = pl.pallas_call(
        feed_kernel,
        grid=(steps,),
        in_specs=[whole(vectors.shape), row, flat, flat, flat, flat]
        + [up_block] * 2
        + [down_block] * 2,
        out_specs=[flat, across, across, across, across, flat, whole((16, width)), row],
        out_shape=[act]
        + [shaped((tokens, hidden), BF16)] * 4
        + [act, shaped((16, width)), shaped((1, hidden))],
        scratch_shapes=[pltpu.VMEM((tokens, width), F32)] * 2
        + [pltpu.VMEM((tokens, width), BF16)] * 2,
        compiler_params=pltpu.CompilerParams(vmem_limit_bytes=LIMIT),
    )(vectors, vectors[5:].reshape(1, hidden), sh, sl, dout, resid, uph[0], upl[0], dnh[0], dnl[0])

    dn, dd, dstate = call(
        functools.partial(attend_back_kernel, slots, rows),
        [act, act, state_shape],
        [info, dresid, oh, ol, q, att, inv],
        specs=[SMEM] + [VMEM] * 6,
    )
    dstate_in = entering(dstate, begin_docs, last_doc, True)

    share = hidden // n

    def block_of(j, half):
        return jnp.where(j < half, 2 * j + 1, 2 * (j - half))

    down_theirs, down_mine = pl.pallas_call(
        lambda info, *refs: down_grad_kernel(*refs),
        grid_spec=pltpu.PrefetchScalarGridSpec(
            num_scalar_prefetch=1,
            grid=(n,),
            in_specs=[
                pl.BlockSpec((tokens, share), lambda j, info: (0, info[0] ^ block_of(j, n // 2)))
            ]
            * 2
            + [pl.BlockSpec((tokens, width), lambda j, info: (0, 0))],
            out_specs=[
                pl.BlockSpec((1, share, width), lambda j, info: (jnp.minimum(j, n // 2 - 1), 0, 0)),
                pl.BlockSpec((1, share, width), lambda j, info: (jnp.maximum(j - n // 2, 0), 0, 0)),
            ],
            scratch_shapes=[pltpu.VMEM((tokens, width), BF16)] * 2,
        ),
        out_shape=[shaped((n // 2, share, width))] * 2,
        compiler_params=pltpu.CompilerParams(vmem_limit_bytes=LIMIT),
    )(info, gh, gl, dout)
    up_out = pl.BlockSpec((n // 2, 1, block, wide), lambda j: (0, j, 0, 0))
    up_theirs, up_mine = pl.pallas_call(
        functools.partial(up_grad_kernel, n),
        grid=(steps,),
        in_specs=[SMEM, flat, flat, across, across],
        out_specs=[up_out, up_out],
        out_shape=[shaped((n // 2, steps, block, wide))] * 2,
        scratch_shapes=[pltpu.VMEM((width, wide), F32)],
        compiler_params=pltpu.CompilerParams(vmem_limit_bytes=LIMIT),
    )(info, sh, sl, eh, el)

    pair = shaped((n // 2, 2, block, width))
    dk, dv, dnormed, qo_theirs, qo_mine = call(
        functools.partial(local_back_kernel, n, slots, rows),
        [act, act, act, pair, pair],
        [info, nh, nl, q, k, v, dn, dd, state_in, att, dresid, qh, ql],
        scratch=[pltpu.VMEM((tokens, width), F32), pltpu.VMEM((width, width), F32)],
        specs=[SMEM] + [VMEM] * 12,
    )
    dx, kv_theirs, kv_mine, small = call(
        functools.partial(keys_back_kernel, n, slots, rows),
        [act, pair, pair, shaped((16, width))],
        [info, x, vectors, nh, nl, k, v, dk, dv, dnormed, dresid, dstate_in, kvh, kvl, small, dbias],
        scratch=[pltpu.VMEM((tokens, width), F32)] * 2 + [pltpu.VMEM((width, width), F32)],
        specs=[SMEM] + [VMEM] * 15,
    )

    def rowed(a):
        return a.reshape(n // 2, -1, width)

    sum_down, _ = sum_scatter(rowed(down_theirs), rowed(down_mine), None)
    sum_up, _ = sum_scatter(rowed(up_theirs), rowed(up_mine), None)
    sum_qo, _ = sum_scatter(rowed(qo_theirs), rowed(qo_mine), None)
    sum_kv, total_small = sum_scatter(rowed(kv_theirs), rowed(kv_mine), small)
    total_vec = total_small[: vectors.shape[0]]
    sum_qo, sum_kv = (a.reshape(2, block, width) for a in (sum_qo, sum_kv))
    shard_attn = jnp.stack([sum_qo[0], sum_kv[0], sum_kv[1], sum_qo[1]])
    shard_up = jnp.swapaxes(sum_up.reshape(steps, block, wide), 0, 1).reshape(block, hidden)
    shard_down = sum_down

    part_square = (
        jnp.sum(shard_attn * shard_attn)
        + jnp.sum(shard_up * shard_up)
        + jnp.sum(shard_down * shard_down)
    )
    for bit in bits_of("rows"):
        part_square = part_square + swap(part_square, "rows", bit)
    square = part_square + jnp.sum(total_vec * total_vec)
    grad_norm = jnp.sqrt(square)
    factor = jnp.minimum(1.0, CLIP_AT / (grad_norm + 1e-06))
    attn_g, attn_new, attn_m_new, attn_v_new = adamw_step(
        attn_weight, shard_attn, attn_m, attn_v, factor, RATE_MAT, DECAY_MAT
    )
    up_g, up_new, up_m_new, up_v_new = adamw_step(
        up_weight, shard_up, up_m, up_v, factor, RATE_MAT, DECAY_MAT
    )
    down_g, down_new, down_m_new, down_v_new = adamw_step(
        down_weight, shard_down, down_m, down_v, factor, RATE_MAT, DECAY_MAT
    )
    vec_g, vec_new, vec_m_new, vec_v_new = adamw_step(
        vectors, total_vec, vec_m, vec_v, factor, RATE_VEC, 0.0
    )
    return (
        out.reshape(activations.shape),
        dx.reshape(activations.shape),
        grad_norm,
        attn_g,
        up_g,
        down_g,
        vec_g,
        attn_new,
        up_new,
        down_new,
        vec_new,
        attn_m_new,
        up_m_new,
        down_m_new,
        vec_m_new,
        attn_v_new,
        up_v_new,
        down_v_new,
        vec_v_new,
    )


def solution(mesh):
    stretch = P("rows", "seq", None)
    stacked = P(None, "rows", None)
    split_rows = P("rows", None)
    weights = (stacked, split_rows, split_rows, P())
    return jax.shard_map(
        body,
        mesh=mesh,
        in_specs=(stretch, stretch, split_rows) + weights * 3,
        out_specs=(stretch, stretch, P()) + weights * 4,
        check_vma=False,
    )
```

```python
import functools
import math

import jax
import jax.numpy as jnp
from jax import lax
from jax.experimental import pallas as pl
from jax.experimental.pallas import tpu as pltpu
from jax.sharding import PartitionSpec as P

HEADS = 8
HEAD_DIM = 64
PAIRS = HEADS // 2
LANES = 2 * HEAD_DIM
STEP = 5

EPS_NORM = 1e-05
EPS_DEN = 1e-06
CLIP_AT = 1.0
BETA_ONE = 0.5
BETA_TWO = 0.5
RATE_MAT = 0.02
RATE_VEC = 0.1
DECAY_MAT = 0.1
EPS_ADAM = 1e-08

F32 = jnp.float32
FORWARD = 0.01
LIMIT = 56 * 1024 * 1024


def cost(us):
    return pl.CostEstimate(flops=int(us * 1e9), bytes_accessed=int(us * 2e6), transcendentals=0)


class Given:
    def __init__(self, ref, copies):
        self.ref, self.copies, self.shape = ref, copies, ref.shape

    def __getitem__(self, at):
        while self.copies:
            self.copies.pop(0).wait()
        return self.ref[at]


class Made:
    def __init__(self, ref, out, send):
        self.ref, self.out, self.send, self.shape = ref, out, send, out.shape
        self.sent = False

    def __getitem__(self, at):
        return self.ref[at]

    def __setitem__(self, at, value):
        self.ref[at] = value

    def flush(self, at=slice(None)):
        self.sent = True
        self.send(self.ref.at[at], self.out.at[at])


class Built:
    def __init__(self, shape, arrays, plan, copies=1):
        self.shape, self.arrays, self.plan, self.copies = shape, arrays, plan, copies


def whole(info, refs, buffer):
    return [(refs[0], buffer)]


def built(operand):
    return operand if isinstance(operand, Built) else Built(operand.shape, [operand], whole)


def call(us, kernel, outs, info, ins, scratch=(), direct=(), smem=(), sends=None):
    ins = [built(a) for a in ins]
    arrays = []
    for a in ins:
        arrays += [b for b in a.arrays if not any(b is c for c in arrays)]
    places = [[next(i for i, c in enumerate(arrays) if c is b) for b in a.arrays] for a in ins]
    sends = sends or len(outs)

    def body(info_ref, *refs):
        refs = list(refs)

        def take(count):
            part, refs[:] = refs[:count], refs[count:]
            return part

        extra, given, results = take(len(smem)), take(len(arrays)), take(len(outs))
        in_buffers, out_buffers = take(len(ins)), take(len(outs) - len(direct))
        in_sems, out_sems = refs.pop(), refs.pop()
        operands, count = [], 0
        for a, at, buffer in zip(ins, places, in_buffers):
            copies = []
            for source, target in a.plan(info_ref, [given[i] for i in at], buffer):
                copies.append(pltpu.make_async_copy(source, target, in_sems.at[count]))
                copies[-1].start()
                count += 1
            operands.append(Given(buffer, copies))
        sent = []

        def send(source, target):
            sent.append(pltpu.make_async_copy(source, target, out_sems.at[len(sent)]))
            sent[-1].start()

        made = [
            Made(None if i in direct else out_buffers.pop(0), out, send)
            for i, out in enumerate(results)
        ]
        kernel(info_ref, *extra, *operands, *made, *refs)
        for operand in operands:
            for copy in operand.copies:
                copy.wait()
        for i, out in enumerate(made):
            if i not in direct and not out.sent:
                out.flush()
        for copy in sent:
            copy.wait()
        assert len(sent) == sends, (len(sent), sends)

    hbm = pl.BlockSpec(memory_space=pltpu.HBM)
    smem_spec = pl.BlockSpec(memory_space=pltpu.SMEM)
    buffers = [pltpu.VMEM(a.shape, F32) for a in ins]
    buffers += [pltpu.VMEM(a.shape, F32) for i, a in enumerate(outs) if i not in direct]
    sems = [pltpu.SemaphoreType.DMA((count,)) for count in (sends, max(1, sum(a.copies for a in ins)))]
    return pl.pallas_call(
        body,
        out_shape=outs,
        in_specs=[smem_spec] * (1 + len(smem)) + [hbm] * len(arrays),
        out_specs=[hbm] * len(outs),
        scratch_shapes=buffers + list(scratch) + sems,
        compiler_params=pltpu.CompilerParams(vmem_limit_bytes=LIMIT),
        cost_estimate=cost(us),
    )(info, *smem, *arrays)


def shaped(shape):
    return jax.ShapeDtypeStruct(tuple(shape), F32)


def row_blocks(pieces, lead=None, top=0):
    def plan(info, refs, buffer):
        rows = buffer.shape[0] // len(refs)
        for j, ref in enumerate(refs):
            at = pl.ds(pl.multiple_of((info[0] ^ j) * rows, rows), rows)
            source = ref if lead is None else ref.at[lead]
            yield source.at[top : top + rows, :], buffer.at[at, :]

    width = pieces[0].shape[-1]
    return Built((width, width), pieces, plan, len(pieces))


def split(a):
    high = a.astype(jnp.bfloat16)
    return high, (a - high.astype(F32)).astype(jnp.bfloat16)


def dot(a, b, ca=1, cb=0):
    dims = (((ca,), (cb,)), ((), ()))
    a, b = (x if isinstance(x, tuple) else split(x) for x in (a, b))

    def one(p, q):
        return lax.dot_general(p, q, dims, preferred_element_type=F32)

    return one(a[0], b[0]) + (one(a[0], b[1]) + one(a[1], b[0]))


def phi(u):
    return jnp.where(u > 0, u + 1.0, jnp.exp(jnp.minimum(u, 0.0)))


def normalise(x):
    centred = x - jnp.mean(x, axis=1, keepdims=True)
    scale = lax.rsqrt(jnp.mean(centred * centred, axis=1, keepdims=True) + EPS_NORM)
    return centred * scale, scale


def normalise_back(grad, unit, scale):
    inner = jnp.mean(grad * unit, axis=1, keepdims=True)
    return scale * (grad - jnp.mean(grad, axis=1, keepdims=True) - unit * inner)


def first_head(shape):
    return lax.broadcasted_iota(jnp.int32, shape, len(shape) - 1) % LANES < HEAD_DIM


def pick(value, head):
    return jnp.where(first_head(value.shape) == (head == 0), value, 0.0)


def lower(shape):
    return lax.broadcasted_iota(jnp.int32, shape, 1) < HEAD_DIM


def halves_of(pair):
    high, low = split(pair)
    turned = pltpu.roll(pair, HEAD_DIM, 1)
    return (high, low), split(turned)


def streamed(plain, turned, tail=None):
    first = lower(plain[0].shape)
    out = []
    for head in range(2):
        here, there = (plain, turned) if head == 0 else (turned, plain)
        end = here[0]
        if tail is not None:
            end = jnp.where(first, end, tail[1 - head])
        out.append(jnp.concatenate([jnp.where(first, here[0], there[1]), end], axis=1))
    return out


def held(plain, turned, fill):
    first = lower(plain[0].shape)
    out = []
    for head in range(2):
        here, there = (plain, turned) if head == 0 else (turned, plain)
        end = jnp.where(first, here[1], jnp.full_like(here[1], fill))
        out.append(jnp.concatenate([jnp.where(first, here[0], there[0]), end], axis=1))
    return out


def alternate(high, low):
    lanes = lax.broadcasted_iota(jnp.int32, high.shape, 1)
    return jnp.where(lanes % HEAD_DIM < HEAD_DIM // 2, high, low)


def once(a, b):
    return lax.dot_general(a, b, (((1,), (1,)), ((), ())), preferred_element_type=F32)


def beside(halves, head, fill=0.0):
    high, low = halves
    mine = lower(high.shape) == (head == 0)
    return jnp.concatenate(
        [jnp.where(mine, high, jnp.full_like(high, fill)), jnp.where(mine, low, jnp.zeros_like(low))],
        axis=1,
    )


def mixed(scores, pair):
    high, low = split(scores)
    count = high.shape[0]
    both = lax.dot_general(
        jnp.concatenate([high, low], axis=0), pair, (((1,), (0,)), ((), ())), preferred_element_type=F32
    )
    both = both[:count] + both[count:]
    return both[:, :LANES] + both[:, LANES:]


def block_ones():
    shape = (LANES, LANES)
    rows, lanes = (lax.broadcasted_iota(jnp.int32, shape, d) // HEAD_DIM for d in (0, 1))
    return jnp.where(rows == lanes, 1.0, 0.0)


class Info:
    def __init__(self, ref, length, slots):
        self.ref, self.length, self.slots = ref, length, slots
        self.me, self.place, self.first = ref[0], ref[1], ref[2]

    def starts(self, r):
        return [self.ref[3 + r * self.slots + i] for i in range(self.slots)]

    def document(self, r, position):
        return sum(jnp.where(a <= position, 1, 0) for a in self.starts(r))

    def causal(self, r, flipped=False):
        shape = (self.length, self.length)
        t = self.first + lax.broadcasted_iota(jnp.int32, shape, 1 if flipped else 0)
        s = self.first + lax.broadcasted_iota(jnp.int32, shape, 0 if flipped else 1)
        ok = t >= s
        for a in self.starts(r):
            ok = ok & ((t < a) | (s >= a))
        return jnp.where(ok, 1.0, 0.0)

    def from_before(self, r, width):
        t = self.first + lax.broadcasted_iota(jnp.int32, (self.length, width), 0)
        ok = t >= 0
        for a in self.starts(r):
            ok = ok & ((a < self.first) | (t < a))
        return jnp.where(ok, 1.0, 0.0)

    def to_after(self, r, width):
        s = self.first + lax.broadcasted_iota(jnp.int32, (self.length, width), 0)
        last = self.first + self.length - 1
        ok = s >= 0
        for a in self.starts(r):
            ok = ok & ((s >= a) | (a > last))
        return jnp.where(ok, 1.0, 0.0)


def state_blocks(ref, r, p):
    at = (r * PAIRS + p) * HEAD_DIM
    packed = ref[at : at + HEAD_DIM, :]
    sums = ref.shape[0] // (HEAD_DIM + 1) * HEAD_DIM + r * PAIRS + p
    return (
        jnp.concatenate([pick(packed, 0), pick(packed, 1)], axis=0),
        ref[sums : sums + 1, :],
    )


def store_state(ref, r, p, full, key_sum):
    at = (r * PAIRS + p) * HEAD_DIM
    top, bottom = full[:HEAD_DIM], full[HEAD_DIM:]
    ref[at : at + HEAD_DIM, :] = jnp.where(first_head(top.shape), top, bottom)
    sums = ref.shape[0] // (HEAD_DIM + 1) * HEAD_DIM + r * PAIRS + p
    ref[sums : sums + 1, :] = key_sum


def pair_slices(length, r, p):
    return slice(r * length, (r + 1) * length), slice(p * LANES, (p + 1) * LANES)


def row_slice(length, r):
    return slice(r * length, (r + 1) * length)


def keys_kernel(slots, rows, ref, x, vec, wk, wv, wq, normed, k, v, state, query, key, value):
    length = x.shape[0] // rows
    info = Info(ref, length, slots)
    unit, _ = normalise(x[...])
    normed[...] = unit * vec[0:1, :] + vec[1:2, :]
    normed.flush()
    k[...] = phi(dot(normed[...], wk[...]))
    v[...] = dot(normed[...], wv[...])
    k.flush()
    v.flush()
    for r in range(rows):
        kept = info.to_after(r, LANES)
        for p in range(PAIRS):
            at = pair_slices(length, r, p)
            masked = k[at] * kept
            store_state(state, r, p, dot(masked, v[at], 0, 0), jnp.sum(masked, axis=0, keepdims=True))
    state.flush()
    for source, out in ((wq, query), (wk, key), (wv, value)):
        source[0:8, 0:128]
        out.send(source.ref, out.out)


def queries_kernel(slots, rows, ref, normed, wq, k, v, q, numer, denom):
    length = k.shape[0] // rows
    info = Info(ref, length, slots)
    q[...] = phi(dot(normed[...], wq[...]))
    q.flush()
    for r in range(rows):
        mask = info.causal(r)
        for p in range(PAIRS):
            at = pair_slices(length, r, p)
            lefts, rights = streamed(*halves_of(q[at])), held(*halves_of(k[at]), 0.0)
            values = split(v[at])
            sums = [
                mixed(once(lefts[head], rights[head]) * mask, beside(values, head, 1.0))
                for head in range(2)
            ]
            first = lower(sums[0].shape)
            numer[at] = jnp.where(first, *sums)
            denom[at] = pltpu.roll(jnp.where(first, sums[1], sums[0]), HEAD_DIM, 1)
        numer.flush(row_slice(length, r))
        denom.flush(row_slice(length, r))


def attend_kernel(slots, rows, bit, ref, prefix, other, q, numer, denom, wo, x, vec, att, inv, resid, second, state, out_w):
    length = x.shape[0] // rows
    info = Info(ref, length, slots)
    enter(info, bit, False, prefix, other, state)
    state.flush()
    ones = block_ones()
    for r in range(rows):
        use = info.from_before(r, LANES)
        for p in range(PAIRS):
            at = pair_slices(length, r, p)
            block, key_sum = state_blocks(state, r, p)
            q_pair = q[at] * use
            top = numer[at] + dot(q_pair, block)
            under = denom[at] + dot(q_pair * key_sum, ones) + EPS_DEN
            inverse = 1.0 / under
            inv[at] = inverse
            att[at] = top * inverse
        att.flush(row_slice(length, r))
        inv.flush(row_slice(length, r))
    resid[...] = x[...] + dot(att[...], wo[...])
    resid.flush()
    unit, _ = normalise(resid[...])
    second[...] = unit * vec[2:3, :] + vec[3:4, :]
    second.flush()
    out_w.send(wo.ref, out_w.out)


def feed_kernel(js, last, info, second, dout, *refs):
    count = len(js)
    blocks, refs = [refs[2 * i : 2 * i + 2] for i in range(count)], refs[2 * count :]
    if last:
        bias, vec, back_in, resid, g, e, dresid, small, dbias, back = refs
    else:
        bias, vec, g, e, back, acc, dbias = refs
    share = dbias.shape[1] // count
    for i, (up, down) in enumerate(blocks):
        at = pl.ds(pl.multiple_of((info[0] ^ js[i]) * share, share), share)
        here = (slice(None), slice(i * share, (i + 1) * share))
        h = dot(second[...], up[...]) + bias[:, at]
        cdf = 0.5 * (1.0 + lax.erf(h * math.sqrt(0.5)))
        g[here] = h * cdf
        g.flush(here)
        slope = cdf + h * (jnp.exp(-0.5 * h * h) * (1.0 / math.sqrt(2.0 * math.pi)))
        grad = dot(dout[...], down[...], 1, 1) * slope
        e[here] = grad
        e.flush(here)
        dbias[here] = jnp.sum(grad, axis=0, keepdims=True)
        part = dot(e[here], up[...], 1, 1)
        if i == 0:
            back[...] = back_in[...] + part if last else part
        else:
            back[...] = back[...] + part
        if not last:
            ahead = dot(g[here], down[...])
            acc[...] = ahead if i == 0 else acc[...] + ahead
    if last:
        unit, scale = normalise(resid[...])
        grad_second = back[...]
        small[...] = jnp.zeros(small.shape, F32)
        small[2:3, :] = jnp.sum(grad_second * unit, axis=0, keepdims=True)
        small[3:4, :] = jnp.sum(grad_second, axis=0, keepdims=True)
        small[4:5, :] = jnp.sum(dout[...], axis=0, keepdims=True)
        dresid[...] = dout[...] + normalise_back(grad_second * vec[2:3, :], unit, scale)


def out_kernel(info, vec, resid, acc, *refs):
    *refs, out = refs
    total = resid[...] + acc[...] + vec[4:5, :]
    g, *downs = refs
    share = g.shape[1] // len(downs)
    for i, down in enumerate(downs):
        total = total + dot(g[:, i * share : (i + 1) * share], down[...])
    out[...] = total


def state_rows(ref):
    sums = ref.shape[0] // (HEAD_DIM + 1)
    for r in range(sums // PAIRS):
        yield r, slice(r * PAIRS * HEAD_DIM, (r + 1) * PAIRS * HEAD_DIM)
        yield r, slice(sums * HEAD_DIM + r * PAIRS, sums * HEAD_DIM + (r + 1) * PAIRS)


def enter(info, bit, reverse, prefix, other, out):
    for r, at in state_rows(out):
        out[at, :] = prefix[at, :] + other[at, :] * meet(info, bit, reverse, r)[2]


def joins_kernel(slots, length, stretches, ref, out):
    info = Info(ref, length, slots)
    bits = [1 << i for i in range(stretches.bit_length() - 1)][:-1]
    for i, (reverse, bit) in enumerate((reverse, bit) for reverse in (False, True) for bit in bits):
        for r, at in state_rows(out.ref.at[0]):
            mine_late, same, reaches = meet(info, bit, reverse, r)
            values = (jnp.where(mine_late, 1.0, same), jnp.where(mine_late, same, 1.0), reaches)
            for part, value in enumerate(values):
                out[3 * i + part, at, :] = jnp.full((at.stop - at.start, LANES), value)


def meet(info, bit, reverse, r):
    place, length = info.place, info.length
    bits = place & bit
    mine_late = (bits == 0) if reverse else (bits != 0)
    low = place & ~(bit - 1)
    shift = -1 if reverse else bit * length - 1
    here, there = (info.document(r, group * length + shift) for group in (low, low ^ bit))
    own = info.document(r, info.first + (length - 1 if reverse else -1))
    return mine_late, jnp.where(here == there, 1.0, 0.0), jnp.where(mine_late & (there == own), 1.0, 0.0)


def attend_back_kernel(slots, rows, ref, dresid, wo, inv, att, q, dn, dd, state):
    length = q.shape[0] // rows
    info = Info(ref, length, slots)
    grad = dot(dresid[...], wo[...], 1, 1)
    ones = block_ones()
    for r in range(rows):
        use = info.from_before(r, LANES)
        for p in range(PAIRS):
            at = pair_slices(length, r, p)
            grad_pair = grad[at]
            over = grad_pair * inv[at]
            dn[at] = over
            under = -dot(grad_pair * att[at], ones) * inv[at]
            dd[at] = under
            q_pair = q[at] * use
            full = dot(q_pair, over, 0, 0)
            store_state(state, r, p, full, jnp.sum(q_pair * under, axis=0, keepdims=True))
        dn.flush(row_slice(length, r))
        dd.flush(row_slice(length, r))


def put_block(info, stretches, group, odd, stretch, source, theirs, mine, lanes=slice(None)):
    rows = source.shape[0]
    groups = theirs.shape[0] // (stretches * rows)
    core = (info[0] & 1) ^ odd
    mask = group + groups * (info[1] ^ stretch)
    at = Plan(groups, stretches).position(mask, core) * rows
    out = theirs if odd else mine
    out.send(source, out.out.at[pl.ds(pl.multiple_of(at, rows), rows), lanes])


def down_grads_kernel(n, stretches, info, dout, *refs):
    *refs, theirs, mine, full = refs
    grad_out = dout[...]
    rows = full.shape[1] // stretches
    j = 0
    for g in refs:
        share = full.shape[1]
        for i in range(g.shape[1] // share):
            full[j] = dot(g[:, i * share : (i + 1) * share], grad_out, 0, 0)
            for s in range(stretches):
                source = full.at[j, s * rows : (s + 1) * rows, :]
                put_block(info, stretches, j // 2, j & 1, s, source, theirs, mine)
            j += 1


def up_grads_kernel(n, stretches, info, second, *refs):
    *refs, theirs, mine, full = refs
    share, width = full.shape[2], theirs.shape[1]
    tall = full.shape[1] // n
    rows = tall * (n * share // width) // stretches
    j = 0
    for e in refs:
        for i in range(e.shape[1] // share):
            full[j] = dot(second[...], e[:, i * share : (i + 1) * share], 0, 0)
            column = (info[0] ^ j) * share
            lanes = pl.ds(pl.multiple_of(lax.rem(column, width), share), share)
            for m in range(n):
                for b in range(tall // rows):
                    start = (info[0] ^ m) * tall + b * rows
                    source = full.at[j, pl.ds(pl.multiple_of(start, rows), rows), :]
                    stretch = lax.div(column, width) * (tall // rows) + b
                    put_block(info, stretches, m // 2, m & 1, stretch, source, theirs, mine, lanes)
            j += 1


def deal(info, n, stretches, full, theirs, mine, slot, slots=4):
    tall = full.shape[0] // n
    rows = tall * slots // stretches
    for m in range(n):
        for i in range(tall // rows):
            start = (info[0] ^ m) * tall + i * rows
            source = full.at[pl.ds(pl.multiple_of(start, rows), rows), :]
            stretch = slot * (tall // rows) + i
            put_block(info, stretches, m // 2, m & 1, stretch, source, theirs, mine)


def local_back_kernel(slots, rows, ref, q, k, v, dn, dd, state, normed, wq, att, dresid, dk, dv, dnormed, gq, go, dq):
    length = q.shape[0] // rows
    info = Info(ref, length, slots)
    for r in range(rows):
        use = info.from_before(r, LANES)
        mask, flipped = info.causal(r), info.causal(r, True)
        for p in range(PAIRS):
            at = pair_slices(length, r, p)
            q_pair, k_pair, v_pair, dn_pair, dd_pair = q[at], k[at], v[at], dn[at], dd[at]
            block, key_sum = state_blocks(state, r, p)
            grad_q = use * (dot(dn_pair, block, 1, 1) + dd_pair * key_sum)
            grad_k = grad_v = 0.0
            q_halves, k_halves, v_halves, dn_halves = (
                halves_of(a) for a in (q_pair, k_pair, v_pair, dn_pair)
            )
            tops = streamed(*dn_halves, [alternate(*h) for h in halves_of(dd_pair)])
            values = held(*v_halves, 2.0 / HEAD_DIM)
            queries, keys = streamed(*q_halves), held(*k_halves, 0.0)
            for head in range(2):
                grad_scores = once(tops[head], values[head]) * mask
                grad_q = grad_q + mixed(grad_scores, beside(k_halves[0], head))
                grad_flipped = once(values[head], tops[head]) * flipped
                grad_k = grad_k + mixed(grad_flipped, beside(q_halves[0], head))
                scores_flipped = once(keys[head], queries[head]) * flipped
                grad_v = grad_v + mixed(scores_flipped, beside(dn_halves[0], head))
            dq[at] = grad_q * jnp.minimum(q_pair, 1.0)
            dk[at] = grad_k
            dv[at] = grad_v
        dk.flush(row_slice(length, r))
        dv.flush(row_slice(length, r))
    dnormed[...] = dot(dq[...], wq[...], 1, 1)
    dnormed.flush()
    gq[...] = dot(normed[...], dq[...], 0, 0)
    gq.flush()
    go[...] = dot(att[...], dresid[...], 0, 0)


def keys_back_kernel(n, slots, rows, bit, stretches, ref, prefix, other, v, k, dk, dv, normed, gq, go, theirs, mine, gk, gv, full, state):
    length = k.shape[0] // rows
    info = Info(ref, length, slots)
    enter(info, bit, True, prefix, other, state)
    for r in range(rows):
        kept = info.to_after(r, LANES)
        for p in range(PAIRS):
            at = pair_slices(length, r, p)
            block, key_sum = state_blocks(state, r, p)
            k_pair = k[at]
            grad_k = dk[at] + kept * (dot(v[at], block, 1, 1) + key_sum)
            gk[at] = grad_k * jnp.minimum(k_pair, 1.0)
            gv[at] = dv[at] + dot(k_pair * kept, block)
    full[0] = dot(normed[...], gk[...], 0, 0)
    deal(ref, n, stretches, full.at[0], theirs, mine, 1)
    full[1] = dot(normed[...], gv[...], 0, 0)
    deal(ref, n, stretches, full.at[1], theirs, mine, 2)
    for slot, source in ((0, gq), (3, go)):
        source[0:8, 0:128]
        deal(ref, n, stretches, source.ref, theirs, mine, slot)


def input_back_kernel(n, info, gk, wk, gv, wv, dnormed, x, dresid, vec, small_in, *refs):
    *biases, dx, small = refs
    grad = dnormed[...] + dot(gk[...], wk[...], 1, 1) + dot(gv[...], wv[...], 1, 1)
    unit, scale = normalise(x[...])
    dx[...] = dresid[...] + normalise_back(grad * vec[0:1, :], unit, scale)
    dx.flush()
    small[...] = small_in[...]
    small[0:1, :] = jnp.sum(grad * unit, axis=0, keepdims=True)
    small[1:2, :] = jnp.sum(grad, axis=0, keepdims=True)
    width = small.shape[1]
    share = sum(ref.shape[1] for ref in biases) // n
    j = 0
    for bias in biases:
        for i in range(bias.shape[1] // share):
            column = (info[0] ^ j) * share
            lanes = pl.ds(pl.multiple_of(lax.rem(column, width), share), share)
            small[pl.ds(5 + lax.div(column, width), 1), lanes] = bias[0:1, i * share : (i + 1) * share]
            j += 1


def adamw_step(weight, gradient, first_m, second_m, factor, rate, decay):
    clipped = gradient * factor
    new_m = BETA_ONE * first_m + (1.0 - BETA_ONE) * clipped
    new_v = BETA_TWO * second_m + (1.0 - BETA_TWO) * clipped * clipped
    moved = new_m / (1.0 - BETA_ONE**STEP) / (jnp.sqrt(new_v / (1.0 - BETA_TWO**STEP)) + EPS_ADAM)
    return (clipped, weight - rate * (moved + decay * weight), new_m, new_v)


def update_kernel(place_of, count, info, factor, *refs):
    ins, outs, buffers = refs[: 4 * count], refs[4 * count : -1], refs[-1]
    for i in range(count):
        gradient, weight, first_m, second_m = (a[...] for a in ins[4 * i : 4 * i + 4])
        chunk, at = place_of(info, i)
        results = adamw_step(weight, gradient, first_m, second_m, factor[0], RATE_MAT, DECAY_MAT)
        for part, result in enumerate(results):
            buffers[4 * i + part] = result
            out = outs[4 * chunk + part]
            out.send(buffers.at[4 * i + part], out.out.at[at])


def swap(part, axis, bit):
    return lax.ppermute(part, axis, [(i, i ^ bit) for i in range(lax.axis_size(axis))])


def bits_of(axis):
    return [1 << i for i in range(lax.axis_size(axis).bit_length() - 1)]


def after(part, *others):
    return lax.optimization_barrier((part, *others))[0]


class Plan:
    def __init__(self, groups=None, stretches=None):
        self.groups = groups or lax.axis_size("rows") // 2
        self.stretches = stretches or lax.axis_size("seq")
        ys = [1 << i for i in range(self.groups.bit_length() - 1)]
        seq = [self.groups << i for i in range(self.stretches.bit_length() - 1)]
        xs, zs = seq[: len(ys)], seq[len(ys) :]
        first, second = [], []
        for y, x in zip(ys, xs):
            first += [y, x]
            second += [x, y]
        self.down = list(zip(first + zs, second + zs))
        zs, xs = zs[::-1], xs[::-1]
        self.up = list(zip(zs + xs, xs + zs))
        order = [[0], [0]]
        for bits in self.up:
            order = [o + [m ^ bit for m in o] for o, bit in zip(order, bits)]
        self.order = [[m // self.groups for m in o] for o in order]

    def position(self, mask, core):
        steps = len(self.down)
        places = [
            sum(jnp.where(mask & bits[c], 1 << (steps - 1 - t), 0) for t, bits in enumerate(self.down))
            for c in (0, 1)
        ]
        return jnp.where(core == 0, *places)

    def move(self, part, bits):
        rows = 2 * self.groups
        pairs = []
        for i in range(rows * self.stretches):
            bit = bits[i & 1]
            flip = bit * 2 if bit < self.groups else bit // self.groups * rows
            pairs.append((i, i ^ flip))
        return lax.ppermute(part, ("seq", "rows"), pairs)


def by_core(info, pair):
    return jnp.where(info[0] & 1 == 0, pair[0], pair[1])


class Chunk:
    def __init__(self, theirs, mine):
        self.plan, self.step, self.tail, self.result = Plan(), 0, 0, None
        self.got, self.held = [swap(theirs, "rows", 1)], mine

    def add(self, extra):
        self.tail, self.extra = extra.shape[0], extra
        self.got.append(swap(extra, "rows", 1))

    def advance(self):
        plan, step, held = self.plan, self.step, self.held
        self.step += 1
        got, *extra = self.got
        if self.tail and 0 < step <= len(plan.down):
            got, extra = got[: -self.tail], [got[-self.tail :]]
        if extra:
            self.extra = self.extra + extra[0]
        if step < len(plan.down):
            half = held.shape[0] // 2
            send = held[half:] + got[half:]
            self.held = held[:half] + got[:half]
            if self.tail:
                send = jnp.concatenate([send, self.extra], axis=0)
            self.got = [plan.move(send, plan.down[step])]
            return
        rise = step - len(plan.down)
        if rise < len(plan.up):
            self.held = held + got if rise == 0 else jnp.concatenate([held, got], axis=0)
            self.got = [plan.move(self.held, plan.up[rise])]
            return
        self.result = [held, got]


def meeting(arrays, chunks=()):
    waits = [a for chunk in chunks for a in chunk.got]
    out = lax.optimization_barrier((*arrays, *waits))
    rest = list(out[len(arrays) :])
    for chunk in chunks:
        chunk.got = [rest.pop(0) for _ in chunk.got]
    return out[: len(arrays)]


def meeting_of(arrays, parts):
    out = lax.optimization_barrier((*arrays, *parts.values()))
    return out[: len(arrays)], dict(zip(parts, out[len(arrays) :]))


def sum_rows(part, axes):
    for axis in axes:
        for bit in bits_of(axis):
            part = part + swap(part, axis, bit)
    return part


def update(info, factor, chunks):
    plan = Plan()
    half = plan.stretches // 2
    ins, places = [], []
    for k in range(plan.stretches):
        masks = [order[k] for order in plan.order]
        for i, (gathered, *arrays) in enumerate(chunks):
            rows, wide = gathered[0].shape[0] // half, gathered[0].shape[1]
            tall = arrays[0].shape[0]

            def at(info, masks=masks, rows=rows, wide=wide, tall=tall):
                start = (info[1] ^ by_core(info, masks)) * rows
                return (
                    pl.ds(pl.multiple_of(lax.rem(start, tall), rows), rows),
                    pl.ds(pl.multiple_of(lax.div(start, tall) * wide, wide), wide),
                )

            def part(info, refs, buffer, at=at):
                return [(refs[0].at[at(info)], buffer)]

            def gradient(info, refs, buffer, top=k % half * rows, rows=rows):
                return [(refs[0].at[top : top + rows, :], buffer)]

            ins.append(Built((rows, wide), [gathered[k // half]], gradient))
            ins += [Built((rows, wide), [a], part) for a in arrays]
            places.append((i, at))
    outs = [shaped(chunk[1].shape) for chunk in chunks for _ in range(4)]

    def place_of(info, i):
        chunk, at = places[i]
        return chunk, at(info)

    return call(
        10,
        functools.partial(update_kernel, place_of, len(places)),
        outs,
        info,
        ins,
        smem=[factor],
        direct=range(len(outs)),
        sends=4 * len(places),
        scratch=[pltpu.VMEM((4 * len(places),) + ins[0].shape, F32)],
    )


def body(
    activations,
    cotangent,
    seq_starts,
    attn_weight,
    up_weight,
    down_weight,
    vectors,
    attn_m,
    up_m,
    down_m,
    vec_m,
    attn_v,
    up_v,
    down_v,
    vec_v,
):
    rows, length, width = activations.shape
    n = lax.axis_size("rows")
    hidden = up_weight.shape[1]
    tokens = rows * length
    slots = seq_starts.shape[1]
    block = width // n
    me, place = lax.axis_index("rows"), lax.axis_index("seq")
    first = place * length
    info = jnp.concatenate(
        [jnp.stack([me, place, first]).astype(jnp.int32), seq_starts.reshape(-1)]
    )

    x = activations.reshape(tokens, width)
    dout = cotangent.reshape(tokens, width)
    state_shape = shaped((rows * PAIRS * (HEAD_DIM + 1), LANES))
    act = shaped((tokens, width))

    seq_bits = bits_of("seq")
    joins, bit = len(seq_bits) - 1, seq_bits[-1]
    stretches = lax.axis_size("seq")

    def start(total, i):
        return swap(total, "seq", seq_bits[i])

    def joined(total, other, prefix, reverse, i):
        own, its, entered = (factors[3 * (joins * reverse + i) + part] for part in range(3))
        prefix = [part + other * entered for part in prefix] or [other * entered]
        return prefix[0], total * own + other * its

    factors = call(
        FORWARD * 2.5,
        functools.partial(joins_kernel, slots, length, stretches),
        [shaped((6 * joins,) + state_shape.shape)],
        info,
        [],
    )[0]
    share = hidden // n
    distances = range(1, n // 2)

    def columns(distance):
        chip = (me // 2) ^ distance
        part = lax.dynamic_slice_in_dim(up_weight, chip * 2 * share, 2 * share, 1)
        return jnp.split(part, 2 * share // width, axis=1)

    first = {d: swap(attn_weight[:3], "rows", 2 * d) for d in distances}
    link = first[n // 2 - 1]
    near_parts = {d: jnp.concatenate([attn_weight[3]] + columns(d), axis=0) for d in distances}
    near = {d: swap(after(part, link), "rows", 2 * d) for d, part in near_parts.items()}
    far_parts = {
        d: jnp.concatenate([c for e in distances for c in columns(d ^ e)] + [down_weight], axis=0)
        for d in distances
    }

    def both_cores(chips):
        got = {2 * d: part for d, part in chips.items()}
        got.update({2 * d + 1: swap(part, "rows", 1) for d, part in chips.items()})
        return got

    def ordered(pieces):
        return [pieces[j] for j in sorted(pieces)]

    qkv = both_cores({0: attn_weight[:3], **{d: after(part, factors) for d, part in first.items()}})
    own = both_cores({0: attn_weight[3]}), both_cores({0: up_weight}), both_cores({0: down_weight})
    own_out, own_up, own_down = (ordered(pieces) for pieces in own)
    qkv = ordered(qkv)
    square_shape = shaped((width, width))
    normed, k, v, state, wq, wk, wv = call(
        FORWARD * 5.6,
        functools.partial(keys_kernel, slots, rows),
        [act, act, act, state_shape] + [square_shape] * 3,
        info,
        [x, vectors] + [row_blocks(qkv, lead) for lead in (1, 2, 0)],
        direct=(4, 5, 6),
    )
    other = start(state, 0)
    q, numer, denom = call(
        FORWARD * 8.5,
        functools.partial(queries_kernel, slots, rows),
        [act, act, act],
        info,
        [after(normed, state), wq, k, v],
        sends=1 + 2 * rows,
    )
    (other, q), near = meeting_of([other, q], near)
    prefix, total = joined(state, other, [], False, 0)
    other = start(total, 1)
    near_all = ordered(both_cores({d: after(part, total) for d, part in near.items()}))
    for i in range(1, joins):
        prefix, total = joined(total, after(other, *near_all), [prefix], False, i)
        other = start(total, i + 1)
    far = {d: swap(after(part, link), "rows", 2 * d) for d, part in far_parts.items()}
    att, inv, resid, second, state_in, wo = call(
        FORWARD * 6.3,
        functools.partial(attend_kernel, slots, rows, bit),
        [act, act, act, act, state_shape, square_shape],
        info,
        [prefix, other, q, numer, denom, row_blocks(own_out + near_all), x, vectors],
        direct=(5,),
        sends=4 + 2 * rows,
    )

    bias = vectors[5:].reshape(1, hidden)
    small_shape = shaped((16, width))

    def up_columns(j, parts, top):
        def plan(info, refs, buffer):
            mine = (info[0] ^ j) * share
            column = ((info[0] ^ j) & 1) * share
            for m, ref in enumerate(refs):
                at = pl.ds(pl.multiple_of((info[0] ^ m) * block, block), block)
                if m < 2:
                    source = ref.at[:, pl.ds(pl.multiple_of(mine, share), share)]
                else:
                    row = top + lax.div(column, width) * block
                    lanes = pl.ds(pl.multiple_of(lax.rem(column, width), share), share)
                    source = ref.at[pl.ds(pl.multiple_of(row, block), block), lanes]
                yield source, buffer.at[at, :]

        return Built((width, share), own_up + parts, plan, n)

    def bottom(part):
        top = part.shape[0] - share
        return Built((share, width), [part], lambda info, refs, buffer: [(refs[0].at[top:, :], buffer)])

    def feed(js, blocks, extra, outs, scratch=()):
        wide = shaped((tokens, share * len(js)))
        return call(
            FORWARD * 11.5,
            functools.partial(feed_kernel, js, bool(extra)),
            [wide, wide] + outs + [shaped((1, share * len(js)))],
            info,
            [second, dout] + blocks + [bias, vectors] + extra,
            scratch=scratch,
            sends=2 * len(js) + len(outs) + 1,
        )

    js = list(range(2))
    blocks = [a for j in js for a in (up_columns(j, near_all, block), own_down[j])]
    g0, e0, back, acc, dbias0 = feed(js, blocks, [], [act, act])
    (g0,), far = meeting_of([g0], far)
    far_all = ordered(both_cores(far))
    js = list(range(2, n))
    tops = [(j // 2 - 1) * (2 * share // width) * block for j in js]
    far_down = [bottom(part) for part in far_all]
    blocks = [a for j, top, down in zip(js, tops, far_down) for a in (up_columns(j, far_all, top), down)]
    g1, e1, dresid, small, dbias1 = feed(
        js, blocks, [back, resid], [act, small_shape], [pltpu.VMEM((tokens, width), F32)]
    )

    dn, dd, dstate = call(
        5.4,
        functools.partial(attend_back_kernel, slots, rows),
        [act, act, state_shape],
        info,
        [dresid, wo, inv, att, q],
        sends=1 + 2 * rows,
    )

    half_rows = shaped((n // 2 * share, width))

    def gradients(kernel, common, tops):
        full = (n, width, share) if kernel is up_grads_kernel else (n, share, width)
        return call(
            7,
            functools.partial(kernel, n, stretches),
            [half_rows] * 2,
            info,
            [common] + tops,
            direct=(0, 1),
            scratch=[pltpu.VMEM(full, F32)],
            sends=n * n * stretches * width // hidden if kernel is up_grads_kernel else n * stretches,
        )

    other = start(dstate, 0)
    down_theirs, down_mine = gradients(down_grads_kernel, after(dout, dstate), [g0, g1])
    other, down_theirs, down_mine = meeting([other, down_theirs, down_mine])

    dprefix, dtotal = joined(dstate, other, [], True, 0)
    other = start(dtotal, 1)
    chunk_down = Chunk(down_theirs, down_mine)
    up_theirs, up_mine = gradients(up_grads_kernel, after(second, dtotal), [e0, e1])
    chunks = [chunk_down]
    other, up_theirs, up_mine, dprefix = meeting([other, up_theirs, up_mine, dprefix], chunks)

    for i in range(1, joins):
        dprefix, dtotal = joined(dtotal, other, [dprefix], True, i)
        other = start(dtotal, i + 1)
        if i + 1 < joins:
            (other,) = meeting([other], chunks)
    chunk_down.advance()
    chunk_up = Chunk(up_theirs, up_mine)
    dk, dv, dnormed, gq, go = call(
        16,
        functools.partial(local_back_kernel, slots, rows),
        [act, act, act, square_shape, square_shape],
        info,
        [after(q, dtotal), k, v, dn, dd, state_in, normed, wq, att, dresid],
        scratch=[pltpu.VMEM((tokens, width), F32)],
        sends=3 + 2 * rows,
    )
    chunks = [chunk_down, chunk_up]
    dk, other, dprefix = meeting([dk, other, dprefix], chunks)

    chunk_down.advance()
    chunk_up.advance()
    four = shaped((n // 2 * 4 * block, width))
    attn_theirs, attn_mine, gk, gv = call(
        6,
        functools.partial(keys_back_kernel, n, slots, rows, bit, stretches),
        [four, four, act, act],
        info,
        [dprefix, other, v, k, dk, dv, normed, gq, go],
        direct=(0, 1),
        scratch=[pltpu.VMEM((2, width, width), F32), pltpu.VMEM(state_shape.shape, F32)],
        sends=n * stretches + 2,
    )
    attn_theirs, attn_mine, gk = meeting([attn_theirs, attn_mine, gk], chunks)

    chunk_attn = Chunk(attn_theirs, attn_mine)
    chunk_down.advance()
    chunk_up.advance()
    dx, small = call(
        5,
        functools.partial(input_back_kernel, n),
        [act, small_shape],
        info,
        [gk, wk, gv, wv, dnormed, x, dresid, vectors, small, dbias0, dbias1],
    )
    chunks = [chunk_attn, chunk_down, chunk_up]
    small, late = meeting([small, resid], chunks)

    chunk_attn.add(small)
    for chunk in chunks:
        chunk.advance()
    out = call(5, out_kernel, [act], info, [vectors, late, acc, g1] + far_down)[0]
    while chunks:
        (out,) = meeting([out], chunks)
        for chunk in chunks:
            chunk.advance()
        chunks = [chunk for chunk in chunks if chunk.result is None]
    up_all, down_all, attn_all = chunk_up.result, chunk_down.result, chunk_attn.result
    total_vec = chunk_attn.extra[: vectors.shape[0]]
    squares = [jnp.sum(a * a) for a in up_all + down_all + attn_all]
    square = sum_rows(sum(squares), ("rows",)) + jnp.sum(total_vec * total_vec)
    grad_norm = jnp.sqrt(square)
    factor = jnp.minimum(1.0, CLIP_AT / (grad_norm + 1e-06))
    scale = factor.reshape(1)

    def flat(a):
        return a.reshape(-1, width)

    results = update(
        info,
        scale,
        [
            (up_all, up_weight, up_m, up_v),
            (down_all, down_weight, down_m, down_v),
            (attn_all, flat(attn_weight), flat(attn_m), flat(attn_v)),
        ],
    )
    up_g, up_new, up_m_new, up_v_new = results[:4]
    down_g, down_new, down_m_new, down_v_new = results[4:8]
    attn_g, attn_new, attn_m_new, attn_v_new = results[8:]
    attn_g, attn_new, attn_m_new, attn_v_new = (
        a.reshape(attn_weight.shape) for a in (attn_g, attn_new, attn_m_new, attn_v_new)
    )
    vec_g, vec_new, vec_m_new, vec_v_new = adamw_step(
        vectors, total_vec, vec_m, vec_v, factor, RATE_VEC, 0.0
    )
    return (
        out.reshape(activations.shape),
        dx.reshape(activations.shape),
        grad_norm,
        attn_g,
        up_g,
        down_g,
        vec_g,
        attn_new,
        up_new,
        down_new,
        vec_new,
        attn_m_new,
        up_m_new,
        down_m_new,
        vec_m_new,
        attn_v_new,
        up_v_new,
        down_v_new,
        vec_v_new,
    )


def solution(mesh):
    stretch = P("rows", "seq", None)
    stacked = P(None, "rows", None)
    split_rows = P("rows", None)
    weights = (stacked, split_rows, split_rows, P())
    return jax.shard_map(
        body,
        mesh=mesh,
        in_specs=(stretch, stretch, split_rows) + weights * 3,
        out_specs=(stretch, stretch, P()) + weights * 4,
        check_vma=False,
    )
```

```python
import functools
import math

import jax
import jax.numpy as jnp
from jax import lax
from jax.experimental import pallas as pl
from jax.experimental.pallas import tpu as pltpu
from jax.sharding import PartitionSpec as P

HEADS = 8
HEAD_DIM = 64
PAIRS = HEADS // 2
LANES = 2 * HEAD_DIM
STEP = 5

EPS_NORM = 1e-05
EPS_DEN = 1e-06
CLIP_AT = 1.0
BETA_ONE = 0.5
BETA_TWO = 0.5
RATE_MAT = 0.02
RATE_VEC = 0.1
DECAY_MAT = 0.1
EPS_ADAM = 1e-08

F32 = jnp.float32
FORWARD = 0.01
LIMIT = 56 * 1024 * 1024


def cost(us):
    return pl.CostEstimate(flops=int(us * 1e9), bytes_accessed=int(us * 2e6), transcendentals=0)


class Given:
    def __init__(self, ref, copies):
        self.ref, self.copies, self.shape = ref, copies, ref.shape

    def __getitem__(self, at):
        while self.copies:
            self.copies.pop(0).wait()
        return self.ref[at]


class Made:
    def __init__(self, ref, out, send):
        self.ref, self.out, self.send, self.shape = ref, out, send, out.shape
        self.sent = False

    def __getitem__(self, at):
        return self.ref[at]

    def __setitem__(self, at, value):
        self.ref[at] = value

    def flush(self, at=slice(None)):
        self.sent = True
        self.send(self.ref.at[at], self.out.at[at])


class Built:
    def __init__(self, shape, arrays, plan, copies=1):
        self.shape, self.arrays, self.plan, self.copies = shape, arrays, plan, copies


def whole(info, refs, buffer):
    return [(refs[0], buffer)]


def built(operand):
    return operand if isinstance(operand, Built) else Built(operand.shape, [operand], whole)


def call(us, kernel, outs, info, ins, scratch=(), direct=(), smem=(), sends=None):
    ins = [built(a) for a in ins]
    arrays = []
    for a in ins:
        arrays += [b for b in a.arrays if not any(b is c for c in arrays)]
    places = [[next(i for i, c in enumerate(arrays) if c is b) for b in a.arrays] for a in ins]
    sends = sends or len(outs)

    def body(info_ref, *refs):
        refs = list(refs)

        def take(count):
            part, refs[:] = refs[:count], refs[count:]
            return part

        extra, given, results = take(len(smem)), take(len(arrays)), take(len(outs))
        in_buffers, out_buffers = take(len(ins)), take(len(outs) - len(direct))
        in_sems, out_sems = refs.pop(), refs.pop()
        operands, count = [], 0
        for a, at, buffer in zip(ins, places, in_buffers):
            copies = []
            for source, target in a.plan(info_ref, [given[i] for i in at], buffer):
                copies.append(pltpu.make_async_copy(source, target, in_sems.at[count]))
                copies[-1].start()
                count += 1
            operands.append(Given(buffer, copies))
        sent = []

        def send(source, target):
            sent.append(pltpu.make_async_copy(source, target, out_sems.at[len(sent)]))
            sent[-1].start()

        made = [
            Made(None if i in direct else out_buffers.pop(0), out, send)
            for i, out in enumerate(results)
        ]
        kernel(info_ref, *extra, *operands, *made, *refs)
        for operand in operands:
            for copy in operand.copies:
                copy.wait()
        for i, out in enumerate(made):
            if i not in direct and not out.sent:
                out.flush()
        for copy in sent:
            copy.wait()
        assert len(sent) == sends, (len(sent), sends)

    hbm = pl.BlockSpec(memory_space=pltpu.HBM)
    smem_spec = pl.BlockSpec(memory_space=pltpu.SMEM)
    buffers = [pltpu.VMEM(a.shape, F32) for a in ins]
    buffers += [pltpu.VMEM(a.shape, F32) for i, a in enumerate(outs) if i not in direct]
    sems = [pltpu.SemaphoreType.DMA((count,)) for count in (sends, max(1, sum(a.copies for a in ins)))]
    return pl.pallas_call(
        body,
        out_shape=outs,
        in_specs=[smem_spec] * (1 + len(smem)) + [hbm] * len(arrays),
        out_specs=[hbm] * len(outs),
        scratch_shapes=buffers + list(scratch) + sems,
        compiler_params=pltpu.CompilerParams(vmem_limit_bytes=LIMIT),
        cost_estimate=cost(us),
    )(info, *smem, *arrays)


def shaped(shape):
    return jax.ShapeDtypeStruct(tuple(shape), F32)


def row_blocks(pieces, lead=None, top=0):
    def plan(info, refs, buffer):
        rows = buffer.shape[0] // len(refs)
        for j, ref in enumerate(refs):
            at = pl.ds(pl.multiple_of((info[0] ^ j) * rows, rows), rows)
            source = ref if lead is None else ref.at[lead]
            yield source.at[top : top + rows, :], buffer.at[at, :]

    width = pieces[0].shape[-1]
    return Built((width, width), pieces, plan, len(pieces))


def split(a):
    high = a.astype(jnp.bfloat16)
    return high, (a - high.astype(F32)).astype(jnp.bfloat16)


def dot(a, b, ca=1, cb=0):
    dims = (((ca,), (cb,)), ((), ()))
    a, b = (x if isinstance(x, tuple) else split(x) for x in (a, b))

    def one(p, q):
        return lax.dot_general(p, q, dims, preferred_element_type=F32)

    return one(a[0], b[0]) + (one(a[0], b[1]) + one(a[1], b[0]))


def phi(u):
    return jnp.where(u > 0, u + 1.0, jnp.exp(jnp.minimum(u, 0.0)))


def normalise(x):
    centred = x - jnp.mean(x, axis=1, keepdims=True)
    scale = lax.rsqrt(jnp.mean(centred * centred, axis=1, keepdims=True) + EPS_NORM)
    return centred * scale, scale


def normalise_back(grad, unit, scale):
    inner = jnp.mean(grad * unit, axis=1, keepdims=True)
    return scale * (grad - jnp.mean(grad, axis=1, keepdims=True) - unit * inner)


def first_head(shape):
    return lax.broadcasted_iota(jnp.int32, shape, len(shape) - 1) % LANES < HEAD_DIM


def pick(value, head):
    return jnp.where(first_head(value.shape) == (head == 0), value, 0.0)


def lower(shape):
    return lax.broadcasted_iota(jnp.int32, shape, 1) < HEAD_DIM


def halves_of(pair):
    high, low = split(pair)
    turned = pltpu.roll(pair, HEAD_DIM, 1)
    return (high, low), split(turned)


def streamed(plain, turned, tail=None):
    first = lower(plain[0].shape)
    out = []
    for head in range(2):
        here, there = (plain, turned) if head == 0 else (turned, plain)
        end = here[0]
        if tail is not None:
            end = jnp.where(first, end, tail[1 - head])
        out.append(jnp.concatenate([jnp.where(first, here[0], there[1]), end], axis=1))
    return out


def held(plain, turned, fill):
    first = lower(plain[0].shape)
    out = []
    for head in range(2):
        here, there = (plain, turned) if head == 0 else (turned, plain)
        end = jnp.where(first, here[1], jnp.full_like(here[1], fill))
        out.append(jnp.concatenate([jnp.where(first, here[0], there[0]), end], axis=1))
    return out


def alternate(high, low):
    lanes = lax.broadcasted_iota(jnp.int32, high.shape, 1)
    return jnp.where(lanes % HEAD_DIM < HEAD_DIM // 2, high, low)


def once(a, b):
    return lax.dot_general(a, b, (((1,), (1,)), ((), ())), preferred_element_type=F32)


def beside(halves, head, fill=0.0):
    high, low = halves
    mine = lower(high.shape) == (head == 0)
    return jnp.concatenate(
        [jnp.where(mine, high, jnp.full_like(high, fill)), jnp.where(mine, low, jnp.zeros_like(low))],
        axis=1,
    )


def mixed(scores, pair):
    high, low = split(scores)
    count = high.shape[0]
    both = lax.dot_general(
        jnp.concatenate([high, low], axis=0), pair, (((1,), (0,)), ((), ())), preferred_element_type=F32
    )
    both = both[:count] + both[count:]
    return both[:, :LANES] + both[:, LANES:]


def block_ones():
    shape = (LANES, LANES)
    rows, lanes = (lax.broadcasted_iota(jnp.int32, shape, d) // HEAD_DIM for d in (0, 1))
    return jnp.where(rows == lanes, 1.0, 0.0)


class Info:
    def __init__(self, ref, length, slots):
        self.ref, self.length, self.slots = ref, length, slots
        self.me, self.place, self.first = ref[0], ref[1], ref[2]

    def starts(self, r):
        return [self.ref[3 + r * self.slots + i] for i in range(self.slots)]

    def document(self, r, position):
        return sum(jnp.where(a <= position, 1, 0) for a in self.starts(r))

    def causal(self, r, flipped=False):
        shape = (self.length, self.length)
        t = self.first + lax.broadcasted_iota(jnp.int32, shape, 1 if flipped else 0)
        s = self.first + lax.broadcasted_iota(jnp.int32, shape, 0 if flipped else 1)
        ok = t >= s
        for a in self.starts(r):
            ok = ok & ((t < a) | (s >= a))
        return jnp.where(ok, 1.0, 0.0)

    def from_before(self, r, width):
        t = self.first + lax.broadcasted_iota(jnp.int32, (self.length, width), 0)
        ok = t >= 0
        for a in self.starts(r):
            ok = ok & ((a < self.first) | (t < a))
        return jnp.where(ok, 1.0, 0.0)

    def to_after(self, r, width):
        s = self.first + lax.broadcasted_iota(jnp.int32, (self.length, width), 0)
        last = self.first + self.length - 1
        ok = s >= 0
        for a in self.starts(r):
            ok = ok & ((s >= a) | (a > last))
        return jnp.where(ok, 1.0, 0.0)


def state_blocks(ref, r, p):
    at = (r * PAIRS + p) * HEAD_DIM
    packed = ref[at : at + HEAD_DIM, :]
    sums = ref.shape[0] // (HEAD_DIM + 1) * HEAD_DIM + r * PAIRS + p
    return (
        jnp.concatenate([pick(packed, 0), pick(packed, 1)], axis=0),
        ref[sums : sums + 1, :],
    )


def store_state(ref, r, p, full, key_sum):
    at = (r * PAIRS + p) * HEAD_DIM
    top, bottom = full[:HEAD_DIM], full[HEAD_DIM:]
    ref[at : at + HEAD_DIM, :] = jnp.where(first_head(top.shape), top, bottom)
    sums = ref.shape[0] // (HEAD_DIM + 1) * HEAD_DIM + r * PAIRS + p
    ref[sums : sums + 1, :] = key_sum


def pair_slices(length, r, p):
    return slice(r * length, (r + 1) * length), slice(p * LANES, (p + 1) * LANES)


def row_slice(length, r):
    return slice(r * length, (r + 1) * length)


def keys_kernel(slots, rows, ref, x, vec, wk, wv, wq, normed, k, v, state, query, key, value):
    length = x.shape[0] // rows
    info = Info(ref, length, slots)
    unit, _ = normalise(x[...])
    normed[...] = unit * vec[0:1, :] + vec[1:2, :]
    normed.flush()
    k[...] = phi(dot(normed[...], wk[...]))
    v[...] = dot(normed[...], wv[...])
    k.flush()
    v.flush()
    for r in range(rows):
        kept = info.to_after(r, LANES)
        for p in range(PAIRS):
            at = pair_slices(length, r, p)
            masked = k[at] * kept
            store_state(state, r, p, dot(masked, v[at], 0, 0), jnp.sum(masked, axis=0, keepdims=True))
    state.flush()
    for source, out in ((wq, query), (wk, key), (wv, value)):
        source[0:8, 0:128]
        out.send(source.ref, out.out)


def queries_kernel(slots, rows, ref, normed, wq, k, v, q, numer, denom):
    length = k.shape[0] // rows
    info = Info(ref, length, slots)
    q[...] = phi(dot(normed[...], wq[...]))
    q.flush()
    for r in range(rows):
        mask = info.causal(r)
        for p in range(PAIRS):
            at = pair_slices(length, r, p)
            lefts, rights = streamed(*halves_of(q[at])), held(*halves_of(k[at]), 0.0)
            values = split(v[at])
            sums = [
                mixed(once(lefts[head], rights[head]) * mask, beside(values, head, 1.0))
                for head in range(2)
            ]
            first = lower(sums[0].shape)
            numer[at] = jnp.where(first, *sums)
            denom[at] = pltpu.roll(jnp.where(first, sums[1], sums[0]), HEAD_DIM, 1)
        numer.flush(row_slice(length, r))
        denom.flush(row_slice(length, r))


def attend_kernel(slots, rows, bit, ref, prefix, other, q, numer, denom, wo, x, vec, att, inv, resid, second, state, out_w):
    length = x.shape[0] // rows
    info = Info(ref, length, slots)
    enter(info, bit, False, prefix, other, state)
    state.flush()
    ones = block_ones()
    for r in range(rows):
        use = info.from_before(r, LANES)
        for p in range(PAIRS):
            at = pair_slices(length, r, p)
            block, key_sum = state_blocks(state, r, p)
            q_pair = q[at] * use
            top = numer[at] + dot(q_pair, block)
            under = denom[at] + dot(q_pair * key_sum, ones) + EPS_DEN
            inverse = 1.0 / under
            inv[at] = inverse
            att[at] = top * inverse
        att.flush(row_slice(length, r))
        inv.flush(row_slice(length, r))
    resid[...] = x[...] + dot(att[...], wo[...])
    resid.flush()
    unit, _ = normalise(resid[...])
    second[...] = unit * vec[2:3, :] + vec[3:4, :]
    second.flush()
    out_w.send(wo.ref, out_w.out)


def slopes_kernel(info, dout, *refs):
    *downs, out = refs
    grad_out = split(dout[...])
    for i, down in enumerate(downs):
        share = down.shape[0]
        here = (slice(None), slice(i * share, (i + 1) * share))
        out[here] = dot(grad_out, down[...], 1, 1)
        out.flush(here)


def feed_kernel(js, last, info, second, dout, *refs):
    count = len(js)
    blocks, refs = [refs[2 * i : 2 * i + 2] for i in range(count)], refs[2 * count :]
    if last:
        vec, back_in, resid, g, e, dresid, small, dbias, back = refs
        grad_out = split(dout[...])
    else:
        vec, g, e, back, dbias = refs
    share = dbias.shape[1] // count
    inputs = split(second[...])
    for i, (up, down) in enumerate(blocks):
        column, width = (info[0] ^ js[i]) * share, vec.shape[1]
        lanes = pl.ds(pl.multiple_of(lax.rem(column, width), share), share)
        bias = vec[pl.ds(5 + lax.div(column, width), 1), lanes]
        here = (slice(None), slice(i * share, (i + 1) * share))
        weights = split(up[...])
        h = dot(inputs, weights) + bias
        cdf = 0.5 * (1.0 + lax.erf(h * math.sqrt(0.5)))
        g[here] = h * cdf
        g.flush(here)
        slope = cdf + h * (jnp.exp(-0.5 * h * h) * (1.0 / math.sqrt(2.0 * math.pi)))
        grad = (dot(grad_out, down[...], 1, 1) if last else down[...]) * slope
        e[here] = grad
        e.flush(here)
        dbias[here] = jnp.sum(grad, axis=0, keepdims=True)
        part = dot(grad, weights, 1, 1)
        if i == 0:
            back[...] = back_in[...] + part if last else part
        else:
            back[...] = back[...] + part
    if last:
        unit, scale = normalise(resid[...])
        grad_second = back[...]
        small[...] = jnp.zeros(small.shape, F32)
        small[2:3, :] = jnp.sum(grad_second * unit, axis=0, keepdims=True)
        small[3:4, :] = jnp.sum(grad_second, axis=0, keepdims=True)
        small[4:5, :] = jnp.sum(dout[...], axis=0, keepdims=True)
        dresid[...] = dout[...] + normalise_back(grad_second * vec[2:3, :], unit, scale)


def out_kernel(count, info, vec, resid, *refs):
    *refs, out = refs
    tops, downs = refs[:count], list(refs[count:])
    out[...] = resid[...] + vec[4:5, :]
    for g in tops:
        share = downs[0].shape[0]
        for i in range(g.shape[1] // share):
            out[...] = out[...] + dot(g[:, i * share : (i + 1) * share], downs.pop(0)[...])


def state_rows(ref):
    sums = ref.shape[0] // (HEAD_DIM + 1)
    for r in range(sums // PAIRS):
        yield r, slice(r * PAIRS * HEAD_DIM, (r + 1) * PAIRS * HEAD_DIM)
        yield r, slice(sums * HEAD_DIM + r * PAIRS, sums * HEAD_DIM + (r + 1) * PAIRS)


def enter(info, bit, reverse, prefix, other, out):
    for r, at in state_rows(out):
        out[at, :] = prefix[at, :] + other[at, :] * meet(info, bit, reverse, r)[2]


def joins_kernel(slots, length, stretches, ref, out):
    info = Info(ref, length, slots)
    bits = [1 << i for i in range(stretches.bit_length() - 1)][:-1]
    for i, (reverse, bit) in enumerate((reverse, bit) for reverse in (False, True) for bit in bits):
        for r, at in state_rows(out.ref.at[0]):
            mine_late, same, reaches = meet(info, bit, reverse, r)
            values = (jnp.where(mine_late, 1.0, same), jnp.where(mine_late, same, 1.0), reaches)
            for part, value in enumerate(values):
                out[3 * i + part, at, :] = jnp.full((at.stop - at.start, LANES), value)


def meet(info, bit, reverse, r):
    place, length = info.place, info.length
    bits = place & bit
    mine_late = (bits == 0) if reverse else (bits != 0)
    low = place & ~(bit - 1)
    shift = -1 if reverse else bit * length - 1
    here, there = (info.document(r, group * length + shift) for group in (low, low ^ bit))
    own = info.document(r, info.first + (length - 1 if reverse else -1))
    return mine_late, jnp.where(here == there, 1.0, 0.0), jnp.where(mine_late & (there == own), 1.0, 0.0)


def attend_back_kernel(slots, rows, ref, dresid, wo, inv, att, q, dn, dd, state):
    length = q.shape[0] // rows
    info = Info(ref, length, slots)
    grad = dot(dresid[...], wo[...], 1, 1)
    ones = block_ones()
    for r in range(rows):
        use = info.from_before(r, LANES)
        for p in range(PAIRS):
            at = pair_slices(length, r, p)
            grad_pair = grad[at]
            over = grad_pair * inv[at]
            dn[at] = over
            under = -dot(grad_pair * att[at], ones) * inv[at]
            dd[at] = under
            q_pair = q[at] * use
            full = dot(q_pair, over, 0, 0)
            store_state(state, r, p, full, jnp.sum(q_pair * under, axis=0, keepdims=True))
        dn.flush(row_slice(length, r))
        dd.flush(row_slice(length, r))


def put_block(info, stretches, group, odd, stretch, source, theirs, mine, lanes=slice(None), early=False):
    rows = source.shape[0]
    groups = theirs.shape[0] // (stretches * rows)
    core = (info[0] & 1) ^ odd
    mask = group + groups * (info[1] ^ stretch)
    at = Plan(early, groups, stretches).position(mask, core) * rows
    out = theirs if odd else mine
    out.send(source, out.out.at[pl.ds(pl.multiple_of(at, rows), rows), lanes])


def down_grads_kernel(n, stretches, info, dout, *refs):
    *refs, theirs, mine, full = refs
    grad_out = dout[...]
    rows = full.shape[1] // stretches
    j = 0
    for g in refs:
        share = full.shape[1]
        for i in range(g.shape[1] // share):
            full[j] = dot(g[:, i * share : (i + 1) * share], grad_out, 0, 0)
            for s in range(stretches):
                source = full.at[j, s * rows : (s + 1) * rows, :]
                put_block(info, stretches, j // 2, j & 1, s, source, theirs, mine, early=True)
            j += 1


def up_grads_kernel(n, stretches, info, second, *refs):
    *refs, theirs, mine, full = refs
    share, width = full.shape[2], theirs.shape[1]
    tall = full.shape[1] // n
    rows = tall * (n * share // width) // stretches
    j = 0
    for e in refs:
        for i in range(e.shape[1] // share):
            full[j] = dot(second[...], e[:, i * share : (i + 1) * share], 0, 0)
            column = (info[0] ^ j) * share
            lanes = pl.ds(pl.multiple_of(lax.rem(column, width), share), share)
            for m in range(n):
                for b in range(tall // rows):
                    start = (info[0] ^ m) * tall + b * rows
                    source = full.at[j, pl.ds(pl.multiple_of(start, rows), rows), :]
                    stretch = lax.div(column, width) * (tall // rows) + b
                    put_block(info, stretches, m // 2, m & 1, stretch, source, theirs, mine, lanes, True)
            j += 1


def deal(info, n, stretches, full, theirs, mine, slot, slots=4):
    tall = full.shape[0] // n
    rows = tall * slots // stretches
    for m in range(n):
        for i in range(tall // rows):
            start = (info[0] ^ m) * tall + i * rows
            source = full.at[pl.ds(pl.multiple_of(start, rows), rows), :]
            stretch = slot * (tall // rows) + i
            put_block(info, stretches, m // 2, m & 1, stretch, source, theirs, mine)


def local_back_kernel(slots, rows, ref, q, k, v, dn, dd, state, dk, dv, dq):
    length = q.shape[0] // rows
    info = Info(ref, length, slots)
    for r in range(rows):
        use = info.from_before(r, LANES)
        mask, flipped = info.causal(r), info.causal(r, True)
        for p in range(PAIRS):
            at = pair_slices(length, r, p)
            q_pair, k_pair, v_pair, dn_pair, dd_pair = q[at], k[at], v[at], dn[at], dd[at]
            block, key_sum = state_blocks(state, r, p)
            grad_q = use * (dot(dn_pair, block, 1, 1) + dd_pair * key_sum)
            grad_k = grad_v = 0.0
            q_halves, k_halves, v_halves, dn_halves = (
                halves_of(a) for a in (q_pair, k_pair, v_pair, dn_pair)
            )
            tops = streamed(*dn_halves, [alternate(*h) for h in halves_of(dd_pair)])
            values = held(*v_halves, 2.0 / HEAD_DIM)
            queries, keys = streamed(*q_halves), held(*k_halves, 0.0)
            for head in range(2):
                grad_scores = once(tops[head], values[head]) * mask
                grad_q = grad_q + mixed(grad_scores, beside(k_halves[0], head))
                grad_flipped = once(values[head], tops[head]) * flipped
                grad_k = grad_k + mixed(grad_flipped, beside(q_halves[0], head))
                scores_flipped = once(keys[head], queries[head]) * flipped
                grad_v = grad_v + mixed(scores_flipped, beside(dn_halves[0], head))
            dq[at] = grad_q * jnp.minimum(q_pair, 1.0)
            dk[at] = grad_k
            dv[at] = grad_v
        for out in (dk, dv, dq):
            out.flush(row_slice(length, r))


def keys_back_kernel(n, slots, rows, bit, stretches, ref, prefix, other, v, k, dk, dv, normed, dq, att, dresid, theirs, mine, gk, gv, full, state):
    length = k.shape[0] // rows
    info = Info(ref, length, slots)
    enter(info, bit, True, prefix, other, state)
    for r in range(rows):
        kept = info.to_after(r, LANES)
        for p in range(PAIRS):
            at = pair_slices(length, r, p)
            block, key_sum = state_blocks(state, r, p)
            k_pair = k[at]
            grad_k = dk[at] + kept * (dot(v[at], block, 1, 1) + key_sum)
            gk[at] = grad_k * jnp.minimum(k_pair, 1.0)
            gv[at] = dv[at] + dot(k_pair * kept, block)
    inputs = split(normed[...])
    for slot, grad in ((1, gk), (2, gv), (0, dq)):
        full[slot] = dot(inputs, grad[...], 0, 0)
        deal(ref, n, stretches, full.at[slot], theirs, mine, slot)
    full[3] = dot(att[...], dresid[...], 0, 0)
    deal(ref, n, stretches, full.at[3], theirs, mine, 3)


def input_back_kernel(n, info, gk, wk, gv, wv, dq, wq, x, dresid, vec, small_in, *refs):
    *biases, dx, small = refs
    grad = dot(gk[...], wk[...], 1, 1) + dot(gv[...], wv[...], 1, 1) + dot(dq[...], wq[...], 1, 1)
    unit, scale = normalise(x[...])
    dx[...] = dresid[...] + normalise_back(grad * vec[0:1, :], unit, scale)
    dx.flush()
    small[...] = small_in[...]
    small[0:1, :] = jnp.sum(grad * unit, axis=0, keepdims=True)
    small[1:2, :] = jnp.sum(grad, axis=0, keepdims=True)
    width = small.shape[1]
    share = sum(ref.shape[1] for ref in biases) // n
    j = 0
    for bias in biases:
        for i in range(bias.shape[1] // share):
            column = (info[0] ^ j) * share
            lanes = pl.ds(pl.multiple_of(lax.rem(column, width), share), share)
            small[pl.ds(5 + lax.div(column, width), 1), lanes] = bias[0:1, i * share : (i + 1) * share]
            j += 1


def adamw_step(weight, gradient, first_m, second_m, factor, rate, decay):
    clipped = gradient * factor
    new_m = BETA_ONE * first_m + (1.0 - BETA_ONE) * clipped
    new_v = BETA_TWO * second_m + (1.0 - BETA_TWO) * clipped * clipped
    moved = new_m / (1.0 - BETA_ONE**STEP) / (jnp.sqrt(new_v / (1.0 - BETA_TWO**STEP)) + EPS_ADAM)
    return (clipped, weight - rate * (moved + decay * weight), new_m, new_v)


def update_kernel(plan, heights, info, part_square, small, vec, vec_m, vec_v, *refs):
    count = len(heights)
    halves, arrays, refs = refs[: 2 * count], refs[2 * count : 5 * count], refs[5 * count :]
    outs, (norm, *small_outs), refs = refs[: 4 * count], refs[4 * count : 4 * count + 5], refs[4 * count + 5 :]
    buffers, results, in_sems, out_sems = refs
    stretches = plan.stretches
    spots = []
    for k in range(stretches):
        stretch = info[1] ^ by_core(info, [order[k] for order in plan.order])
        for i, rows in enumerate(heights):
            tall, wide = arrays[3 * i].shape[0], halves[0].shape[1]
            start = stretch * rows
            spot = (
                pl.ds(pl.multiple_of(lax.rem(start, tall), rows), rows),
                pl.ds(pl.multiple_of(lax.div(start, tall) * wide, wide), wide),
            )
            spots.append(spot)
            top = k % (stretches // 2) * rows
            half = halves[2 * i + k // (stretches // 2)]
            sources = [half.at[top : top + rows, :]] + [a.at[spot] for a in arrays[3 * i : 3 * i + 3]]
            for part, source in enumerate(sources):
                pltpu.make_async_copy(source, buffers.at[k, i, part], in_sems.at[k]).start()
    gradient = small[0 : vec.shape[0], :]
    square = jnp.sum(jnp.sum(gradient * gradient, axis=1, keepdims=True), axis=0, keepdims=True)
    length = jnp.sqrt(square + jnp.full((1, 1), part_square[0]))
    norm[...] = length
    factor = jnp.minimum(1.0, CLIP_AT / (length + 1e-06))
    new = adamw_step(vec[...], gradient, vec_m[...], vec_v[...], factor, RATE_VEC, 0.0)
    for out, result in zip(small_outs, new):
        out[...] = result
    for k in range(stretches):
        pltpu.make_async_copy(buffers.at[k], buffers.at[k], in_sems.at[k]).wait()
        for i in range(count):
            gradient, weight, first_m, second_m = (buffers[k, i, part] for part in range(4))
            new = adamw_step(weight, gradient, first_m, second_m, factor, RATE_MAT, DECAY_MAT)
            for part, result in enumerate(new):
                results[k, i, part] = result
                out = outs[4 * i + part].at[spots[k * count + i]]
                pltpu.make_async_copy(results.at[k, i, part], out, out_sems.at[k]).start()
    for k in range(stretches):
        pltpu.make_async_copy(results.at[k], results.at[k], out_sems.at[k]).wait()


def swap(part, axis, bit):
    return lax.ppermute(part, axis, [(i, i ^ bit) for i in range(lax.axis_size(axis))])


def bits_of(axis):
    return [1 << i for i in range(lax.axis_size(axis).bit_length() - 1)]


def after(part, *others):
    return lax.optimization_barrier((part, *others))[0]


class Plan:
    def __init__(self, early=False, groups=None, stretches=None):
        self.groups = groups or lax.axis_size("rows") // 2
        self.stretches = stretches or lax.axis_size("seq")
        ys = [1 << i for i in range(self.groups.bit_length() - 1)]
        seq = [self.groups << i for i in range(self.stretches.bit_length() - 1)]
        xs, zs = seq[: len(ys)], seq[len(ys) :]
        first, second = [], []
        for y, x in zip(ys, xs):
            first += [y, x]
            second += [x, y]
        pairs = list(zip(first, second))
        alone = [(z, z) for z in zs]
        self.down = pairs[:1] + alone[:1] + pairs[1:] + alone[1:] if early else pairs + alone
        zs, xs = zs[::-1], xs[::-1]
        self.up = [(z, z) for z in zs[:-1]] + list(zip(zs[-1:] + xs, xs + zs[-1:]))
        order = [[0], [0]]
        for bits in self.up:
            order = [o + [m ^ bit for m in o] for o, bit in zip(order, bits)]
        self.order = [[m // self.groups for m in o] for o in order]

    def position(self, mask, core):
        steps = len(self.down)
        places = [
            sum(jnp.where(mask & bits[c], 1 << (steps - 1 - t), 0) for t, bits in enumerate(self.down))
            for c in (0, 1)
        ]
        return jnp.where(core == 0, *places)

    def move(self, part, bits):
        rows = 2 * self.groups
        pairs = []
        for i in range(rows * self.stretches):
            bit = bits[i & 1]
            flip = bit * 2 if bit < self.groups else bit // self.groups * rows
            pairs.append((i, i ^ flip))
        return lax.ppermute(part, ("seq", "rows"), pairs)


def by_core(info, pair):
    return jnp.where(info[0] & 1 == 0, pair[0], pair[1])


class Chunk:
    def __init__(self, theirs, mine, early=False):
        self.plan, self.step, self.result = Plan(early), 0, None
        self.extra, self.carried = None, False
        self.got, self.held = swap(theirs, "rows", 1), mine

    def advance(self):
        plan, step, held, got = self.plan, self.step, self.held, self.got
        self.step += 1
        if self.carried:
            count = self.extra.shape[0]
            self.extra = self.extra + got[-count:]
            got, self.carried = got[:-count], False
        if step < len(plan.down):
            half = held.shape[0] // 2
            send = held[half:] + got[half:]
            self.held = held[:half] + got[:half]
            if self.extra is not None:
                send, self.carried = jnp.concatenate([send, self.extra], axis=0), True
            self.got = plan.move(send, plan.down[step])
            return
        rise = step - len(plan.down)
        if rise < len(plan.up):
            self.held = held + got if rise == 0 else jnp.concatenate([held, got], axis=0)
            self.got = plan.move(self.held, plan.up[rise])
            return
        self.result = [held, got]


def meeting(arrays, chunks=()):
    out = lax.optimization_barrier((*arrays, *(chunk.got for chunk in chunks)))
    for chunk, got in zip(chunks, out[len(arrays) :]):
        chunk.got = got
    return out[: len(arrays)]


def meeting_of(arrays, parts):
    out = lax.optimization_barrier((*arrays, *parts.values()))
    return out[: len(arrays)], dict(zip(parts, out[len(arrays) :]))


def update(info, part_square, small, vectors, chunks):
    plan = Plan()
    halves = [half for gathered, *_ in chunks for half in gathered]
    arrays = [a for _, *part in chunks for a in part]
    heights = [half.shape[0] // (plan.stretches // 2) for half in halves[::2]]
    assert len(set(heights)) == 1
    buffer = pltpu.VMEM((plan.stretches, len(chunks), 4, heights[0], halves[0].shape[1]), F32)
    outs = [shaped(chunk[1].shape) for chunk in chunks for _ in range(4)]
    outs += [shaped((1, 1))] + [shaped(vectors[0].shape)] * 4
    smem, vmem = (pl.BlockSpec(memory_space=space) for space in (pltpu.SMEM, pltpu.VMEM))
    hbm = pl.BlockSpec(memory_space=pltpu.HBM)
    return pl.pallas_call(
        functools.partial(update_kernel, plan, heights),
        out_shape=outs,
        in_specs=[smem] * 2 + [vmem] * 4 + [hbm] * (len(halves) + len(arrays)),
        out_specs=[hbm] * (4 * len(chunks)) + [vmem] * 5,
        scratch_shapes=[buffer] * 2 + [pltpu.SemaphoreType.DMA((plan.stretches,))] * 2,
        compiler_params=pltpu.CompilerParams(vmem_limit_bytes=LIMIT),
        cost_estimate=cost(10),
    )(info, part_square, small, *vectors, *halves, *arrays)


def body(
    activations,
    cotangent,
    seq_starts,
    attn_weight,
    up_weight,
    down_weight,
    vectors,
    attn_m,
    up_m,
    down_m,
    vec_m,
    attn_v,
    up_v,
    down_v,
    vec_v,
):
    rows, length, width = activations.shape
    n = lax.axis_size("rows")
    hidden = up_weight.shape[1]
    tokens = rows * length
    slots = seq_starts.shape[1]
    block = width // n
    me, place = lax.axis_index("rows"), lax.axis_index("seq")
    first = place * length
    info = jnp.concatenate(
        [jnp.stack([me, place, first]).astype(jnp.int32), seq_starts.reshape(-1)]
    )

    x = activations.reshape(tokens, width)
    dout = cotangent.reshape(tokens, width)
    state_shape = shaped((rows * PAIRS * (HEAD_DIM + 1), LANES))
    act = shaped((tokens, width))

    seq_bits = bits_of("seq")
    joins, bit = len(seq_bits) - 1, seq_bits[-1]
    stretches = lax.axis_size("seq")

    def start(total, i):
        return swap(total, "seq", seq_bits[i])

    def joined(total, other, prefix, reverse, i):
        own, its, entered = (factors[3 * (joins * reverse + i) + part] for part in range(3))
        prefix = [part + other * entered for part in prefix] or [other * entered]
        return prefix[0], total * own + other * its

    factors = call(
        FORWARD * 2.5,
        functools.partial(joins_kernel, slots, length, stretches),
        [shaped((6 * joins,) + state_shape.shape)],
        info,
        [],
    )[0]
    share = hidden // n
    distances = range(1, n // 2)

    def columns(distance):
        chip = (me // 2) ^ distance
        part = lax.dynamic_slice_in_dim(up_weight, chip * 2 * share, 2 * share, 1)
        return jnp.split(part, 2 * share // width, axis=1)

    first = {d: swap(attn_weight[:3], "rows", 2 * d) for d in distances}
    near_parts = {d: jnp.concatenate([attn_weight[3]] + columns(d), axis=0) for d in distances}
    near = {d: swap(part, "rows", 2 * d) for d, part in near_parts.items()}
    far_parts = {
        d: jnp.concatenate([c for e in distances for c in columns(d ^ e)] + [down_weight], axis=0)
        for d in distances
    }

    def both_cores(chips):
        got = {2 * d: part for d, part in chips.items()}
        got.update({2 * d + 1: swap(part, "rows", 1) for d, part in chips.items()})
        return got

    def ordered(pieces):
        return [pieces[j] for j in sorted(pieces)]

    qkv = both_cores(
        {0: attn_weight[:3], **{d: after(first[d], factors, near_parts[d]) for d in distances}}
    )
    own = both_cores({0: attn_weight[3]}), both_cores({0: up_weight}), both_cores({0: down_weight})
    own_out, own_up, own_down = (ordered(pieces) for pieces in own)
    qkv = ordered(qkv)
    square_shape = shaped((width, width))
    normed, k, v, state, wq, wk, wv = call(
        FORWARD * 5.6,
        functools.partial(keys_kernel, slots, rows),
        [act, act, act, state_shape] + [square_shape] * 3,
        info,
        [x, vectors] + [row_blocks(qkv, lead) for lead in (1, 2, 0)],
        direct=(4, 5, 6),
    )
    other = start(state, 0)
    far = {d: swap(after(part, state), "rows", 2 * d) for d, part in far_parts.items()}
    other, own_out[1], own_up[1], own_down[1] = meeting([other, own_out[1], own_up[1], own_down[1]])
    prefix, total = joined(state, other, [], False, 0)
    other = start(total, 1)
    slopes = call(
        FORWARD * 4,
        slopes_kernel,
        [shaped((tokens, 2 * share))],
        info,
        [after(dout, total)] + own_down,
        sends=2,
    )[0]
    (other, slopes), near = meeting_of([other, slopes], near)
    for i in range(1, joins):
        prefix, total = joined(total, other, [prefix], False, i)
        other = start(total, i + 1)
    near_all = ordered(both_cores({d: after(part, total) for d, part in near.items()}))
    q, numer, denom = call(
        FORWARD * 8.5,
        functools.partial(queries_kernel, slots, rows),
        [act, act, act],
        info,
        [after(normed, total), wq, k, v],
        sends=1 + 2 * rows,
    )
    other, *near_all = meeting([other, *near_all, q])[:-1]
    att, inv, resid, second, state_in, wo = call(
        FORWARD * 6.3,
        functools.partial(attend_kernel, slots, rows, bit),
        [act, act, act, act, state_shape, square_shape],
        info,
        [prefix, other, q, numer, denom, row_blocks(own_out + near_all), x, vectors],
        direct=(5,),
        sends=4 + 2 * rows,
    )

    small_shape = shaped((16, width))

    def up_columns(j, parts, top):
        def plan(info, refs, buffer):
            mine = (info[0] ^ j) * share
            column = ((info[0] ^ j) & 1) * share
            for m, ref in enumerate(refs):
                at = pl.ds(pl.multiple_of((info[0] ^ m) * block, block), block)
                if m < 2:
                    source = ref.at[:, pl.ds(pl.multiple_of(mine, share), share)]
                else:
                    row = top + lax.div(column, width) * block
                    lanes = pl.ds(pl.multiple_of(lax.rem(column, width), share), share)
                    source = ref.at[pl.ds(pl.multiple_of(row, block), block), lanes]
                yield source, buffer.at[at, :]

        return Built((width, share), own_up + parts, plan, n)

    def bottom(part):
        top = part.shape[0] - share
        return Built((share, width), [part], lambda info, refs, buffer: [(refs[0].at[top:, :], buffer)])

    def feed(js, blocks, extra, outs, scratch=()):
        wide = shaped((tokens, share * len(js)))
        return call(
            FORWARD * 11.5,
            functools.partial(feed_kernel, js, bool(extra)),
            [wide, wide] + outs + [shaped((1, share * len(js)))],
            info,
            [second, dout] + blocks + [vectors] + extra,
            scratch=scratch,
            sends=2 * len(js) + len(outs) + 1,
        )

    js = list(range(2))
    own_slopes = [
        Built(
            (tokens, share),
            [slopes],
            lambda info, refs, buffer, j=j: [(refs[0].at[:, j * share : (j + 1) * share], buffer)],
        )
        for j in js
    ]
    blocks = [a for j in js for a in (up_columns(j, near_all, block), own_slopes[j])]
    (second,), far = meeting_of([second], far)
    far_all = ordered(both_cores(far))
    g0, e0, back, dbias0 = feed(js, blocks, [], [act])
    js = list(range(2, n))
    tops = [(j // 2 - 1) * (2 * share // width) * block for j in js]
    far_down = [bottom(part) for part in far_all]
    blocks = [a for j, top, down in zip(js, tops, far_down) for a in (up_columns(j, far_all, top), down)]
    g1, e1, dresid, small, dbias1 = feed(
        js, blocks, [back, resid], [act, small_shape], [pltpu.VMEM((tokens, width), F32)]
    )

    dn, dd, dstate = call(
        5.4,
        functools.partial(attend_back_kernel, slots, rows),
        [act, act, state_shape],
        info,
        [dresid, wo, inv, att, q],
        sends=1 + 2 * rows,
    )

    half_rows = shaped((n // 2 * share, width))

    def gradients(kernel, common, tops):
        full = (n, width, share) if kernel is up_grads_kernel else (n, share, width)
        return call(
            7,
            functools.partial(kernel, n, stretches),
            [half_rows] * 2,
            info,
            [common] + tops,
            direct=(0, 1),
            scratch=[pltpu.VMEM(full, F32)],
            sends=n * n * stretches * width // hidden if kernel is up_grads_kernel else n * stretches,
        )

    other = start(dstate, 0)
    down_theirs, down_mine = gradients(down_grads_kernel, after(dout, dstate), [g0, g1])
    other, down_theirs, down_mine = meeting([other, down_theirs, down_mine])

    dprefix, dtotal = joined(dstate, other, [], True, 0)
    other = start(dtotal, 1)
    chunk_down = Chunk(down_theirs, down_mine, early=True)
    up_theirs, up_mine = gradients(up_grads_kernel, after(second, dtotal), [e0, e1])
    chunks = [chunk_down]
    other, up_theirs, up_mine, dprefix = meeting([other, up_theirs, up_mine, dprefix], chunks)

    for i in range(1, joins):
        dprefix, dtotal = joined(dtotal, other, [dprefix], True, i)
        other = start(dtotal, i + 1)
        if i + 1 < joins:
            (other,) = meeting([other], chunks)
    chunk_down.advance()
    chunk_up = Chunk(up_theirs, up_mine, early=True)
    dk, dv, dq = call(
        13,
        functools.partial(local_back_kernel, slots, rows),
        [act, act, act],
        info,
        [after(q, dtotal), k, v, dn, dd, state_in],
        sends=3 * rows,
    )
    chunks = [chunk_down, chunk_up]
    dk, other, dprefix = meeting([dk, other, dprefix], chunks)

    chunk_down.advance()
    chunk_up.advance()
    four = shaped((n // 2 * 4 * block, width))
    attn_theirs, attn_mine, gk, gv = call(
        6,
        functools.partial(keys_back_kernel, n, slots, rows, bit, stretches),
        [four, four, act, act],
        info,
        [dprefix, other, v, k, dk, dv, normed, dq, att, dresid],
        direct=(0, 1),
        scratch=[pltpu.VMEM((4, width, width), F32), pltpu.VMEM(state_shape.shape, F32)],
        sends=n * stretches + 2,
    )
    attn_theirs, attn_mine, gk = meeting([attn_theirs, attn_mine, gk], chunks)

    chunk_attn = Chunk(attn_theirs, attn_mine)
    chunk_down.advance()
    chunk_up.advance()
    meeting([], [chunk_attn])
    chunk_attn.advance()
    dx, small = call(
        6,
        functools.partial(input_back_kernel, n),
        [act, small_shape],
        info,
        [after(gk, chunk_attn.held), wk, gv, wv, dq, wq, x, dresid, vectors, small, dbias0, dbias1],
    )
    chunks = [chunk_attn, chunk_down, chunk_up]
    small, late = meeting([small, resid])

    small = small + swap(small, "rows", 1)
    chunk_attn.extra = small
    late = after(late, dx)
    for chunk in chunks:
        chunk.advance()
    out = call(
        7,
        functools.partial(out_kernel, 2),
        [act],
        info,
        [vectors, late, g0, g1] + own_down + far_down,
    )[0]
    plan = chunk_attn.plan
    while chunks:
        if chunk_attn.step == 4:
            (out,) = meeting([out], chunks[1:])
        for chunk in chunks:
            chunk.advance()
        chunks = [chunk for chunk in chunks if chunk.result is None]
        if chunk_attn.step == len(plan.down) + 1:
            small = chunk_attn.extra
            for bits in plan.down[:1]:
                small = small + plan.move(small, bits)
    square = sum(jnp.sum(a * a) for chunk in (chunk_up, chunk_down, chunk_attn) for a in chunk.result)
    for bit in bits_of("rows"):
        square = square + swap(square, "rows", bit)

    def flat(a):
        return a.reshape(-1, width)

    results = update(
        info,
        square.reshape(1),
        small,
        [vectors, vec_m, vec_v],
        [
            (chunk_up.result, up_weight, up_m, up_v),
            (chunk_down.result, down_weight, down_m, down_v),
            (chunk_attn.result, flat(attn_weight), flat(attn_m), flat(attn_v)),
        ],
    )
    up_g, up_new, up_m_new, up_v_new = results[:4]
    down_g, down_new, down_m_new, down_v_new = results[4:8]
    attn_g, attn_new, attn_m_new, attn_v_new = (
        a.reshape(attn_weight.shape) for a in results[8:12]
    )
    grad_norm = results[12].reshape(())
    vec_g, vec_new, vec_m_new, vec_v_new = results[13:]
    return (
        out.reshape(activations.shape),
        dx.reshape(activations.shape),
        grad_norm,
        attn_g,
        up_g,
        down_g,
        vec_g,
        attn_new,
        up_new,
        down_new,
        vec_new,
        attn_m_new,
        up_m_new,
        down_m_new,
        vec_m_new,
        attn_v_new,
        up_v_new,
        down_v_new,
        vec_v_new,
    )


def solution(mesh):
    stretch = P("rows", "seq", None)
    stacked = P(None, "rows", None)
    split_rows = P("rows", None)
    weights = (stacked, split_rows, split_rows, P())
    return jax.shard_map(
        body,
        mesh=mesh,
        in_specs=(stretch, stretch, split_rows) + weights * 3,
        out_specs=(stretch, stretch, P()) + weights * 4,
        check_vma=False,
    )
```

```python
import functools
import math

import jax
import jax.numpy as jnp
from jax import lax
from jax.experimental import pallas as pl
from jax.experimental.pallas import tpu as pltpu
from jax.sharding import PartitionSpec as P

HEADS = 8
HEAD_DIM = 64
PAIRS = HEADS // 2
LANES = 2 * HEAD_DIM
STEP = 5

EPS_NORM = 1e-05
EPS_DEN = 1e-06
CLIP_AT = 1.0
BETA_ONE = 0.5
BETA_TWO = 0.5
RATE_MAT = 0.02
RATE_VEC = 0.1
DECAY_MAT = 0.1
EPS_ADAM = 1e-08

F32 = jnp.float32
FORWARD = 0.01
DOWN, UP = 1, 1
LIMIT = 56 * 1024 * 1024
ALL = 63 * 1024 * 1024


def cost(us):
    return pl.CostEstimate(flops=int(us * 1e9), bytes_accessed=int(us * 2e6), transcendentals=0)


class Given:
    def __init__(self, ref, copies):
        self.ref, self.copies, self.shape = ref, copies, ref.shape

    def __getitem__(self, at):
        while self.copies:
            self.copies.pop(0).wait()
        return self.ref[at]


class Made:
    def __init__(self, ref, out, send):
        self.ref, self.out, self.send, self.shape = ref, out, send, out.shape
        self.sent = False

    def __getitem__(self, at):
        return self.ref[at]

    def __setitem__(self, at, value):
        self.ref[at] = value

    def flush(self, at=slice(None)):
        self.sent = True
        self.send(self.ref.at[at], self.out.at[at])


class Built:
    def __init__(self, shape, arrays, plan, copies=1):
        self.shape, self.arrays, self.plan, self.copies = shape, arrays, plan, copies


def whole(info, refs, buffer):
    return [(refs[0], buffer)]


def built(operand):
    return operand if isinstance(operand, Built) else Built(operand.shape, [operand], whole)


def call(us, kernel, outs, info, ins, scratch=(), direct=(), smem=(), sends=None, limit=LIMIT):
    ins = [built(a) for a in ins]
    arrays = []
    for a in ins:
        arrays += [b for b in a.arrays if not any(b is c for c in arrays)]
    places = [[next(i for i, c in enumerate(arrays) if c is b) for b in a.arrays] for a in ins]
    sends = sends or len(outs)

    def body(info_ref, *refs):
        refs = list(refs)

        def take(count):
            part, refs[:] = refs[:count], refs[count:]
            return part

        extra, given, results = take(len(smem)), take(len(arrays)), take(len(outs))
        in_buffers, out_buffers = take(len(ins)), take(len(outs) - len(direct))
        in_sems, out_sems = refs.pop(), refs.pop()
        operands, count = [], 0
        for a, at, buffer in zip(ins, places, in_buffers):
            copies = []
            for source, target in a.plan(info_ref, [given[i] for i in at], buffer):
                copies.append(pltpu.make_async_copy(source, target, in_sems.at[count]))
                copies[-1].start()
                count += 1
            operands.append(Given(buffer, copies))
        sent = []

        def send(source, target):
            sent.append(pltpu.make_async_copy(source, target, out_sems.at[len(sent)]))
            sent[-1].start()

        made = [
            Made(None if i in direct else out_buffers.pop(0), out, send)
            for i, out in enumerate(results)
        ]
        kernel(info_ref, *extra, *operands, *made, *refs)
        for operand in operands:
            for copy in operand.copies:
                copy.wait()
        for i, out in enumerate(made):
            if i not in direct and not out.sent:
                out.flush()
        for copy in sent:
            copy.wait()
        assert len(sent) == sends, (len(sent), sends)

    hbm = pl.BlockSpec(memory_space=pltpu.HBM)
    smem_spec = pl.BlockSpec(memory_space=pltpu.SMEM)
    buffers = [pltpu.VMEM(a.shape, F32) for a in ins]
    buffers += [pltpu.VMEM(a.shape, F32) for i, a in enumerate(outs) if i not in direct]
    sems = [pltpu.SemaphoreType.DMA((count,)) for count in (sends, max(1, sum(a.copies for a in ins)))]
    return pl.pallas_call(
        body,
        out_shape=outs,
        in_specs=[smem_spec] * (1 + len(smem)) + [hbm] * len(arrays),
        out_specs=[hbm] * len(outs),
        scratch_shapes=buffers + list(scratch) + sems,
        compiler_params=pltpu.CompilerParams(vmem_limit_bytes=limit),
        cost_estimate=cost(us),
    )(info, *smem, *arrays)


def shaped(shape):
    return jax.ShapeDtypeStruct(tuple(shape), F32)


def row_blocks(pieces, lead=None, top=0):
    def plan(info, refs, buffer):
        rows = buffer.shape[0] // len(refs)
        for j, ref in enumerate(refs):
            at = pl.ds(pl.multiple_of((info[0] ^ j) * rows, rows), rows)
            source = ref if lead is None else ref.at[lead]
            yield source.at[top : top + rows, :], buffer.at[at, :]

    width = pieces[0].shape[-1]
    return Built((width, width), pieces, plan, len(pieces))


def split(a):
    high = a.astype(jnp.bfloat16)
    return high, (a - high.astype(F32)).astype(jnp.bfloat16)


def dot(a, b, ca=1, cb=0):
    dims = (((ca,), (cb,)), ((), ()))
    a, b = (x if isinstance(x, tuple) else split(x) for x in (a, b))

    def one(p, q):
        return lax.dot_general(p, q, dims, preferred_element_type=F32)

    return one(a[0], b[0]) + (one(a[0], b[1]) + one(a[1], b[0]))


def phi(u):
    return jnp.where(u > 0, u + 1.0, jnp.exp(jnp.minimum(u, 0.0)))


def normalise(x):
    centred = x - jnp.mean(x, axis=1, keepdims=True)
    scale = lax.rsqrt(jnp.mean(centred * centred, axis=1, keepdims=True) + EPS_NORM)
    return centred * scale, scale


def normalise_back(grad, unit, scale):
    inner = jnp.mean(grad * unit, axis=1, keepdims=True)
    return scale * (grad - jnp.mean(grad, axis=1, keepdims=True) - unit * inner)


def first_head(shape):
    return lax.broadcasted_iota(jnp.int32, shape, len(shape) - 1) % LANES < HEAD_DIM


def pick(value, head):
    return jnp.where(first_head(value.shape) == (head == 0), value, 0.0)


def lower(shape):
    return lax.broadcasted_iota(jnp.int32, shape, 1) < HEAD_DIM


def halves_of(pair):
    high, low = split(pair)
    turned = pltpu.roll(pair, HEAD_DIM, 1)
    return (high, low), split(turned)


def streamed(plain, turned, tail=None):
    first = lower(plain[0].shape)
    out = []
    for head in range(2):
        here, there = (plain, turned) if head == 0 else (turned, plain)
        end = here[0]
        if tail is not None:
            end = jnp.where(first, end, tail[1 - head])
        out.append(jnp.concatenate([jnp.where(first, here[0], there[1]), end], axis=1))
    return out


def held(plain, turned, fill):
    first = lower(plain[0].shape)
    out = []
    for head in range(2):
        here, there = (plain, turned) if head == 0 else (turned, plain)
        end = jnp.where(first, here[1], jnp.full_like(here[1], fill))
        out.append(jnp.concatenate([jnp.where(first, here[0], there[0]), end], axis=1))
    return out


def alternate(high, low):
    lanes = lax.broadcasted_iota(jnp.int32, high.shape, 1)
    return jnp.where(lanes % HEAD_DIM < HEAD_DIM // 2, high, low)


def once(a, b):
    return lax.dot_general(a, b, (((1,), (1,)), ((), ())), preferred_element_type=F32)


def beside(halves, head, fill=0.0):
    high, low = halves
    mine = lower(high.shape) == (head == 0)
    return jnp.concatenate(
        [jnp.where(mine, high, jnp.full_like(high, fill)), jnp.where(mine, low, jnp.zeros_like(low))],
        axis=1,
    )


def mixed(scores, pair):
    high, low = split(scores)
    count = high.shape[0]
    both = lax.dot_general(
        jnp.concatenate([high, low], axis=0), pair, (((1,), (0,)), ((), ())), preferred_element_type=F32
    )
    both = both[:count] + both[count:]
    return both[:, :LANES] + both[:, LANES:]


def block_ones():
    shape = (LANES, LANES)
    rows, lanes = (lax.broadcasted_iota(jnp.int32, shape, d) // HEAD_DIM for d in (0, 1))
    return jnp.where(rows == lanes, 1.0, 0.0)


class Info:
    def __init__(self, ref, length, slots):
        self.ref, self.length, self.slots = ref, length, slots
        self.me, self.place, self.first = ref[0], ref[1], ref[2]

    def starts(self, r):
        return [self.ref[3 + r * self.slots + i] for i in range(self.slots)]

    def document(self, r, position):
        return sum(jnp.where(a <= position, 1, 0) for a in self.starts(r))

    def causal(self, r, flipped=False):
        shape = (self.length, self.length)
        t = self.first + lax.broadcasted_iota(jnp.int32, shape, 1 if flipped else 0)
        s = self.first + lax.broadcasted_iota(jnp.int32, shape, 0 if flipped else 1)
        ok = t >= s
        for a in self.starts(r):
            ok = ok & ((t < a) | (s >= a))
        return jnp.where(ok, 1.0, 0.0)

    def from_before(self, r, width):
        t = self.first + lax.broadcasted_iota(jnp.int32, (self.length, width), 0)
        ok = t >= 0
        for a in self.starts(r):
            ok = ok & ((a < self.first) | (t < a))
        return jnp.where(ok, 1.0, 0.0)

    def to_after(self, r, width):
        s = self.first + lax.broadcasted_iota(jnp.int32, (self.length, width), 0)
        last = self.first + self.length - 1
        ok = s >= 0
        for a in self.starts(r):
            ok = ok & ((s >= a) | (a > last))
        return jnp.where(ok, 1.0, 0.0)


def state_blocks(ref, r, p):
    at = (r * PAIRS + p) * HEAD_DIM
    packed = ref[at : at + HEAD_DIM, :]
    sums = ref.shape[0] // (HEAD_DIM + 1) * HEAD_DIM + r * PAIRS + p
    return (
        jnp.concatenate([pick(packed, 0), pick(packed, 1)], axis=0),
        ref[sums : sums + 1, :],
    )


def store_state(ref, r, p, full, key_sum):
    at = (r * PAIRS + p) * HEAD_DIM
    top, bottom = full[:HEAD_DIM], full[HEAD_DIM:]
    ref[at : at + HEAD_DIM, :] = jnp.where(first_head(top.shape), top, bottom)
    sums = ref.shape[0] // (HEAD_DIM + 1) * HEAD_DIM + r * PAIRS + p
    ref[sums : sums + 1, :] = key_sum


def pair_slices(length, r, p):
    return slice(r * length, (r + 1) * length), slice(p * LANES, (p + 1) * LANES)


def row_slice(length, r):
    return slice(r * length, (r + 1) * length)


def keys_kernel(slots, rows, ref, x, vec, wk, wv, normed, k, v, state):
    length = x.shape[0] // rows
    info = Info(ref, length, slots)
    unit, _ = normalise(x[...])
    normed[...] = unit * vec[0:1, :] + vec[1:2, :]
    normed.flush()
    k[...] = phi(dot(normed[...], wk[...]))
    v[...] = dot(normed[...], wv[...])
    k.flush()
    v.flush()
    for r in range(rows):
        kept = info.to_after(r, LANES)
        for p in range(PAIRS):
            at = pair_slices(length, r, p)
            masked = k[at] * kept
            store_state(state, r, p, dot(masked, v[at], 0, 0), jnp.sum(masked, axis=0, keepdims=True))
    state.flush()


def queries_kernel(slots, rows, ref, normed, wq, k, v, q, numer, denom):
    length = k.shape[0] // rows
    info = Info(ref, length, slots)
    q[...] = phi(dot(normed[...], wq[...]))
    q.flush()
    for r in range(rows):
        mask = info.causal(r)
        for p in range(PAIRS):
            at = pair_slices(length, r, p)
            lefts, rights = streamed(*halves_of(q[at])), held(*halves_of(k[at]), 0.0)
            values = split(v[at])
            sums = [
                mixed(once(lefts[head], rights[head]) * mask, beside(values, head, 1.0))
                for head in range(2)
            ]
            first = lower(sums[0].shape)
            numer[at] = jnp.where(first, *sums)
            denom[at] = pltpu.roll(jnp.where(first, sums[1], sums[0]), HEAD_DIM, 1)
        numer.flush(row_slice(length, r))
        denom.flush(row_slice(length, r))


def attend_kernel(slots, rows, bit, ref, prefix, other, q, numer, denom, wo, x, vec, att, inv, resid, second, state):
    length = x.shape[0] // rows
    info = Info(ref, length, slots)
    enter(info, bit, False, prefix, other, state)
    state.flush()
    ones = block_ones()
    for r in range(rows):
        use = info.from_before(r, LANES)
        for p in range(PAIRS):
            at = pair_slices(length, r, p)
            block, key_sum = state_blocks(state, r, p)
            q_pair = q[at] * use
            top = numer[at] + dot(q_pair, block)
            under = denom[at] + dot(q_pair * key_sum, ones) + EPS_DEN
            inverse = 1.0 / under
            inv[at] = inverse
            att[at] = top * inverse
        att.flush(row_slice(length, r))
        inv.flush(row_slice(length, r))
    resid[...] = x[...] + dot(att[...], wo[...])
    resid.flush()
    unit, _ = normalise(resid[...])
    second[...] = unit * vec[2:3, :] + vec[3:4, :]
    second.flush()


def slopes_kernel(info, dout, *refs):
    *downs, out = refs
    grad_out = split(dout[...])
    for i, down in enumerate(downs):
        share = down.shape[0]
        here = (slice(None), slice(i * share, (i + 1) * share))
        out[here] = dot(grad_out, down[...], 1, 1)
        out.flush(here)


def feed_kernel(js, last, info, second, dout, *refs):
    count = len(js)
    blocks, refs = [refs[2 * i : 2 * i + 2] for i in range(count)], refs[2 * count :]
    if last:
        vec, back_in, resid, g, e, dresid, small, dbias, back = refs
        grad_out = split(dout[...])
    else:
        vec, g, e, back, dbias = refs
    share = dbias.shape[1] // count
    inputs = split(second[...])
    for i, (up, down) in enumerate(blocks):
        column, width = (info[0] ^ js[i]) * share, vec.shape[1]
        lanes = pl.ds(pl.multiple_of(lax.rem(column, width), share), share)
        bias = vec[pl.ds(5 + lax.div(column, width), 1), lanes]
        here = (slice(None), slice(i * share, (i + 1) * share))
        weights = split(up[...])
        h = dot(inputs, weights) + bias
        cdf = 0.5 * (1.0 + lax.erf(h * math.sqrt(0.5)))
        g[here] = h * cdf
        g.flush(here)
        slope = cdf + h * (jnp.exp(-0.5 * h * h) * (1.0 / math.sqrt(2.0 * math.pi)))
        grad = (dot(grad_out, down[...], 1, 1) if last else down[...]) * slope
        e[here] = grad
        e.flush(here)
        dbias[here] = jnp.sum(grad, axis=0, keepdims=True)
        part = dot(grad, weights, 1, 1)
        if i == 0:
            back[...] = back_in[...] + part if last else part
        else:
            back[...] = back[...] + part
    if last:
        unit, scale = normalise(resid[...])
        grad_second = back[...]
        small[...] = jnp.zeros(small.shape, F32)
        small[2:3, :] = jnp.sum(grad_second * unit, axis=0, keepdims=True)
        small[3:4, :] = jnp.sum(grad_second, axis=0, keepdims=True)
        small[4:5, :] = jnp.sum(dout[...], axis=0, keepdims=True)
        dresid[...] = dout[...] + normalise_back(grad_second * vec[2:3, :], unit, scale)


def turn_kernel(js, slots, rows, info, *refs):
    ins, outs, back = refs[: 2 * len(js) + 9], refs[2 * len(js) + 9 : -1], refs[-1]
    feed_kernel(js, True, info, *ins[:-4], *outs[:5], back)
    outs[2].flush()
    attend_back_kernel(slots, rows, info, outs[2], *ins[-4:], *outs[5:])


def out_kernel(count, info, vec, resid, *refs):
    *refs, out = refs
    tops, downs = refs[:count], list(refs[count:])
    out[...] = resid[...] + vec[4:5, :]
    for g in tops:
        share = downs[0].shape[0]
        for i in range(g.shape[1] // share):
            out[...] = out[...] + dot(g[:, i * share : (i + 1) * share], downs.pop(0)[...])


def state_rows(ref):
    sums = ref.shape[0] // (HEAD_DIM + 1)
    for r in range(sums // PAIRS):
        yield r, slice(r * PAIRS * HEAD_DIM, (r + 1) * PAIRS * HEAD_DIM)
        yield r, slice(sums * HEAD_DIM + r * PAIRS, sums * HEAD_DIM + (r + 1) * PAIRS)


def enter(info, bit, reverse, prefix, other, out):
    for r, at in state_rows(out):
        out[at, :] = prefix[at, :] + other[at, :] * meet(info, bit, reverse, r)[2]


def joins_kernel(slots, length, stretches, ref, out):
    info = Info(ref, length, slots)
    bits = [1 << i for i in range(stretches.bit_length() - 1)][:-1]
    for i, (reverse, bit) in enumerate((reverse, bit) for reverse in (False, True) for bit in bits):
        for r, at in state_rows(out.ref.at[0]):
            mine_late, same, reaches = meet(info, bit, reverse, r)
            values = (jnp.where(mine_late, 1.0, same), jnp.where(mine_late, same, 1.0), reaches)
            for part, value in enumerate(values):
                out[3 * i + part, at, :] = jnp.full((at.stop - at.start, LANES), value)


def meet(info, bit, reverse, r):
    place, length = info.place, info.length
    bits = place & bit
    mine_late = (bits == 0) if reverse else (bits != 0)
    low = place & ~(bit - 1)
    shift = -1 if reverse else bit * length - 1
    here, there = (info.document(r, group * length + shift) for group in (low, low ^ bit))
    own = info.document(r, info.first + (length - 1 if reverse else -1))
    return mine_late, jnp.where(here == there, 1.0, 0.0), jnp.where(mine_late & (there == own), 1.0, 0.0)


def attend_back_kernel(slots, rows, ref, dresid, wo, inv, att, q, dn, dd, state):
    length = q.shape[0] // rows
    info = Info(ref, length, slots)
    grad = dot(dresid[...], wo[...], 1, 1)
    ones = block_ones()
    for r in range(rows):
        use = info.from_before(r, LANES)
        for p in range(PAIRS):
            at = pair_slices(length, r, p)
            grad_pair = grad[at]
            over = grad_pair * inv[at]
            dn[at] = over
            under = -dot(grad_pair * att[at], ones) * inv[at]
            dd[at] = under
            q_pair = q[at] * use
            full = dot(q_pair, over, 0, 0)
            store_state(state, r, p, full, jnp.sum(q_pair * under, axis=0, keepdims=True))
        dn.flush(row_slice(length, r))
        dd.flush(row_slice(length, r))


def put_block(info, stretches, group, odd, stretch, source, theirs, mine, lanes=slice(None), early=False):
    rows = source.shape[0]
    groups = theirs.shape[0] // (stretches * rows)
    core = (info[0] & 1) ^ odd
    mask = group + groups * (info[1] ^ stretch)
    at = Plan(early, groups, stretches).position(mask, core) * rows
    out = theirs if odd else mine
    out.send(source, out.out.at[pl.ds(pl.multiple_of(at, rows), rows), lanes])


def down_grads_kernel(n, stretches, info, dout, *refs):
    *refs, theirs, mine, full = refs
    grad_out = dout[...]
    rows = full.shape[1] // stretches
    j = 0
    for g in refs:
        share = full.shape[1]
        for i in range(g.shape[1] // share):
            full[j] = dot(g[:, i * share : (i + 1) * share], grad_out, 0, 0)
            for s in range(stretches):
                source = full.at[j, s * rows : (s + 1) * rows, :]
                put_block(info, stretches, j // 2, j & 1, s, source, theirs, mine, early=DOWN)
            j += 1


def up_grads_kernel(n, stretches, info, second, *refs):
    *refs, theirs, mine, full = refs
    share, width = full.shape[2], theirs.shape[1]
    tall = full.shape[1] // n
    rows = tall * (n * share // width) // stretches
    j = 0
    for e in refs:
        for i in range(e.shape[1] // share):
            full[j] = dot(second[...], e[:, i * share : (i + 1) * share], 0, 0)
            column = (info[0] ^ j) * share
            lanes = pl.ds(pl.multiple_of(lax.rem(column, width), share), share)
            for m in range(n):
                for b in range(tall // rows):
                    start = (info[0] ^ m) * tall + b * rows
                    source = full.at[j, pl.ds(pl.multiple_of(start, rows), rows), :]
                    stretch = lax.div(column, width) * (tall // rows) + b
                    put_block(info, stretches, m // 2, m & 1, stretch, source, theirs, mine, lanes, UP)
            j += 1


def deal(info, n, stretches, full, theirs, mine, slot, slots=4):
    tall = full.shape[0] // n
    rows = tall * slots // stretches
    for m in range(n):
        for i in range(tall // rows):
            start = (info[0] ^ m) * tall + i * rows
            source = full.at[pl.ds(pl.multiple_of(start, rows), rows), :]
            stretch = slot * (tall // rows) + i
            put_block(info, stretches, m // 2, m & 1, stretch, source, theirs, mine)


def local_back_kernel(slots, rows, ref, q, k, v, dn, dd, state, dk, dv, dq):
    length = q.shape[0] // rows
    info = Info(ref, length, slots)
    for r in range(rows):
        use = info.from_before(r, LANES)
        mask, flipped = info.causal(r), info.causal(r, True)
        for p in range(PAIRS):
            at = pair_slices(length, r, p)
            q_pair, k_pair, v_pair, dn_pair, dd_pair = q[at], k[at], v[at], dn[at], dd[at]
            block, key_sum = state_blocks(state, r, p)
            grad_q = use * (dot(dn_pair, block, 1, 1) + dd_pair * key_sum)
            grad_k = grad_v = 0.0
            q_halves, k_halves, v_halves, dn_halves = (
                halves_of(a) for a in (q_pair, k_pair, v_pair, dn_pair)
            )
            tops = streamed(*dn_halves, [alternate(*h) for h in halves_of(dd_pair)])
            values = held(*v_halves, 2.0 / HEAD_DIM)
            queries, keys = streamed(*q_halves), held(*k_halves, 0.0)
            for head in range(2):
                grad_scores = once(tops[head], values[head]) * mask
                grad_q = grad_q + mixed(grad_scores, beside(k_halves[0], head))
                grad_flipped = once(values[head], tops[head]) * flipped
                grad_k = grad_k + mixed(grad_flipped, beside(q_halves[0], head))
                scores_flipped = once(keys[head], queries[head]) * flipped
                grad_v = grad_v + mixed(scores_flipped, beside(dn_halves[0], head))
            dq[at] = grad_q * jnp.minimum(q_pair, 1.0)
            dk[at] = grad_k
            dv[at] = grad_v
        for out in (dk, dv, dq):
            out.flush(row_slice(length, r))


def keys_back_kernel(n, slots, rows, bit, stretches, ref, prefix, other, v, k, dk, dv, normed, dq, att, dresid, theirs, mine, gk, gv, full, state):
    length = k.shape[0] // rows
    info = Info(ref, length, slots)
    enter(info, bit, True, prefix, other, state)
    for r in range(rows):
        kept = info.to_after(r, LANES)
        for p in range(PAIRS):
            at = pair_slices(length, r, p)
            block, key_sum = state_blocks(state, r, p)
            k_pair = k[at]
            grad_k = dk[at] + kept * (dot(v[at], block, 1, 1) + key_sum)
            gk[at] = grad_k * jnp.minimum(k_pair, 1.0)
            gv[at] = dv[at] + dot(k_pair * kept, block)
    inputs = split(normed[...])
    for slot, grad in ((1, gk), (2, gv), (0, dq)):
        full[slot] = dot(inputs, grad[...], 0, 0)
        deal(ref, n, stretches, full.at[slot], theirs, mine, slot)
    full[3] = dot(att[...], dresid[...], 0, 0)
    deal(ref, n, stretches, full.at[3], theirs, mine, 3)


def input_back_kernel(n, info, gk, wk, gv, wv, dq, wq, x, dresid, vec, small_in, *refs):
    *biases, dx, small = refs
    grad = dot(gk[...], wk[...], 1, 1) + dot(gv[...], wv[...], 1, 1) + dot(dq[...], wq[...], 1, 1)
    unit, scale = normalise(x[...])
    dx[...] = dresid[...] + normalise_back(grad * vec[0:1, :], unit, scale)
    dx.flush()
    small[...] = small_in[...]
    small[0:1, :] = jnp.sum(grad * unit, axis=0, keepdims=True)
    small[1:2, :] = jnp.sum(grad, axis=0, keepdims=True)
    width = small.shape[1]
    share = sum(ref.shape[1] for ref in biases) // n
    j = 0
    for bias in biases:
        for i in range(bias.shape[1] // share):
            column = (info[0] ^ j) * share
            lanes = pl.ds(pl.multiple_of(lax.rem(column, width), share), share)
            small[pl.ds(5 + lax.div(column, width), 1), lanes] = bias[0:1, i * share : (i + 1) * share]
            j += 1


def adamw_step(weight, gradient, first_m, second_m, factor, rate, decay):
    clipped = gradient * factor
    new_m = BETA_ONE * first_m + (1.0 - BETA_ONE) * clipped
    new_v = BETA_TWO * second_m + (1.0 - BETA_TWO) * clipped * clipped
    moved = new_m / (1.0 - BETA_ONE**STEP) / (jnp.sqrt(new_v / (1.0 - BETA_TWO**STEP)) + EPS_ADAM)
    return (clipped, weight - rate * (moved + decay * weight), new_m, new_v)


def update_kernel(plan, heights, info, part_square, small, vec, vec_m, vec_v, *refs):
    count = len(heights)
    halves, arrays, refs = refs[: 2 * count], refs[2 * count : 5 * count], refs[5 * count :]
    outs, (norm, *small_outs), refs = refs[: 4 * count], refs[4 * count : 4 * count + 5], refs[4 * count + 5 :]
    buffers, results, in_sems, out_sems = refs
    stretches = plan.stretches
    spots = []
    for k in range(stretches):
        stretch = info[1] ^ by_core(info, [order[k] for order in plan.order])
        for i, rows in enumerate(heights):
            tall, wide = arrays[3 * i].shape[0], halves[0].shape[1]
            start = stretch * rows
            spot = (
                pl.ds(pl.multiple_of(lax.rem(start, tall), rows), rows),
                pl.ds(pl.multiple_of(lax.div(start, tall) * wide, wide), wide),
            )
            spots.append(spot)
            top = k % (stretches // 2) * rows
            half = halves[2 * i + k // (stretches // 2)]
            sources = [half.at[top : top + rows, :]] + [a.at[spot] for a in arrays[3 * i : 3 * i + 3]]
            for part, source in enumerate(sources):
                pltpu.make_async_copy(source, buffers.at[k, i, part], in_sems.at[k]).start()
    gradient = small[0 : vec.shape[0], :]
    square = jnp.sum(jnp.sum(gradient * gradient, axis=1, keepdims=True), axis=0, keepdims=True)
    length = jnp.sqrt(square + jnp.full((1, 1), part_square[0]))
    norm[...] = length
    factor = jnp.minimum(1.0, CLIP_AT / (length + 1e-06))
    new = adamw_step(vec[...], gradient, vec_m[...], vec_v[...], factor, RATE_VEC, 0.0)
    for out, result in zip(small_outs, new):
        out[...] = result
    for k in range(stretches):
        pltpu.make_async_copy(buffers.at[k], buffers.at[k], in_sems.at[k]).wait()
        for i in range(count):
            gradient, weight, first_m, second_m = (buffers[k, i, part] for part in range(4))
            new = adamw_step(weight, gradient, first_m, second_m, factor, RATE_MAT, DECAY_MAT)
            for part, result in enumerate(new):
                results[k, i, part] = result
                out = outs[4 * i + part].at[spots[k * count + i]]
                pltpu.make_async_copy(results.at[k, i, part], out, out_sems.at[k]).start()
    for k in range(stretches):
        pltpu.make_async_copy(results.at[k], results.at[k], out_sems.at[k]).wait()


def swap(part, axis, bit):
    return lax.ppermute(part, axis, [(i, i ^ bit) for i in range(lax.axis_size(axis))])


def bits_of(axis):
    return [1 << i for i in range(lax.axis_size(axis).bit_length() - 1)]


def after(part, *others):
    return lax.optimization_barrier((part, *others))[0]


class Plan:
    def __init__(self, early=False, groups=None, stretches=None):
        self.groups = groups or lax.axis_size("rows") // 2
        self.stretches = stretches or lax.axis_size("seq")
        ys = [1 << i for i in range(self.groups.bit_length() - 1)]
        seq = [self.groups << i for i in range(self.stretches.bit_length() - 1)]
        xs, zs = seq[: len(ys)], seq[len(ys) :]
        first, second = [], []
        for y, x in zip(ys, xs):
            first += [y, x]
            second += [x, y]
        pairs = list(zip(first, second))
        alone = [(z, z) for z in zs]
        if early == 1:
            self.down = pairs[:1] + alone[:1] + pairs[1:] + alone[1:]
        elif early == 2:
            both, rest = [(y, y) for y in ys], list(zip(zs[:1] + xs, xs + zs[:1]))
            self.down = both + rest + alone[1:]
        else:
            self.down = pairs + alone
        zs, xs = zs[::-1], xs[::-1]
        self.up = [(z, z) for z in zs[:-1]] + list(zip(zs[-1:] + xs, xs + zs[-1:]))
        order = [[0], [0]]
        for bits in self.up:
            order = [o + [m ^ bit for m in o] for o, bit in zip(order, bits)]
        self.order = [[m // self.groups for m in o] for o in order]

    def position(self, mask, core):
        steps = len(self.down)
        places = [
            sum(jnp.where(mask & bits[c], 1 << (steps - 1 - t), 0) for t, bits in enumerate(self.down))
            for c in (0, 1)
        ]
        return jnp.where(core == 0, *places)

    def move(self, part, bits):
        rows = 2 * self.groups
        pairs = []
        for i in range(rows * self.stretches):
            bit = bits[i & 1]
            flip = bit * 2 if bit < self.groups else bit // self.groups * rows
            pairs.append((i, i ^ flip))
        return lax.ppermute(part, ("seq", "rows"), pairs)


def by_core(info, pair):
    return jnp.where(info[0] & 1 == 0, pair[0], pair[1])


class Chunk:
    def __init__(self, theirs, mine, early=False):
        self.plan, self.step, self.result = Plan(early), 0, None
        self.extra, self.carried = None, False
        self.got, self.held = swap(theirs, "rows", 1), mine

    def advance(self):
        plan, step, held, got = self.plan, self.step, self.held, self.got
        self.step += 1
        if self.carried:
            count = self.extra.shape[0]
            self.extra = self.extra + got[-count:]
            got, self.carried = got[:-count], False
        if step < len(plan.down):
            half = held.shape[0] // 2
            send = held[half:] + got[half:]
            self.held = held[:half] + got[:half]
            if self.extra is not None:
                send, self.carried = jnp.concatenate([send, self.extra], axis=0), True
            self.got = plan.move(send, plan.down[step])
            return
        rise = step - len(plan.down)
        if rise < len(plan.up):
            self.held = held + got if rise == 0 else jnp.concatenate([held, got], axis=0)
            self.got = plan.move(self.held, plan.up[rise])
            return
        self.result = [held, got]


def meeting(arrays, chunks=()):
    out = lax.optimization_barrier((*arrays, *(chunk.got for chunk in chunks)))
    for chunk, got in zip(chunks, out[len(arrays) :]):
        chunk.got = got
    return out[: len(arrays)]


def meeting_of(arrays, parts):
    out = lax.optimization_barrier((*arrays, *parts.values()))
    return out[: len(arrays)], dict(zip(parts, out[len(arrays) :]))


def update(info, part_square, small, vectors, chunks):
    plan = Plan()
    halves = [half for gathered, *_ in chunks for half in gathered]
    arrays = [a for _, *part in chunks for a in part]
    heights = [half.shape[0] // (plan.stretches // 2) for half in halves[::2]]
    assert len(set(heights)) == 1
    buffer = pltpu.VMEM((plan.stretches, len(chunks), 4, heights[0], halves[0].shape[1]), F32)
    outs = [shaped(chunk[1].shape) for chunk in chunks for _ in range(4)]
    outs += [shaped((1, 1))] + [shaped(vectors[0].shape)] * 4
    smem, vmem = (pl.BlockSpec(memory_space=space) for space in (pltpu.SMEM, pltpu.VMEM))
    hbm = pl.BlockSpec(memory_space=pltpu.HBM)
    return pl.pallas_call(
        functools.partial(update_kernel, plan, heights),
        out_shape=outs,
        in_specs=[smem] * 2 + [vmem] * 4 + [hbm] * (len(halves) + len(arrays)),
        out_specs=[hbm] * (4 * len(chunks)) + [vmem] * 5,
        scratch_shapes=[buffer] * 2 + [pltpu.SemaphoreType.DMA((plan.stretches,))] * 2,
        compiler_params=pltpu.CompilerParams(vmem_limit_bytes=LIMIT),
        cost_estimate=cost(10),
    )(info, part_square, small, *vectors, *halves, *arrays)


def body(
    activations,
    cotangent,
    seq_starts,
    attn_weight,
    up_weight,
    down_weight,
    vectors,
    attn_m,
    up_m,
    down_m,
    vec_m,
    attn_v,
    up_v,
    down_v,
    vec_v,
):
    rows, length, width = activations.shape
    n = lax.axis_size("rows")
    hidden = up_weight.shape[1]
    tokens = rows * length
    slots = seq_starts.shape[1]
    block = width // n
    me, place = lax.axis_index("rows"), lax.axis_index("seq")
    first = place * length
    info = jnp.concatenate(
        [jnp.stack([me, place, first]).astype(jnp.int32), seq_starts.reshape(-1)]
    )

    x = activations.reshape(tokens, width)
    dout = cotangent.reshape(tokens, width)
    state_shape = shaped((rows * PAIRS * (HEAD_DIM + 1), LANES))
    act = shaped((tokens, width))

    seq_bits = bits_of("seq")
    joins, bit = len(seq_bits) - 1, seq_bits[-1]
    stretches = lax.axis_size("seq")

    def start(total, i):
        return swap(total, "seq", seq_bits[i])

    def joined(total, other, prefix, reverse, i):
        own, its, entered = (factors[3 * (joins * reverse + i) + part] for part in range(3))
        prefix = [part + other * entered for part in prefix] or [other * entered]
        return prefix[0], total * own + other * its

    factors = call(
        FORWARD * 2.5,
        functools.partial(joins_kernel, slots, length, stretches),
        [shaped((6 * joins,) + state_shape.shape)],
        info,
        [],
    )[0]
    share = hidden // n
    distances = range(1, n // 2)

    def columns(distance):
        chip = (me // 2) ^ distance
        part = lax.dynamic_slice_in_dim(up_weight, chip * 2 * share, 2 * share, 1)
        return jnp.split(part, 2 * share // width, axis=1)

    first = {d: swap(attn_weight[:3], "rows", 2 * d) for d in distances}
    near_parts = {d: jnp.concatenate([attn_weight[3]] + columns(d), axis=0) for d in distances}
    near = {d: swap(part, "rows", 2 * d) for d, part in near_parts.items()}
    far_parts = {
        d: jnp.concatenate([c for e in distances for c in columns(d ^ e)] + [down_weight], axis=0)
        for d in distances
    }

    def both_cores(chips):
        got = {2 * d: part for d, part in chips.items()}
        got.update({2 * d + 1: swap(part, "rows", 1) for d, part in chips.items()})
        return got

    def ordered(pieces):
        return [pieces[j] for j in sorted(pieces)]

    qkv = both_cores(
        {0: attn_weight[:3], **{d: after(first[d], factors, near_parts[d]) for d in distances}}
    )
    own = both_cores({0: attn_weight[3]}), both_cores({0: up_weight}), both_cores({0: down_weight})
    own_out, own_up, own_down = (ordered(pieces) for pieces in own)
    qkv = ordered(qkv)
    wq, wk, wv = (row_blocks(qkv, lead) for lead in range(3))
    normed, k, v, state = call(
        FORWARD * 5.6,
        functools.partial(keys_kernel, slots, rows),
        [act, act, act, state_shape],
        info,
        [x, vectors, wk, wv],
    )
    other = start(state, 0)
    far = {d: swap(after(part, state), "rows", 2 * d) for d, part in far_parts.items()}
    other, own_out[1], own_up[1], own_down[1] = meeting([other, own_out[1], own_up[1], own_down[1]])
    prefix, total = joined(state, other, [], False, 0)
    other = start(total, 1)
    slopes = call(
        FORWARD * 4,
        slopes_kernel,
        [shaped((tokens, 2 * share))],
        info,
        [after(dout, total)] + own_down,
        sends=2,
    )[0]
    (other, slopes), near = meeting_of([other, slopes], near)
    for i in range(1, joins):
        prefix, total = joined(total, other, [prefix], False, i)
        other = start(total, i + 1)
    near_all = ordered(both_cores({d: after(part, total) for d, part in near.items()}))
    q, numer, denom = call(
        FORWARD * 8.5,
        functools.partial(queries_kernel, slots, rows),
        [act, act, act],
        info,
        [after(normed, total), wq, k, v],
        sends=1 + 2 * rows,
    )
    other, *near_all = meeting([other, *near_all, q])[:-1]
    wo = row_blocks(own_out + near_all)
    att, inv, resid, second, state_in = call(
        FORWARD * 6.3,
        functools.partial(attend_kernel, slots, rows, bit),
        [act, act, act, act, state_shape],
        info,
        [prefix, other, q, numer, denom, wo, x, vectors],
        sends=3 + 2 * rows,
    )

    small_shape = shaped((16, width))

    def up_columns(j, parts, top):
        def plan(info, refs, buffer):
            mine = (info[0] ^ j) * share
            column = ((info[0] ^ j) & 1) * share
            for m, ref in enumerate(refs):
                at = pl.ds(pl.multiple_of((info[0] ^ m) * block, block), block)
                if m < 2:
                    source = ref.at[:, pl.ds(pl.multiple_of(mine, share), share)]
                else:
                    row = top + lax.div(column, width) * block
                    lanes = pl.ds(pl.multiple_of(lax.rem(column, width), share), share)
                    source = ref.at[pl.ds(pl.multiple_of(row, block), block), lanes]
                yield source, buffer.at[at, :]

        return Built((width, share), own_up + parts, plan, n)

    def bottom(part):
        top = part.shape[0] - share
        return Built((share, width), [part], lambda info, refs, buffer: [(refs[0].at[top:, :], buffer)])

    js = list(range(2))
    own_slopes = [
        Built(
            (tokens, share),
            [slopes],
            lambda info, refs, buffer, j=j: [(refs[0].at[:, j * share : (j + 1) * share], buffer)],
        )
        for j in js
    ]
    blocks = [a for j in js for a in (up_columns(j, near_all, block), own_slopes[j])]
    (second,), far = meeting_of([second], far)
    far_all = ordered(both_cores(far))
    wide, narrow = shaped((tokens, share * 2)), shaped((1, share * 2))
    g0, e0, back, dbias0 = call(
        FORWARD * 9,
        functools.partial(feed_kernel, js, False),
        [wide, wide, act, narrow],
        info,
        [second, dout] + blocks + [vectors],
        sends=2 * len(js) + 2,
    )
    js = list(range(2, n))
    tops = [(j // 2 - 1) * (2 * share // width) * block for j in js]
    far_down = [bottom(part) for part in far_all]
    blocks = [a for j, top, down in zip(js, tops, far_down) for a in (up_columns(j, far_all, top), down)]
    wide, narrow = shaped((tokens, share * len(js))), shaped((1, share * len(js)))
    g1, e1, dresid, small, dbias1, dn, dd, dstate = call(
        FORWARD * 16,
        functools.partial(turn_kernel, js, slots, rows),
        [wide, wide, act, small_shape, narrow, act, act, state_shape],
        info,
        [second, dout] + blocks + [vectors, back, resid, wo, inv, att, q],
        limit=ALL,
        scratch=[pltpu.VMEM((tokens, width), F32)],
        sends=2 * len(js) + 4 + 2 * rows,
    )

    half_rows = shaped((n // 2 * share, width))

    def gradients(kernel, common, tops):
        full = (n, width, share) if kernel is up_grads_kernel else (n, share, width)
        return call(
            7,
            functools.partial(kernel, n, stretches),
            [half_rows] * 2,
            info,
            [common] + tops,
            direct=(0, 1),
            scratch=[pltpu.VMEM(full, F32)],
            sends=n * n * stretches * width // hidden if kernel is up_grads_kernel else n * stretches,
        )

    other = start(dstate, 0)
    down_theirs, down_mine = gradients(down_grads_kernel, after(dout, dstate), [g0, g1])
    other, down_theirs, down_mine = meeting([other, down_theirs, down_mine])

    dprefix, dtotal = joined(dstate, other, [], True, 0)
    other = start(dtotal, 1)
    chunk_down = Chunk(down_theirs, down_mine, early=DOWN)
    up_theirs, up_mine = gradients(up_grads_kernel, after(second, dtotal), [e0, e1])
    chunks = [chunk_down]
    other, up_theirs, up_mine, dprefix = meeting([other, up_theirs, up_mine, dprefix], chunks)

    for i in range(1, joins):
        dprefix, dtotal = joined(dtotal, other, [dprefix], True, i)
        other = start(dtotal, i + 1)
        if i + 1 < joins:
            (other,) = meeting([other], chunks)
    chunk_down.advance()
    chunk_up = Chunk(up_theirs, up_mine, early=UP)
    dk, dv, dq = call(
        13,
        functools.partial(local_back_kernel, slots, rows),
        [act, act, act],
        info,
        [after(q, dtotal), k, v, dn, dd, state_in],
        sends=3 * rows,
    )
    chunks = [chunk_down, chunk_up]
    dk, other, dprefix = meeting([dk, other, dprefix])

    chunk_down.advance()
    chunk_up.advance()
    four = shaped((n // 2 * 4 * block, width))
    attn_theirs, attn_mine, gk, gv = call(
        6,
        functools.partial(keys_back_kernel, n, slots, rows, bit, stretches),
        [four, four, act, act],
        info,
        [dprefix, other, v, k, dk, dv, normed, dq, att, dresid],
        direct=(0, 1),
        scratch=[pltpu.VMEM((4, width, width), F32), pltpu.VMEM(state_shape.shape, F32)],
        sends=n * stretches + 2,
    )
    attn_theirs, attn_mine, gk = meeting([attn_theirs, attn_mine, gk], chunks)

    chunk_attn = Chunk(attn_theirs, attn_mine)
    chunk_down.advance()
    chunk_up.advance()
    meeting([], [chunk_attn])
    chunk_attn.advance()
    dx, small = call(
        6,
        functools.partial(input_back_kernel, n),
        [act, small_shape],
        info,
        [after(gk, chunk_attn.held), wk, gv, wv, dq, wq, x, dresid, vectors, small, dbias0, dbias1],
    )
    chunks = [chunk_attn, chunk_down, chunk_up]
    small, late = meeting([small, resid])

    small = small + swap(small, "rows", 1)
    chunk_attn.extra = small
    late = after(late, dx)
    for chunk in chunks:
        chunk.advance()
    out = call(
        7,
        functools.partial(out_kernel, 2),
        [act],
        info,
        [vectors, late, g0, g1] + own_down + far_down,
    )[0]
    plan = chunk_attn.plan
    while chunks:
        if chunk_attn.step == 4:
            (out,) = meeting([out], chunks[1:])
        for chunk in chunks:
            chunk.advance()
        chunks = [chunk for chunk in chunks if chunk.result is None]
        if chunk_attn.step == len(plan.down) + 1:
            small = chunk_attn.extra
            for bits in plan.down[:1]:
                small = small + plan.move(small, bits)
    square = sum(jnp.sum(a * a) for chunk in (chunk_up, chunk_down, chunk_attn) for a in chunk.result)
    for bit in bits_of("rows"):
        square = square + swap(square, "rows", bit)

    def flat(a):
        return a.reshape(-1, width)

    results = update(
        info,
        square.reshape(1),
        small,
        [vectors, vec_m, vec_v],
        [
            (chunk_up.result, up_weight, up_m, up_v),
            (chunk_down.result, down_weight, down_m, down_v),
            (chunk_attn.result, flat(attn_weight), flat(attn_m), flat(attn_v)),
        ],
    )
    up_g, up_new, up_m_new, up_v_new = results[:4]
    down_g, down_new, down_m_new, down_v_new = results[4:8]
    attn_g, attn_new, attn_m_new, attn_v_new = (
        a.reshape(attn_weight.shape) for a in results[8:12]
    )
    grad_norm = results[12].reshape(())
    vec_g, vec_new, vec_m_new, vec_v_new = results[13:]
    return (
        out.reshape(activations.shape),
        dx.reshape(activations.shape),
        grad_norm,
        attn_g,
        up_g,
        down_g,
        vec_g,
        attn_new,
        up_new,
        down_new,
        vec_new,
        attn_m_new,
        up_m_new,
        down_m_new,
        vec_m_new,
        attn_v_new,
        up_v_new,
        down_v_new,
        vec_v_new,
    )


def solution(mesh):
    stretch = P("rows", "seq", None)
    stacked = P(None, "rows", None)
    split_rows = P("rows", None)
    weights = (stacked, split_rows, split_rows, P())
    return jax.shard_map(
        body,
        mesh=mesh,
        in_specs=(stretch, stretch, split_rows) + weights * 3,
        out_specs=(stretch, stretch, P()) + weights * 4,
        check_vma=False,
    )
```

```python
import functools
import math

import jax
import jax.numpy as jnp
from jax import lax
from jax.experimental import pallas as pl
from jax.experimental.pallas import tpu as pltpu
from jax.sharding import PartitionSpec as P

HEADS = 8
HEAD_DIM = 64
PAIRS = HEADS // 2
LANES = 2 * HEAD_DIM
STEP = 5

EPS_NORM = 1e-05
EPS_DEN = 1e-06
CLIP_AT = 1.0
BETA_ONE = 0.5
BETA_TWO = 0.5
RATE_MAT = 0.02
RATE_VEC = 0.1
DECAY_MAT = 0.1
EPS_ADAM = 1e-08

F32 = jnp.float32
FORWARD = 0.01
DOWN, UP = 1, 1
LIMIT = 56 * 1024 * 1024
ALL = 63 * 1024 * 1024


def cost(us):
    return pl.CostEstimate(flops=int(us * 1e9), bytes_accessed=int(us * 2e6), transcendentals=0)


class Given:
    def __init__(self, ref, copies):
        self.ref, self.copies, self.shape = ref, copies, ref.shape

    def __getitem__(self, at):
        while self.copies:
            self.copies.pop(0).wait()
        return self.ref[at]


class Made:
    def __init__(self, ref, out, send):
        self.ref, self.out, self.send, self.shape = ref, out, send, out.shape
        self.sent = False

    def __getitem__(self, at):
        return self.ref[at]

    def __setitem__(self, at, value):
        self.ref[at] = value

    def flush(self, at=slice(None)):
        self.sent = True
        self.send(self.ref.at[at], self.out.at[at])


class Built:
    def __init__(self, shape, arrays, plan, copies=1):
        self.shape, self.arrays, self.plan, self.copies = shape, arrays, plan, copies


def whole(info, refs, buffer):
    return [(refs[0], buffer)]


def built(operand):
    return operand if isinstance(operand, Built) else Built(operand.shape, [operand], whole)


def call(us, kernel, outs, info, ins, scratch=(), direct=(), smem=(), sends=None, limit=LIMIT):
    ins = [built(a) for a in ins]
    arrays = []
    for a in ins:
        arrays += [b for b in a.arrays if not any(b is c for c in arrays)]
    places = [[next(i for i, c in enumerate(arrays) if c is b) for b in a.arrays] for a in ins]
    sends = sends or len(outs)

    def body(info_ref, *refs):
        refs = list(refs)

        def take(count):
            part, refs[:] = refs[:count], refs[count:]
            return part

        extra, given, results = take(len(smem)), take(len(arrays)), take(len(outs))
        in_buffers, out_buffers = take(len(ins)), take(len(outs) - len(direct))
        in_sems, out_sems = refs.pop(), refs.pop()
        operands, count = [], 0
        for a, at, buffer in zip(ins, places, in_buffers):
            copies = []
            for source, target in a.plan(info_ref, [given[i] for i in at], buffer):
                copies.append(pltpu.make_async_copy(source, target, in_sems.at[count]))
                copies[-1].start()
                count += 1
            operands.append(Given(buffer, copies))
        sent = []

        def send(source, target):
            sent.append(pltpu.make_async_copy(source, target, out_sems.at[len(sent)]))
            sent[-1].start()

        made = [
            Made(None if i in direct else out_buffers.pop(0), out, send)
            for i, out in enumerate(results)
        ]
        kernel(info_ref, *extra, *operands, *made, *refs)
        for operand in operands:
            for copy in operand.copies:
                copy.wait()
        for i, out in enumerate(made):
            if i not in direct and not out.sent:
                out.flush()
        for copy in sent:
            copy.wait()
        assert len(sent) == sends, (len(sent), sends)

    hbm = pl.BlockSpec(memory_space=pltpu.HBM)
    smem_spec = pl.BlockSpec(memory_space=pltpu.SMEM)
    buffers = [pltpu.VMEM(a.shape, F32) for a in ins]
    buffers += [pltpu.VMEM(a.shape, F32) for i, a in enumerate(outs) if i not in direct]
    sems = [pltpu.SemaphoreType.DMA((count,)) for count in (sends, max(1, sum(a.copies for a in ins)))]
    return pl.pallas_call(
        body,
        out_shape=outs,
        in_specs=[smem_spec] * (1 + len(smem)) + [hbm] * len(arrays),
        out_specs=[hbm] * len(outs),
        scratch_shapes=buffers + list(scratch) + sems,
        compiler_params=pltpu.CompilerParams(vmem_limit_bytes=limit),
        cost_estimate=cost(us),
    )(info, *smem, *arrays)


def shaped(shape):
    return jax.ShapeDtypeStruct(tuple(shape), F32)


def row_blocks(pieces, lead=None, top=0):
    def plan(info, refs, buffer):
        rows = buffer.shape[0] // len(refs)
        for j, ref in enumerate(refs):
            at = pl.ds(pl.multiple_of((info[0] ^ j) * rows, rows), rows)
            source = ref if lead is None else ref.at[lead]
            first = top if source.shape[0] > rows else 0
            yield source.at[first : first + rows, :], buffer.at[at, :]

    width = pieces[0].shape[-1]
    return Built((width, width), pieces, plan, len(pieces))


def split(a):
    high = a.astype(jnp.bfloat16)
    return high, (a - high.astype(F32)).astype(jnp.bfloat16)


def dot(a, b, ca=1, cb=0):
    dims = (((ca,), (cb,)), ((), ()))
    a, b = (x if isinstance(x, tuple) else split(x) for x in (a, b))

    def one(p, q):
        return lax.dot_general(p, q, dims, preferred_element_type=F32)

    return one(a[0], b[0]) + (one(a[0], b[1]) + one(a[1], b[0]))


def phi(u):
    return jnp.where(u > 0, u + 1.0, jnp.exp(jnp.minimum(u, 0.0)))


def normalise(x):
    centred = x - jnp.mean(x, axis=1, keepdims=True)
    scale = lax.rsqrt(jnp.mean(centred * centred, axis=1, keepdims=True) + EPS_NORM)
    return centred * scale, scale


def normalise_back(grad, unit, scale):
    inner = jnp.mean(grad * unit, axis=1, keepdims=True)
    return scale * (grad - jnp.mean(grad, axis=1, keepdims=True) - unit * inner)


def first_head(shape):
    return lax.broadcasted_iota(jnp.int32, shape, len(shape) - 1) % LANES < HEAD_DIM


def pick(value, head):
    return jnp.where(first_head(value.shape) == (head == 0), value, 0.0)


def lower(shape):
    return lax.broadcasted_iota(jnp.int32, shape, 1) < HEAD_DIM


def halves_of(pair):
    high, low = split(pair)
    turned = pltpu.roll(pair, HEAD_DIM, 1)
    return (high, low), split(turned)


def streamed(plain, turned, tail=None):
    first = lower(plain[0].shape)
    out = []
    for head in range(2):
        here, there = (plain, turned) if head == 0 else (turned, plain)
        end = here[0]
        if tail is not None:
            end = jnp.where(first, end, tail[1 - head])
        out.append(jnp.concatenate([jnp.where(first, here[0], there[1]), end], axis=1))
    return out


def held(plain, turned, fill):
    first = lower(plain[0].shape)
    out = []
    for head in range(2):
        here, there = (plain, turned) if head == 0 else (turned, plain)
        end = jnp.where(first, here[1], jnp.full_like(here[1], fill))
        out.append(jnp.concatenate([jnp.where(first, here[0], there[0]), end], axis=1))
    return out


def alternate(high, low):
    lanes = lax.broadcasted_iota(jnp.int32, high.shape, 1)
    return jnp.where(lanes % HEAD_DIM < HEAD_DIM // 2, high, low)


def once(a, b):
    return lax.dot_general(a, b, (((1,), (1,)), ((), ())), preferred_element_type=F32)


def beside(halves, head, fill=0.0):
    high, low = halves
    mine = lower(high.shape) == (head == 0)
    return jnp.concatenate(
        [jnp.where(mine, high, jnp.full_like(high, fill)), jnp.where(mine, low, jnp.zeros_like(low))],
        axis=1,
    )


def mixed(scores, pair):
    high, low = split(scores)
    count = high.shape[0]
    both = lax.dot_general(
        jnp.concatenate([high, low], axis=0), pair, (((1,), (0,)), ((), ())), preferred_element_type=F32
    )
    both = both[:count] + both[count:]
    return both[:, :LANES] + both[:, LANES:]


def block_ones():
    shape = (LANES, LANES)
    rows, lanes = (lax.broadcasted_iota(jnp.int32, shape, d) // HEAD_DIM for d in (0, 1))
    return jnp.where(rows == lanes, 1.0, 0.0)


class Info:
    def __init__(self, ref, length, slots):
        self.ref, self.length, self.slots = ref, length, slots
        self.me, self.place, self.first = ref[0], ref[1], ref[2]

    def starts(self, r):
        return [self.ref[3 + r * self.slots + i] for i in range(self.slots)]

    def document(self, r, position):
        return sum(jnp.where(a <= position, 1, 0) for a in self.starts(r))

    def causal(self, r, flipped=False):
        shape = (self.length, self.length)
        t = self.first + lax.broadcasted_iota(jnp.int32, shape, 1 if flipped else 0)
        s = self.first + lax.broadcasted_iota(jnp.int32, shape, 0 if flipped else 1)
        ok = t >= s
        for a in self.starts(r):
            ok = ok & ((t < a) | (s >= a))
        return jnp.where(ok, 1.0, 0.0)

    def from_before(self, r, width):
        t = self.first + lax.broadcasted_iota(jnp.int32, (self.length, width), 0)
        ok = t >= 0
        for a in self.starts(r):
            ok = ok & ((a < self.first) | (t < a))
        return jnp.where(ok, 1.0, 0.0)

    def to_after(self, r, width):
        s = self.first + lax.broadcasted_iota(jnp.int32, (self.length, width), 0)
        last = self.first + self.length - 1
        ok = s >= 0
        for a in self.starts(r):
            ok = ok & ((s >= a) | (a > last))
        return jnp.where(ok, 1.0, 0.0)


def state_blocks(ref, r, p):
    at = (r * PAIRS + p) * HEAD_DIM
    packed = ref[at : at + HEAD_DIM, :]
    sums = ref.shape[0] // (HEAD_DIM + 1) * HEAD_DIM + r * PAIRS + p
    return (
        jnp.concatenate([pick(packed, 0), pick(packed, 1)], axis=0),
        ref[sums : sums + 1, :],
    )


def store_state(ref, r, p, full, key_sum):
    at = (r * PAIRS + p) * HEAD_DIM
    top, bottom = full[:HEAD_DIM], full[HEAD_DIM:]
    ref[at : at + HEAD_DIM, :] = jnp.where(first_head(top.shape), top, bottom)
    sums = ref.shape[0] // (HEAD_DIM + 1) * HEAD_DIM + r * PAIRS + p
    ref[sums : sums + 1, :] = key_sum


def pair_slices(length, r, p):
    return slice(r * length, (r + 1) * length), slice(p * LANES, (p + 1) * LANES)


def row_slice(length, r):
    return slice(r * length, (r + 1) * length)


def keys_kernel(slots, rows, ref, x, vec, wk, wv, normed, k, v, state):
    length = x.shape[0] // rows
    info = Info(ref, length, slots)
    unit, _ = normalise(x[...])
    normed[...] = unit * vec[0:1, :] + vec[1:2, :]
    normed.flush()
    k[...] = phi(dot(normed[...], wk[...]))
    v[...] = dot(normed[...], wv[...])
    k.flush()
    v.flush()
    for r in range(rows):
        kept = info.to_after(r, LANES)
        for p in range(PAIRS):
            at = pair_slices(length, r, p)
            masked = k[at] * kept
            store_state(state, r, p, dot(masked, v[at], 0, 0), jnp.sum(masked, axis=0, keepdims=True))
    state.flush()


def queries_kernel(slots, rows, ref, normed, wq, k, v, q, numer, denom):
    length = k.shape[0] // rows
    info = Info(ref, length, slots)
    q[...] = phi(dot(normed[...], wq[...]))
    q.flush()
    for r in range(rows):
        mask = info.causal(r)
        for p in range(PAIRS):
            at = pair_slices(length, r, p)
            lefts, rights = streamed(*halves_of(q[at])), held(*halves_of(k[at]), 0.0)
            values = split(v[at])
            sums = [
                mixed(once(lefts[head], rights[head]) * mask, beside(values, head, 1.0))
                for head in range(2)
            ]
            first = lower(sums[0].shape)
            numer[at] = jnp.where(first, *sums)
            denom[at] = pltpu.roll(jnp.where(first, sums[1], sums[0]), HEAD_DIM, 1)
        numer.flush(row_slice(length, r))
        denom.flush(row_slice(length, r))


def attend_kernel(slots, rows, bit, ref, prefix, other, q, numer, denom, wo, x, vec, att, inv, resid, second, state):
    length = x.shape[0] // rows
    info = Info(ref, length, slots)
    enter(info, bit, False, prefix, other, state)
    state.flush()
    ones = block_ones()
    for r in range(rows):
        use = info.from_before(r, LANES)
        for p in range(PAIRS):
            at = pair_slices(length, r, p)
            block, key_sum = state_blocks(state, r, p)
            q_pair = q[at] * use
            top = numer[at] + dot(q_pair, block)
            under = denom[at] + dot(q_pair * key_sum, ones) + EPS_DEN
            inverse = 1.0 / under
            inv[at] = inverse
            att[at] = top * inverse
        att.flush(row_slice(length, r))
        inv.flush(row_slice(length, r))
    resid[...] = x[...] + dot(att[...], wo[...])
    resid.flush()
    unit, _ = normalise(resid[...])
    second[...] = unit * vec[2:3, :] + vec[3:4, :]
    second.flush()


def slopes_kernel(info, dout, *refs):
    *downs, out = refs
    grad_out = split(dout[...])
    for i, down in enumerate(downs):
        share = down.shape[0]
        here = (slice(None), slice(i * share, (i + 1) * share))
        out[here] = dot(grad_out, down[...], 1, 1)
        out.flush(here)


def feed_kernel(js, last, info, second, dout, *refs):
    count = len(js)
    blocks, refs = [refs[2 * i : 2 * i + 2] for i in range(count)], refs[2 * count :]
    if last:
        vec, back_in, resid, g, e, dresid, small, dbias, back = refs
        grad_out = split(dout[...])
    else:
        vec, g, e, back, dbias = refs
    share = dbias.shape[1] // count
    inputs = split(second[...])
    for i, (up, down) in enumerate(blocks):
        column, width = (info[0] ^ js[i]) * share, vec.shape[1]
        lanes = pl.ds(pl.multiple_of(lax.rem(column, width), share), share)
        bias = vec[pl.ds(5 + lax.div(column, width), 1), lanes]
        here = (slice(None), slice(i * share, (i + 1) * share))
        weights = split(up[...])
        h = dot(inputs, weights) + bias
        cdf = 0.5 * (1.0 + lax.erf(h * math.sqrt(0.5)))
        g[here] = h * cdf
        g.flush(here)
        slope = cdf + h * (jnp.exp(-0.5 * h * h) * (1.0 / math.sqrt(2.0 * math.pi)))
        grad = (dot(grad_out, down[...], 1, 1) if last else down[...]) * slope
        e[here] = grad
        e.flush(here)
        dbias[here] = jnp.sum(grad, axis=0, keepdims=True)
        part = dot(grad, weights, 1, 1)
        if i == 0:
            back[...] = back_in[...] + part if last else part
        else:
            back[...] = back[...] + part
    if last:
        unit, scale = normalise(resid[...])
        grad_second = back[...]
        small[...] = jnp.zeros(small.shape, F32)
        small[2:3, :] = jnp.sum(grad_second * unit, axis=0, keepdims=True)
        small[3:4, :] = jnp.sum(grad_second, axis=0, keepdims=True)
        small[4:5, :] = jnp.sum(dout[...], axis=0, keepdims=True)
        dresid[...] = dout[...] + normalise_back(grad_second * vec[2:3, :], unit, scale)


def turn_kernel(js, slots, rows, info, *refs):
    ins, outs, back = refs[: 2 * len(js) + 9], refs[2 * len(js) + 9 : -1], refs[-1]
    feed_kernel(js, True, info, *ins[:-4], *outs[:5], back)
    outs[2].flush()
    attend_back_kernel(slots, rows, info, outs[2], *ins[-4:], *outs[5:])


def out_kernel(count, info, vec, resid, *refs):
    *refs, out = refs
    tops, downs = refs[:count], list(refs[count:])
    out[...] = resid[...] + vec[4:5, :]
    for g in tops:
        share = downs[0].shape[0]
        for i in range(g.shape[1] // share):
            out[...] = out[...] + dot(g[:, i * share : (i + 1) * share], downs.pop(0)[...])


def state_rows(ref):
    sums = ref.shape[0] // (HEAD_DIM + 1)
    for r in range(sums // PAIRS):
        yield r, slice(r * PAIRS * HEAD_DIM, (r + 1) * PAIRS * HEAD_DIM)
        yield r, slice(sums * HEAD_DIM + r * PAIRS, sums * HEAD_DIM + (r + 1) * PAIRS)


def enter(info, bit, reverse, prefix, other, out):
    for r, at in state_rows(out):
        out[at, :] = prefix[at, :] + other[at, :] * meet(info, bit, reverse, r)[2]


def joins_kernel(slots, length, stretches, ref, out):
    info = Info(ref, length, slots)
    bits = [1 << i for i in range(stretches.bit_length() - 1)][:-1]
    for i, (reverse, bit) in enumerate((reverse, bit) for reverse in (False, True) for bit in bits):
        for r, at in state_rows(out.ref.at[0]):
            mine_late, same, reaches = meet(info, bit, reverse, r)
            values = (jnp.where(mine_late, 1.0, same), jnp.where(mine_late, same, 1.0), reaches)
            for part, value in enumerate(values):
                out[3 * i + part, at, :] = jnp.full((at.stop - at.start, LANES), value)


def meet(info, bit, reverse, r):
    place, length = info.place, info.length
    bits = place & bit
    mine_late = (bits == 0) if reverse else (bits != 0)
    low = place & ~(bit - 1)
    shift = -1 if reverse else bit * length - 1
    here, there = (info.document(r, group * length + shift) for group in (low, low ^ bit))
    own = info.document(r, info.first + (length - 1 if reverse else -1))
    return mine_late, jnp.where(here == there, 1.0, 0.0), jnp.where(mine_late & (there == own), 1.0, 0.0)


def attend_back_kernel(slots, rows, ref, dresid, wo, inv, att, q, dn, dd, state):
    length = q.shape[0] // rows
    info = Info(ref, length, slots)
    grad = dot(dresid[...], wo[...], 1, 1)
    ones = block_ones()
    for r in range(rows):
        use = info.from_before(r, LANES)
        for p in range(PAIRS):
            at = pair_slices(length, r, p)
            grad_pair = grad[at]
            over = grad_pair * inv[at]
            dn[at] = over
            under = -dot(grad_pair * att[at], ones) * inv[at]
            dd[at] = under
            q_pair = q[at] * use
            full = dot(q_pair, over, 0, 0)
            store_state(state, r, p, full, jnp.sum(q_pair * under, axis=0, keepdims=True))
        dn.flush(row_slice(length, r))
        dd.flush(row_slice(length, r))


def put_block(info, stretches, group, odd, stretch, source, theirs, mine, lanes=slice(None), early=False):
    rows = source.shape[0]
    groups = theirs.shape[0] // (stretches * rows)
    core = (info[0] & 1) ^ odd
    mask = group + groups * (info[1] ^ stretch)
    at = Plan(early, groups, stretches).position(mask, core) * rows
    out = theirs if odd else mine
    out.send(source, out.out.at[pl.ds(pl.multiple_of(at, rows), rows), lanes])


def down_grads_kernel(n, stretches, info, dout, *refs):
    *refs, theirs, mine, full = refs
    grad_out = dout[...]
    rows = full.shape[1] // stretches
    j = 0
    for g in refs:
        share = full.shape[1]
        for i in range(g.shape[1] // share):
            full[j] = dot(g[:, i * share : (i + 1) * share], grad_out, 0, 0)
            for s in range(stretches):
                source = full.at[j, s * rows : (s + 1) * rows, :]
                put_block(info, stretches, j // 2, j & 1, s, source, theirs, mine, early=DOWN)
            j += 1


def up_grads_kernel(n, stretches, info, second, *refs):
    *refs, theirs, mine, full = refs
    share, width = full.shape[2], theirs.shape[1]
    tall = full.shape[1] // n
    rows = tall * (n * share // width) // stretches
    j = 0
    for e in refs:
        for i in range(e.shape[1] // share):
            full[j] = dot(second[...], e[:, i * share : (i + 1) * share], 0, 0)
            column = (info[0] ^ j) * share
            lanes = pl.ds(pl.multiple_of(lax.rem(column, width), share), share)
            for m in range(n):
                for b in range(tall // rows):
                    start = (info[0] ^ m) * tall + b * rows
                    source = full.at[j, pl.ds(pl.multiple_of(start, rows), rows), :]
                    stretch = lax.div(column, width) * (tall // rows) + b
                    put_block(info, stretches, m // 2, m & 1, stretch, source, theirs, mine, lanes, UP)
            j += 1


def deal(info, n, stretches, full, theirs, mine, slot, slots=4):
    tall = full.shape[0] // n
    rows = tall * slots // stretches
    for m in range(n):
        for i in range(tall // rows):
            start = (info[0] ^ m) * tall + i * rows
            source = full.at[pl.ds(pl.multiple_of(start, rows), rows), :]
            stretch = slot * (tall // rows) + i
            put_block(info, stretches, m // 2, m & 1, stretch, source, theirs, mine)


def local_back_kernel(slots, rows, ref, q, k, v, dn, dd, state, dk, dv, dq):
    length = q.shape[0] // rows
    info = Info(ref, length, slots)
    for r in range(rows):
        use = info.from_before(r, LANES)
        mask, flipped = info.causal(r), info.causal(r, True)
        for p in range(PAIRS):
            at = pair_slices(length, r, p)
            q_pair, k_pair, v_pair, dn_pair, dd_pair = q[at], k[at], v[at], dn[at], dd[at]
            block, key_sum = state_blocks(state, r, p)
            grad_q = use * (dot(dn_pair, block, 1, 1) + dd_pair * key_sum)
            grad_k = grad_v = 0.0
            q_halves, k_halves, v_halves, dn_halves = (
                halves_of(a) for a in (q_pair, k_pair, v_pair, dn_pair)
            )
            tops = streamed(*dn_halves, [alternate(*h) for h in halves_of(dd_pair)])
            values = held(*v_halves, 2.0 / HEAD_DIM)
            queries, keys = streamed(*q_halves), held(*k_halves, 0.0)
            for head in range(2):
                grad_scores = once(tops[head], values[head]) * mask
                grad_q = grad_q + mixed(grad_scores, beside(k_halves[0], head))
                grad_flipped = once(values[head], tops[head]) * flipped
                grad_k = grad_k + mixed(grad_flipped, beside(q_halves[0], head))
                scores_flipped = once(keys[head], queries[head]) * flipped
                grad_v = grad_v + mixed(scores_flipped, beside(dn_halves[0], head))
            dq[at] = grad_q * jnp.minimum(q_pair, 1.0)
            dk[at] = grad_k
            dv[at] = grad_v
        for out in (dk, dv, dq):
            out.flush(row_slice(length, r))


def keys_back_kernel(n, slots, rows, bit, stretches, ref, prefix, other, v, k, dk, dv, normed, dq, att, dresid, theirs, mine, gk, gv, full, state):
    length = k.shape[0] // rows
    info = Info(ref, length, slots)
    enter(info, bit, True, prefix, other, state)
    for r in range(rows):
        kept = info.to_after(r, LANES)
        for p in range(PAIRS):
            at = pair_slices(length, r, p)
            block, key_sum = state_blocks(state, r, p)
            k_pair = k[at]
            grad_k = dk[at] + kept * (dot(v[at], block, 1, 1) + key_sum)
            gk[at] = grad_k * jnp.minimum(k_pair, 1.0)
            gv[at] = dv[at] + dot(k_pair * kept, block)
    inputs = split(normed[...])
    for slot, grad in ((1, gk), (2, gv), (0, dq)):
        full[slot] = dot(inputs, grad[...], 0, 0)
        deal(ref, n, stretches, full.at[slot], theirs, mine, slot)
    full[3] = dot(att[...], dresid[...], 0, 0)
    deal(ref, n, stretches, full.at[3], theirs, mine, 3)


def input_back_kernel(n, info, gk, wk, gv, wv, dq, wq, x, dresid, vec, small_in, *refs):
    *biases, dx, small = refs
    grad = dot(gk[...], wk[...], 1, 1) + dot(gv[...], wv[...], 1, 1) + dot(dq[...], wq[...], 1, 1)
    unit, scale = normalise(x[...])
    dx[...] = dresid[...] + normalise_back(grad * vec[0:1, :], unit, scale)
    dx.flush()
    small[...] = small_in[...]
    small[0:1, :] = jnp.sum(grad * unit, axis=0, keepdims=True)
    small[1:2, :] = jnp.sum(grad, axis=0, keepdims=True)
    width = small.shape[1]
    share = sum(ref.shape[1] for ref in biases) // n
    j = 0
    for bias in biases:
        for i in range(bias.shape[1] // share):
            column = (info[0] ^ j) * share
            lanes = pl.ds(pl.multiple_of(lax.rem(column, width), share), share)
            small[pl.ds(5 + lax.div(column, width), 1), lanes] = bias[0:1, i * share : (i + 1) * share]
            j += 1


def adamw_step(weight, gradient, first_m, second_m, factor, rate, decay):
    clipped = gradient * factor
    new_m = BETA_ONE * first_m + (1.0 - BETA_ONE) * clipped
    new_v = BETA_TWO * second_m + (1.0 - BETA_TWO) * clipped * clipped
    moved = new_m / (1.0 - BETA_ONE**STEP) / (jnp.sqrt(new_v / (1.0 - BETA_TWO**STEP)) + EPS_ADAM)
    return (clipped, weight - rate * (moved + decay * weight), new_m, new_v)


def update_kernel(plan, heights, info, part_square, small, vec, vec_m, vec_v, *refs):
    count = len(heights)
    halves, arrays, refs = refs[: 2 * count], refs[2 * count : 5 * count], refs[5 * count :]
    outs, (norm, *small_outs), refs = refs[: 4 * count], refs[4 * count : 4 * count + 5], refs[4 * count + 5 :]
    buffers, results, in_sems, out_sems = refs
    stretches = plan.stretches
    spots = []
    for k in range(stretches):
        stretch = info[1] ^ by_core(info, [order[k] for order in plan.order])
        for i, rows in enumerate(heights):
            tall, wide = arrays[3 * i].shape[0], halves[0].shape[1]
            start = stretch * rows
            spot = (
                pl.ds(pl.multiple_of(lax.rem(start, tall), rows), rows),
                pl.ds(pl.multiple_of(lax.div(start, tall) * wide, wide), wide),
            )
            spots.append(spot)
            top = k % (stretches // 2) * rows
            half = halves[2 * i + k // (stretches // 2)]
            sources = [half.at[top : top + rows, :]] + [a.at[spot] for a in arrays[3 * i : 3 * i + 3]]
            for part, source in enumerate(sources):
                pltpu.make_async_copy(source, buffers.at[k, i, part], in_sems.at[k]).start()
    gradient = small[0 : vec.shape[0], :]
    square = jnp.sum(jnp.sum(gradient * gradient, axis=1, keepdims=True), axis=0, keepdims=True)
    length = jnp.sqrt(square + jnp.full((1, 1), part_square[0]))
    norm[...] = length
    factor = jnp.minimum(1.0, CLIP_AT / (length + 1e-06))
    new = adamw_step(vec[...], gradient, vec_m[...], vec_v[...], factor, RATE_VEC, 0.0)
    for out, result in zip(small_outs, new):
        out[...] = result
    for k in range(stretches):
        pltpu.make_async_copy(buffers.at[k], buffers.at[k], in_sems.at[k]).wait()
        for i in range(count):
            gradient, weight, first_m, second_m = (buffers[k, i, part] for part in range(4))
            new = adamw_step(weight, gradient, first_m, second_m, factor, RATE_MAT, DECAY_MAT)
            for part, result in enumerate(new):
                results[k, i, part] = result
                out = outs[4 * i + part].at[spots[k * count + i]]
                pltpu.make_async_copy(results.at[k, i, part], out, out_sems.at[k]).start()
    for k in range(stretches):
        pltpu.make_async_copy(results.at[k], results.at[k], out_sems.at[k]).wait()


def swap(part, axis, bit):
    return lax.ppermute(part, axis, [(i, i ^ bit) for i in range(lax.axis_size(axis))])


def bits_of(axis):
    return [1 << i for i in range(lax.axis_size(axis).bit_length() - 1)]


def after(part, *others):
    return lax.optimization_barrier((part, *others))[0]


class Plan:
    def __init__(self, early=False, groups=None, stretches=None):
        self.groups = groups or lax.axis_size("rows") // 2
        self.stretches = stretches or lax.axis_size("seq")
        ys = [1 << i for i in range(self.groups.bit_length() - 1)]
        seq = [self.groups << i for i in range(self.stretches.bit_length() - 1)]
        xs, zs = seq[: len(ys)], seq[len(ys) :]
        first, second = [], []
        for y, x in zip(ys, xs):
            first += [y, x]
            second += [x, y]
        pairs = list(zip(first, second))
        alone = [(z, z) for z in zs]
        if early == 1:
            self.down = pairs[:1] + alone[:1] + pairs[1:] + alone[1:]
        elif early == 2:
            both, rest = [(y, y) for y in ys], list(zip(zs[:1] + xs, xs + zs[:1]))
            self.down = both + rest + alone[1:]
        else:
            self.down = pairs + alone
        zs, xs = zs[::-1], xs[::-1]
        self.up = [(z, z) for z in zs[:-1]] + list(zip(zs[-1:] + xs, xs + zs[-1:]))
        order = [[0], [0]]
        for bits in self.up:
            order = [o + [m ^ bit for m in o] for o, bit in zip(order, bits)]
        self.order = [[m // self.groups for m in o] for o in order]

    def position(self, mask, core):
        steps = len(self.down)
        places = [
            sum(jnp.where(mask & bits[c], 1 << (steps - 1 - t), 0) for t, bits in enumerate(self.down))
            for c in (0, 1)
        ]
        return jnp.where(core == 0, *places)

    def move(self, part, bits):
        rows = 2 * self.groups
        pairs = []
        for i in range(rows * self.stretches):
            bit = bits[i & 1]
            flip = bit * 2 if bit < self.groups else bit // self.groups * rows
            pairs.append((i, i ^ flip))
        return lax.ppermute(part, ("seq", "rows"), pairs)


def by_core(info, pair):
    return jnp.where(info[0] & 1 == 0, pair[0], pair[1])


class Chunk:
    def __init__(self, theirs, mine, early=False):
        self.plan, self.step, self.result = Plan(early), 0, None
        self.extra, self.carried = None, False
        self.got, self.held = swap(theirs, "rows", 1), mine

    def advance(self):
        plan, step, held, got = self.plan, self.step, self.held, self.got
        self.step += 1
        if self.carried:
            count = self.extra.shape[0]
            self.extra = self.extra + got[-count:]
            got, self.carried = got[:-count], False
        if step < len(plan.down):
            half = held.shape[0] // 2
            send = held[half:] + got[half:]
            self.held = held[:half] + got[:half]
            if self.extra is not None:
                send, self.carried = jnp.concatenate([send, self.extra], axis=0), True
            self.got = plan.move(send, plan.down[step])
            return
        rise = step - len(plan.down)
        if rise < len(plan.up):
            self.held = held + got if rise == 0 else jnp.concatenate([held, got], axis=0)
            self.got = plan.move(self.held, plan.up[rise])
            return
        self.result = [held, got]


def meeting(arrays, chunks=()):
    out = lax.optimization_barrier((*arrays, *(chunk.got for chunk in chunks)))
    for chunk, got in zip(chunks, out[len(arrays) :]):
        chunk.got = got
    return out[: len(arrays)]


def meeting_of(arrays, parts):
    out = lax.optimization_barrier((*arrays, *parts.values()))
    return out[: len(arrays)], dict(zip(parts, out[len(arrays) :]))


def update(info, part_square, small, vectors, chunks):
    plan = Plan()
    halves = [half for gathered, *_ in chunks for half in gathered]
    arrays = [a for _, *part in chunks for a in part]
    heights = [half.shape[0] // (plan.stretches // 2) for half in halves[::2]]
    assert len(set(heights)) == 1
    buffer = pltpu.VMEM((plan.stretches, len(chunks), 4, heights[0], halves[0].shape[1]), F32)
    outs = [shaped(chunk[1].shape) for chunk in chunks for _ in range(4)]
    outs += [shaped((1, 1))] + [shaped(vectors[0].shape)] * 4
    smem, vmem = (pl.BlockSpec(memory_space=space) for space in (pltpu.SMEM, pltpu.VMEM))
    hbm = pl.BlockSpec(memory_space=pltpu.HBM)
    return pl.pallas_call(
        functools.partial(update_kernel, plan, heights),
        out_shape=outs,
        in_specs=[smem] * 2 + [vmem] * 4 + [hbm] * (len(halves) + len(arrays)),
        out_specs=[hbm] * (4 * len(chunks)) + [vmem] * 5,
        scratch_shapes=[buffer] * 2 + [pltpu.SemaphoreType.DMA((plan.stretches,))] * 2,
        compiler_params=pltpu.CompilerParams(vmem_limit_bytes=LIMIT),
        cost_estimate=cost(10),
    )(info, part_square, small, *vectors, *halves, *arrays)


def body(
    activations,
    cotangent,
    seq_starts,
    attn_weight,
    up_weight,
    down_weight,
    vectors,
    attn_m,
    up_m,
    down_m,
    vec_m,
    attn_v,
    up_v,
    down_v,
    vec_v,
):
    rows, length, width = activations.shape
    n = lax.axis_size("rows")
    hidden = up_weight.shape[1]
    tokens = rows * length
    slots = seq_starts.shape[1]
    block = width // n
    me, place = lax.axis_index("rows"), lax.axis_index("seq")
    first = place * length
    info = jnp.concatenate(
        [jnp.stack([me, place, first]).astype(jnp.int32), seq_starts.reshape(-1)]
    )

    x = activations.reshape(tokens, width)
    dout = cotangent.reshape(tokens, width)
    state_shape = shaped((rows * PAIRS * (HEAD_DIM + 1), LANES))
    act = shaped((tokens, width))

    seq_bits = bits_of("seq")
    joins, bit = len(seq_bits) - 1, seq_bits[-1]
    stretches = lax.axis_size("seq")

    def start(total, i):
        return swap(total, "seq", seq_bits[i])

    def joined(total, other, prefix, reverse, i):
        own, its, entered = (factors[3 * (joins * reverse + i) + part] for part in range(3))
        prefix = [part + other * entered for part in prefix] or [other * entered]
        return prefix[0], total * own + other * its

    factors = call(
        FORWARD * 2.5,
        functools.partial(joins_kernel, slots, length, stretches),
        [shaped((6 * joins,) + state_shape.shape)],
        info,
        [],
    )[0]
    share = hidden // n
    distances = range(1, n // 2)

    def columns(distance):
        chip = (me // 2) ^ distance
        part = lax.dynamic_slice_in_dim(up_weight, chip * 2 * share, 2 * share, 1)
        return jnp.split(part, 2 * share // width, axis=1)

    first = {d: swap(attn_weight[1:3], "rows", 2 * d) for d in distances}
    near_parts = {d: jnp.concatenate([attn_weight[3], attn_weight[0]] + columns(d), axis=0) for d in distances}
    near = {d: swap(part, "rows", 2 * d) for d, part in near_parts.items()}
    far_parts = {
        d: jnp.concatenate([c for e in distances for c in columns(d ^ e)] + [down_weight], axis=0)
        for d in distances
    }

    def both_cores(chips):
        got = {2 * d: part for d, part in chips.items()}
        got.update({2 * d + 1: swap(part, "rows", 1) for d, part in chips.items()})
        return got

    def ordered(pieces):
        return [pieces[j] for j in sorted(pieces)]

    qkv = both_cores(
        {0: attn_weight[1:3], **{d: after(first[d], factors, near_parts[d]) for d in distances}}
    )
    own = both_cores({0: attn_weight[3]}), both_cores({0: up_weight}), both_cores({0: down_weight})
    own_query = ordered(both_cores({0: attn_weight[0]}))
    own_out, own_up, own_down = (ordered(pieces) for pieces in own)
    qkv = ordered(qkv)
    wk, wv = (row_blocks(qkv, lead) for lead in range(2))
    normed, k, v, state = call(
        FORWARD * 5.6,
        functools.partial(keys_kernel, slots, rows),
        [act, act, act, state_shape],
        info,
        [x, vectors, wk, wv],
    )
    other = start(state, 0)
    far = {d: swap(after(part, state), "rows", 2 * d) for d, part in far_parts.items()}
    other, own_out[1], own_up[1], own_down[1] = meeting([other, own_out[1], own_up[1], own_down[1]])
    prefix, total = joined(state, other, [], False, 0)
    other = start(total, 1)
    slopes = call(
        FORWARD * 4,
        slopes_kernel,
        [shaped((tokens, 2 * share))],
        info,
        [after(dout, total)] + own_down,
        sends=2,
    )[0]
    (other, slopes), near = meeting_of([other, slopes], near)
    for i in range(1, joins):
        prefix, total = joined(total, other, [prefix], False, i)
        other = start(total, i + 1)
    near_all = ordered(both_cores({d: after(part, total) for d, part in near.items()}))
    wq = row_blocks(own_query + near_all, top=block)
    q, numer, denom = call(
        FORWARD * 8.5,
        functools.partial(queries_kernel, slots, rows),
        [act, act, act],
        info,
        [after(normed, total), wq, k, v],
        sends=1 + 2 * rows,
    )
    other, *near_all = meeting([other, *near_all, q])[:-1]
    wo = row_blocks(own_out + near_all)
    att, inv, resid, second, state_in = call(
        FORWARD * 6.3,
        functools.partial(attend_kernel, slots, rows, bit),
        [act, act, act, act, state_shape],
        info,
        [prefix, other, q, numer, denom, wo, x, vectors],
        sends=3 + 2 * rows,
    )

    small_shape = shaped((16, width))

    def up_columns(j, parts, top):
        def plan(info, refs, buffer):
            mine = (info[0] ^ j) * share
            column = ((info[0] ^ j) & 1) * share
            for m, ref in enumerate(refs):
                at = pl.ds(pl.multiple_of((info[0] ^ m) * block, block), block)
                if m < 2:
                    source = ref.at[:, pl.ds(pl.multiple_of(mine, share), share)]
                else:
                    row = top + lax.div(column, width) * block
                    lanes = pl.ds(pl.multiple_of(lax.rem(column, width), share), share)
                    source = ref.at[pl.ds(pl.multiple_of(row, block), block), lanes]
                yield source, buffer.at[at, :]

        return Built((width, share), own_up + parts, plan, n)

    def bottom(part):
        top = part.shape[0] - share
        return Built((share, width), [part], lambda info, refs, buffer: [(refs[0].at[top:, :], buffer)])

    js = list(range(2))
    own_slopes = [
        Built(
            (tokens, share),
            [slopes],
            lambda info, refs, buffer, j=j: [(refs[0].at[:, j * share : (j + 1) * share], buffer)],
        )
        for j in js
    ]
    blocks = [a for j in js for a in (up_columns(j, near_all, 2 * block), own_slopes[j])]
    wide, narrow = shaped((tokens, share * 2)), shaped((1, share * 2))
    g0, e0, back, dbias0 = call(
        FORWARD * 9,
        functools.partial(feed_kernel, js, False),
        [wide, wide, act, narrow],
        info,
        [second, dout] + blocks + [vectors],
        sends=2 * len(js) + 2,
    )
    (g0,), far = meeting_of([g0], far)
    far_all = ordered(both_cores(far))
    js = list(range(2, n))
    tops = [(j // 2 - 1) * (2 * share // width) * block for j in js]
    far_down = [bottom(part) for part in far_all]
    blocks = [a for j, top, down in zip(js, tops, far_down) for a in (up_columns(j, far_all, top), down)]
    wide, narrow = shaped((tokens, share * len(js))), shaped((1, share * len(js)))
    g1, e1, dresid, small, dbias1, dn, dd, dstate = call(
        FORWARD * 16,
        functools.partial(turn_kernel, js, slots, rows),
        [wide, wide, act, small_shape, narrow, act, act, state_shape],
        info,
        [second, dout] + blocks + [vectors, back, resid, wo, inv, att, q],
        limit=ALL,
        scratch=[pltpu.VMEM((tokens, width), F32)],
        sends=2 * len(js) + 4 + 2 * rows,
    )

    half_rows = shaped((n // 2 * share, width))

    def gradients(kernel, common, tops):
        full = (n, width, share) if kernel is up_grads_kernel else (n, share, width)
        return call(
            7,
            functools.partial(kernel, n, stretches),
            [half_rows] * 2,
            info,
            [common] + tops,
            direct=(0, 1),
            scratch=[pltpu.VMEM(full, F32)],
            sends=n * n * stretches * width // hidden if kernel is up_grads_kernel else n * stretches,
        )

    other = start(dstate, 0)
    down_theirs, down_mine = gradients(down_grads_kernel, after(dout, dstate), [g0, g1])
    other, down_theirs, down_mine = meeting([other, down_theirs, down_mine])

    dprefix, dtotal = joined(dstate, other, [], True, 0)
    other = start(dtotal, 1)
    chunk_down = Chunk(down_theirs, down_mine, early=DOWN)
    up_theirs, up_mine = gradients(up_grads_kernel, after(second, dtotal), [e0, e1])
    chunks = [chunk_down]
    other, up_theirs, up_mine, dprefix = meeting([other, up_theirs, up_mine, dprefix], chunks)

    for i in range(1, joins):
        dprefix, dtotal = joined(dtotal, other, [dprefix], True, i)
        other = start(dtotal, i + 1)
        if i + 1 < joins:
            (other,) = meeting([other], chunks)
    chunk_down.advance()
    chunk_up = Chunk(up_theirs, up_mine, early=UP)
    dk, dv, dq = call(
        13,
        functools.partial(local_back_kernel, slots, rows),
        [act, act, act],
        info,
        [after(q, dtotal), k, v, dn, dd, state_in],
        sends=3 * rows,
    )
    chunks = [chunk_down, chunk_up]
    dk, other, dprefix = meeting([dk, other, dprefix])

    chunk_down.advance()
    chunk_up.advance()
    four = shaped((n // 2 * 4 * block, width))
    attn_theirs, attn_mine, gk, gv = call(
        6,
        functools.partial(keys_back_kernel, n, slots, rows, bit, stretches),
        [four, four, act, act],
        info,
        [dprefix, other, v, k, dk, dv, normed, dq, att, dresid],
        direct=(0, 1),
        scratch=[pltpu.VMEM((4, width, width), F32), pltpu.VMEM(state_shape.shape, F32)],
        sends=n * stretches + 2,
    )
    attn_theirs, attn_mine, gk = meeting([attn_theirs, attn_mine, gk], chunks)

    chunk_attn = Chunk(attn_theirs, attn_mine)
    chunk_down.advance()
    chunk_up.advance()
    meeting([], [chunk_attn])
    chunk_attn.advance()
    dx, small = call(
        6,
        functools.partial(input_back_kernel, n),
        [act, small_shape],
        info,
        [after(gk, chunk_attn.held), wk, gv, wv, dq, wq, x, dresid, vectors, small, dbias0, dbias1],
    )
    chunks = [chunk_attn, chunk_down, chunk_up]
    small, late = meeting([small, resid])

    small = small + swap(small, "rows", 1)
    chunk_attn.extra = small
    late = after(late, dx)
    for chunk in chunks:
        chunk.advance()
    out = call(
        7,
        functools.partial(out_kernel, 2),
        [act],
        info,
        [vectors, late, g0, g1] + own_down + far_down,
    )[0]
    plan = chunk_attn.plan
    while chunks:
        if chunk_attn.step == 4:
            (out,) = meeting([out], chunks[1:])
        for chunk in chunks:
            chunk.advance()
        chunks = [chunk for chunk in chunks if chunk.result is None]
        if chunk_attn.step == len(plan.down) + 1:
            small = chunk_attn.extra
            for bits in plan.down[:1]:
                small = small + plan.move(small, bits)
    square = sum(jnp.sum(a * a) for chunk in (chunk_up, chunk_down, chunk_attn) for a in chunk.result)
    for bit in bits_of("rows"):
        square = square + swap(square, "rows", bit)

    def flat(a):
        return a.reshape(-1, width)

    results = update(
        info,
        square.reshape(1),
        small,
        [vectors, vec_m, vec_v],
        [
            (chunk_up.result, up_weight, up_m, up_v),
            (chunk_down.result, down_weight, down_m, down_v),
            (chunk_attn.result, flat(attn_weight), flat(attn_m), flat(attn_v)),
        ],
    )
    up_g, up_new, up_m_new, up_v_new = results[:4]
    down_g, down_new, down_m_new, down_v_new = results[4:8]
    attn_g, attn_new, attn_m_new, attn_v_new = (
        a.reshape(attn_weight.shape) for a in results[8:12]
    )
    grad_norm = results[12].reshape(())
    vec_g, vec_new, vec_m_new, vec_v_new = results[13:]
    return (
        out.reshape(activations.shape),
        dx.reshape(activations.shape),
        grad_norm,
        attn_g,
        up_g,
        down_g,
        vec_g,
        attn_new,
        up_new,
        down_new,
        vec_new,
        attn_m_new,
        up_m_new,
        down_m_new,
        vec_m_new,
        attn_v_new,
        up_v_new,
        down_v_new,
        vec_v_new,
    )


def solution(mesh):
    stretch = P("rows", "seq", None)
    stacked = P(None, "rows", None)
    split_rows = P("rows", None)
    weights = (stacked, split_rows, split_rows, P())
    return jax.shard_map(
        body,
        mesh=mesh,
        in_specs=(stretch, stretch, split_rows) + weights * 3,
        out_specs=(stretch, stretch, P()) + weights * 4,
        check_vma=False,
    )
```
